32 devices in a mesh: tok: 16 (over z, y, x), mlp: 2 (over core).
Axes of the slice: x: 2, y: 2, z: 4, core: 2. Of those that a mesh axis runs over, the one named last changes fastest.
Arguments:
- block_input: bfloat16 [16384, 1152], P(('tok', 'mlp')), may hold values from -44 to 44, as said below
- out_grad: bfloat16 [16384, 1152], P(('tok', 'mlp')), may hold values from -11 to 11, as said below
- class_table: bfloat16 [1000, 1152], replicated, may hold values from -6 to 6
- time_table: bfloat16 [1000, 1152], replicated, may hold values from -6 to 6
- class_label: int32 [128], P(('tok', 'mlp')), may hold values from 0 to 999
- time_index: int32 [128], P(('tok', 'mlp')), may hold values from 0 to 999
- grid_height: int32 [128], P(('tok', 'mlp')), may hold values from 0 to 16, as said below
- grid_width: int32 [128], P(('tok', 'mlp')), may hold values from 0 to 20, as said below
- mix_weight: float32 [1152, 3456], P('tok', 'mlp'), may hold values from -0.1875 to 0.1875
- proj_weight: float32 [1152, 1152], P('tok', 'mlp'), may hold values from -0.1875 to 0.1875
- cond_weight: float32 [1152, 6912], P('tok', 'mlp'), may hold values from -0.1875 to 0.1875
- cond_bias: float32 [6912], P(('tok', 'mlp')), may hold values from -0.5 to 0.5
- feed_weight: float32 [2, 1152, 3072], P(None, 'tok', 'mlp')
- down_weight: float32 [3072, 1152], P('mlp', 'tok'), may hold values from -0.109375 to 0.109375
- mix_mean: float32 [1152, 3456], P('tok', 'mlp'), may hold values from -0.00010681152 to 0.00010681152
- proj_mean: float32 [1152, 1152], P('tok', 'mlp'), may hold values from -0.00010681152 to 0.00010681152
- cond_mean: float32 [1152, 6912], P('tok', 'mlp'), may hold values from -0.00010681152 to 0.00010681152
- bias_mean: float32 [6912], P(('tok', 'mlp')), may hold values from -0.00010681152 to 0.00010681152
- feed_mean: float32 [2, 1152, 3072], P(None, 'tok', 'mlp'), may hold values from -0.00010681152 to 0.00010681152
- down_mean: float32 [3072, 1152], P('mlp', 'tok'), may hold values from -0.00010681152 to 0.00010681152
- mix_square: float32 [1152, 3456], P('tok', 'mlp'), may hold values from 1.2555041e-09 to 5.0220166e-09
- proj_square: float32 [1152, 1152], P('tok', 'mlp'), may hold values from 1.2555041e-09 to 5.0220166e-09
- cond_square: float32 [1152, 6912], P('tok', 'mlp'), may hold values from 1.2555041e-09 to 5.0220166e-09
- bias_square: float32 [6912], P(('tok', 'mlp')), may hold values from 1.2555041e-09 to 5.0220166e-09
- feed_square: float32 [2, 1152, 3072], P(None, 'tok', 'mlp'), may hold values from 1.2555041e-09 to 5.0220166e-09
- down_square: float32 [3072, 1152], P('mlp', 'tok'), may hold values from 1.2555041e-09 to 5.0220166e-09
Outputs:
- block_output: bfloat16 [16384, 1152], P(('tok', 'mlp'))
- input_grad: float32 [16384, 1152], P(('tok', 'mlp'))
- grad_norm: float32 [], replicated
- mix_mean_new: float32 [1152, 3456], P('tok', 'mlp')
- proj_mean_new: float32 [1152, 1152], P('tok', 'mlp')
- cond_mean_new: float32 [1152, 6912], P('tok', 'mlp')
- bias_mean_new: float32 [6912], P(('tok', 'mlp'))
- feed_mean_new: float32 [2, 1152, 3072], P(None, 'tok', 'mlp')
- down_mean_new: float32 [3072, 1152], P('mlp', 'tok')
- mix_square_new: float32 [1152, 3456], P('tok', 'mlp')
- proj_square_new: float32 [1152, 1152], P('tok', 'mlp')
- cond_square_new: float32 [1152, 6912], P('tok', 'mlp')
- bias_square_new: float32 [6912], P(('tok', 'mlp'))
- feed_square_new: float32 [2, 1152, 3072], P(None, 'tok', 'mlp')
- down_square_new: float32 [3072, 1152], P('mlp', 'tok')
- mix_weight_new: float32 [1152, 3456], P('tok', 'mlp')
- proj_weight_new: float32 [1152, 1152], P('tok', 'mlp')
- cond_weight_new: float32 [1152, 6912], P('tok', 'mlp')
- cond_bias_new: float32 [6912], P(('tok', 'mlp'))
- feed_weight_new: float32 [2, 1152, 3072], P(None, 'tok', 'mlp')
- down_weight_new: float32 [3072, 1152], P('mlp', 'tok')
The draws below stay inside these ranges and needn't reach their ends.
Inputs may be any that keep to these rules, and one draw needn't show every extreme that they name: block_input is finite. out_grad is finite. `grid_height`: the 4 slots of pack n describe its images in order; unused slots have height and width 0 and come after the used ones. An image is 8 x 16, 16 x 16 or 16 x 5*16//4 patches (height x width), and the images of one pack hold at most 512 tokens. `grid_width`: see grid_height.
All inputs are finite; a program needn't handle non-finite values.
Results may differ from the reference program's by a relative error of at most 0.028.
Values may be sent and summed in bfloat16 or wider, within the bound.
No kernel may reach another device: no remote copies, remote signals or barrier semaphores. Data moves between devices by JAX's collectives and lax.ppermute only.
A program may use at most 320 MiB of HBM per device.

```python
import math
import jax
import jax.numpy as jnp
import numpy as np
from jax import lax

HEADS = 16
HEAD = 72
FF = 3072
D = 1152
SIDE = 16
SLOTS = 4
CLASSES = 1000
TSTEPS = 1000
STEP = 10
TOK_DEV = 512
TOKENS = 16384
IMAGES = 128
NPARAM = 23894784
DEVICES = 32


PACK_TABLE = np.array([[3, 1, 0, 0], [2, 2, 0, 0], [1, 1, 1, 1], [2, 1, 0, 0], [1, 3, 0, 0], [1, 2, 1, 0]], dtype=np.int32)


def channel_rise(top):
    return jnp.exp(jnp.log(top) * jnp.arange(D, dtype=jnp.float32) / (D - 1))


def image_codes(key):
    picks = jax.random.randint(jax.random.fold_in(key, 11), (DEVICES,), 0, 6)
    forced = jax.random.randint(jax.random.fold_in(key, 12), (), 0, DEVICES)
    places = jnp.arange(DEVICES, dtype=jnp.int32)
    picks = jnp.where(places == forced, 0, picks)
    picks = jnp.where(places == (forced + 1) % DEVICES, 1, picks)
    return jnp.asarray(PACK_TABLE)[picks].reshape(-1)


def draw_block_input(key, part):
    key = jax.random.fold_in(key, 1)
    row_key, col_key, value_key = jax.random.split(key, 3)
    row_scale = jnp.exp(jax.random.uniform(row_key, (TOKENS, 1), jnp.float32, 0.0, 2.3))
    col_scale = jnp.exp(jax.random.uniform(col_key, (1, D), jnp.float32, 0.0, 1.4))
    base = jnp.clip(jax.random.normal(value_key, (TOKENS, D), jnp.float32), -6.0, 6.0) * channel_rise(1.8)
    return (0.1 * base * row_scale * col_scale).astype(jnp.bfloat16)


def draw_out_grad(key, part):
    key = jax.random.fold_in(key, 2)
    base = jnp.clip(jax.random.normal(key, (TOKENS, D), jnp.float32), -6.0, 6.0) * channel_rise(1.8)
    return base.astype(jnp.bfloat16)


def draw_grid_height(key, part):
    codes = image_codes(key)
    heights = jnp.array([0, SIDE // 2, SIDE, SIDE], dtype=jnp.int32)
    return heights[codes]


def draw_grid_width(key, part):
    codes = image_codes(key)
    widths = jnp.array([0, SIDE, SIDE, 5 * SIDE // 4], dtype=jnp.int32)
    return widths[codes]


def draw_feed_weight(key, part):
    key = jax.random.fold_in(key, 5)
    noise_key, common_key = jax.random.split(key)
    noise = jnp.clip(jax.random.normal(noise_key, (2, D, FF), jnp.float32), -6.0, 6.0)
    common = jax.random.normal(common_key, (2, 1, FF), jnp.float32) * 0.5
    return (noise + common) * D ** (-0.5)


def place_ends(values, own_key, smallest, largest):
    place = [jax.random.randint(jax.random.fold_in(own_key, axis), (), 0, length) for axis, length in enumerate(values.shape)]
    main_axis = values.shape.index(max(values.shape))
    beside = place[:main_axis] + [(place[main_axis] + 1) % values.shape[main_axis]] + place[main_axis + 1:]
    return values.at[tuple(place)].set(smallest).at[tuple(beside)].set(largest)


def shard_levels(key, shape, shards, low, top_value):
    loudness = 1.0
    for dim, blocks in shards:
        draws = jax.random.uniform(jax.random.fold_in(jax.random.fold_in(key, 6), dim), (blocks,), jnp.float32, low / len(shards), top_value / len(shards))
        loudness = loudness * jnp.repeat(jnp.exp(draws), shape[dim] // blocks).reshape((-1,) + (1,) * (len(shape) - 1 - dim))
    return loudness


def gaussian(stream_key, shape, scale, limit, cuts=(), held_as=jnp.bfloat16):
    values = scale * jax.random.normal(stream_key, shape, jnp.float32)
    if cuts:
        values = values * shard_levels(stream_key, shape, cuts, -0.22, 0.18)
    return jnp.clip(values, -limit, limit).astype(held_as)


def setup_inputs(seed: int = 0) -> dict:
    seeds = jax.random.split(jax.random.key(seed), 27)
    return {
        "block_input": draw_block_input(jax.random.fold_in(seeds[26], 71), 0),
        "out_grad": draw_out_grad(jax.random.fold_in(seeds[26], 71), 0),
        "class_table": gaussian(seeds[2], (CLASSES, D), 1.0, 6.0),
        "time_table": gaussian(seeds[3], (TSTEPS, D), 1.0, 6.0),
        "class_label": place_ends(jax.random.randint(seeds[4], (IMAGES,), 0, CLASSES), jax.random.fold_in(seeds[4], 1), 0, CLASSES - 1).astype(jnp.int32),
        "time_index": place_ends(jax.random.randint(seeds[5], (IMAGES,), 0, TSTEPS), jax.random.fold_in(seeds[5], 1), 0, TSTEPS - 1).astype(jnp.int32),
        "grid_height": draw_grid_height(jax.random.fold_in(seeds[26], 71), 0),
        "grid_width": draw_grid_width(jax.random.fold_in(seeds[26], 71), 0),
        "mix_weight": gaussian(seeds[8], (D, 3 * D), D ** -0.5, 0.1875, ((0, 16), (1, 2)), jnp.float32),
        "proj_weight": gaussian(seeds[9], (D, D), D ** -0.5, 0.1875, ((0, 16), (1, 2)), jnp.float32),
        "cond_weight": gaussian(seeds[10], (D, 6 * D), D ** -0.5, 0.1875, ((0, 16), (1, 2)), jnp.float32),
        "cond_bias": gaussian(seeds[11], (6 * D,), 0.1, 0.5, ((0, 32),), jnp.float32),
        "feed_weight": draw_feed_weight(jax.random.fold_in(seeds[26], 71), 0),
        "down_weight": gaussian(seeds[13], (FF, D), FF ** -0.5, 0.109375, ((0, 2), (1, 16)), jnp.float32),
        "mix_mean": gaussian(seeds[14], (D, 3 * D), (0.085 / NPARAM ** 0.5), 0.00010681152, ((0, 16), (1, 2)), jnp.float32),
        "proj_mean": gaussian(seeds[15], (D, D), (0.085 / NPARAM ** 0.5), 0.00010681152, ((0, 16), (1, 2)), jnp.float32),
        "cond_mean": gaussian(seeds[16], (D, 6 * D), (0.085 / NPARAM ** 0.5), 0.00010681152, ((0, 16), (1, 2)), jnp.float32),
        "bias_mean": gaussian(seeds[17], (6 * D,), (0.085 / NPARAM ** 0.5), 0.00010681152, ((0, 32),), jnp.float32),
        "feed_mean": gaussian(seeds[18], (2, D, FF), (0.085 / NPARAM ** 0.5), 0.00010681152, ((1, 16), (2, 2)), jnp.float32),
        "down_mean": gaussian(seeds[19], (FF, D), (0.085 / NPARAM ** 0.5), 0.00010681152, ((0, 2), (1, 16)), jnp.float32),
        "mix_square": jnp.clip(jnp.exp(math.log(5.022016580369382e-09) - 1.3862944 * jax.random.uniform(seeds[20], (D, 3 * D), jnp.float32) ** shard_levels(seeds[20], (D, 3 * D), ((0, 16), (1, 2)), -0.2, 0.2)), 1.2555041450923454e-09, 5.022016580369382e-09),
        "proj_square": jnp.clip(jnp.exp(math.log(5.022016580369382e-09) - 1.3862944 * jax.random.uniform(seeds[21], (D, D), jnp.float32) ** shard_levels(seeds[21], (D, D), ((0, 16), (1, 2)), -0.2, 0.2)), 1.2555041450923454e-09, 5.022016580369382e-09),
        "cond_square": jnp.clip(jnp.exp(math.log(5.022016580369382e-09) - 1.3862944 * jax.random.uniform(seeds[22], (D, 6 * D), jnp.float32) ** shard_levels(seeds[22], (D, 6 * D), ((0, 16), (1, 2)), -0.2, 0.2)), 1.2555041450923454e-09, 5.022016580369382e-09),
        "bias_square": jnp.clip(jnp.exp(math.log(5.022016580369382e-09) - 1.3862944 * jax.random.uniform(seeds[23], (6 * D,), jnp.float32) ** shard_levels(seeds[23], (6 * D,), ((0, 32),), -0.2, 0.2)), 1.2555041450923454e-09, 5.022016580369382e-09),
        "feed_square": jnp.clip(jnp.exp(math.log(5.022016580369382e-09) - 1.3862944 * jax.random.uniform(seeds[24], (2, D, FF), jnp.float32) ** shard_levels(seeds[24], (2, D, FF), ((1, 16), (2, 2)), -0.2, 0.2)), 1.2555041450923454e-09, 5.022016580369382e-09),
        "down_square": jnp.clip(jnp.exp(math.log(5.022016580369382e-09) - 1.3862944 * jax.random.uniform(seeds[25], (FF, D), jnp.float32) ** shard_levels(seeds[25], (FF, D), ((0, 2), (1, 16)), -0.2, 0.2)), 1.2555041450923454e-09, 5.022016580369382e-09),
    }


BETA_ONE = 0.9
BETA_TWO = 0.95
ADAM_EPS = 1e-08
RATE = 0.08
DECAY = 0.01
CLIP_NORM = 1.0
NORM_EPS = 1e-06
MASKED = -1e+30
HIGH = lax.Precision.HIGHEST

@jax.custom_vjp
def low(v):
    return lax.optimization_barrier(v.astype(jnp.bfloat16)).astype(jnp.float32)

@jax.custom_vjp
def low_back(v):
    return v

def low_keep(v):
    return (low(v), None)

def low_pass(kept, grad):
    return (grad,)

def back_keep(v):
    return (v, None)

def back_low(kept, grad):
    return (low(grad),)
low.defvjp(low_keep, low_pass)
low_back.defvjp(back_keep, back_low)

def product(left, right):
    return jnp.dot(left, right, preferred_element_type=jnp.float32, precision=HIGH)

def layer_norm(value):
    centered = value - lax.optimization_barrier(jnp.mean(value, axis=-1, keepdims=True))
    spread = lax.optimization_barrier(jnp.mean(centered * centered, axis=-1, keepdims=True))
    return centered * lax.rsqrt(spread + NORM_EPS)

def geometry(height, width, count):
    lengths = (height * width).astype(jnp.int32)
    ends = jnp.cumsum(lengths).astype(jnp.int32)
    starts = (ends - lengths).astype(jnp.int32)
    places = jnp.arange(count, dtype=jnp.int32)
    segment = lax.optimization_barrier(jnp.sum((places[:, None] >= ends[None, :]).astype(jnp.int32), axis=1)).astype(jnp.int32)
    member = segment[:, None] == jnp.arange(height.shape[0], dtype=jnp.int32)[None, :]
    start_tok = lax.optimization_barrier(jnp.sum(jnp.where(member, starts[None, :], 0), axis=1)).astype(jnp.int32)
    width_tok = jnp.maximum(lax.optimization_barrier(jnp.sum(jnp.where(member, width[None, :], 0), axis=1)), 1).astype(jnp.int32)
    offset = places - start_tok
    return (segment, member.astype(jnp.float32), offset // width_tok, offset % width_tok)

def rope(value, rows, cols):
    quarter = value.shape[-1] // 4
    freq = 10000.0 ** (-jnp.arange(quarter, dtype=jnp.float32) / quarter)
    angle = jnp.concatenate([rows.astype(jnp.float32)[:, None] * freq[None, :], cols.astype(jnp.float32)[:, None] * freq[None, :]], axis=1)[:, None, :]
    cosine = jnp.cos(angle)
    sine = jnp.sin(angle)
    first = jnp.concatenate([value[..., :quarter], value[..., 2 * quarter:3 * quarter]], axis=-1)
    second = jnp.concatenate([value[..., quarter:2 * quarter], value[..., 3 * quarter:]], axis=-1)
    new_first = first * cosine - second * sine
    new_second = second * cosine + first * sine
    return jnp.concatenate([new_first[..., :quarter], new_second[..., :quarter], new_first[..., quarter:], new_second[..., quarter:]], axis=-1)

def block_forward(params, block, cond, member, segment, rows, cols):
    mix, proj, cond_w, bias, feed, down = params
    count = block.shape[0]
    modulation = low_back(product(cond, low(cond_w))) + low(bias)
    per_token = product(member, modulation)
    shift_a, scale_a, gate_a, shift_b, scale_b, gate_b = jnp.split(per_token, 6, axis=1)
    first_in = low(layer_norm(block) * (1.0 + scale_a) + shift_a)
    mixed = low_back(product(first_in, low(mix)))
    query, key, value = jnp.split(mixed, 3, axis=1)
    shape = (count, HEADS, HEAD)
    query = low(rope(query.reshape(shape), rows, cols))
    key = low(rope(key.reshape(shape), rows, cols))
    value = low(value.reshape(shape))
    scores = low_back(jnp.einsum('qhd,khd->hqk', query, key, precision=HIGH)) * HEAD ** (-0.5)
    same = segment[:, None] == segment[None, :]
    scores = jnp.where(same[None], scores, MASKED)
    top = lax.optimization_barrier(jnp.max(scores, axis=-1, keepdims=True))
    weights = jnp.exp(scores - top)
    probs = low(weights / lax.optimization_barrier(jnp.sum(weights, axis=-1, keepdims=True)))
    attended = jnp.einsum('hqk,khd->qhd', probs, value, precision=HIGH).reshape(count, HEADS * HEAD)
    attended = low(low_back(attended))
    branch = low_back(product(attended, low(proj)))
    middle = block + gate_a * branch
    second_in = low(layer_norm(middle) * (1.0 + scale_b) + shift_b)
    feed_low = low(feed)
    gate_pre = low_back(product(second_in, feed_low[0]))
    up_pre = low_back(product(second_in, feed_low[1]))
    hidden = low(jax.nn.silu(gate_pre) * up_pre)
    result = low_back(product(hidden, low(down)))
    valid = (segment < SLOTS).astype(jnp.float32)[:, None]
    return valid * (middle + gate_b * result)

def adam(weight, mean, square, grad):
    mean_new = BETA_ONE * mean + (1.0 - BETA_ONE) * grad
    square_new = BETA_TWO * square + (1.0 - BETA_TWO) * grad * grad
    fixed_mean = mean_new / (1.0 - BETA_ONE ** STEP)
    fixed_square = square_new / (1.0 - BETA_TWO ** STEP)
    weight_new = weight - RATE * (fixed_mean / (jnp.sqrt(fixed_square) + ADAM_EPS) + DECAY * weight)
    return (mean_new, square_new, weight_new)

def reference(block_input, out_grad, class_table, time_table, class_label, time_index, grid_height, grid_width, mix_weight, proj_weight, cond_weight, cond_bias, feed_weight, down_weight, mix_mean, proj_mean, cond_mean, bias_mean, feed_mean, down_mean, mix_square, proj_square, cond_square, bias_square, feed_square, down_square):
    params = (mix_weight, proj_weight, cond_weight, cond_bias, feed_weight, down_weight)
    packs = TOKENS // TOK_DEV
    embed = class_table[class_label].astype(jnp.float32) + time_table[time_index].astype(jnp.float32)
    cond_all = low(jax.nn.silu(embed)).reshape(packs, SLOTS, D)
    blocks = block_input.astype(jnp.float32).reshape(packs, TOK_DEV, D)
    cots = out_grad.astype(jnp.float32).reshape(packs, TOK_DEV, D)
    heights = grid_height.reshape(packs, SLOTS)
    widths = grid_width.reshape(packs, SLOTS)

    def one_pack(total, item):
        block, cond, height, width, cot = item
        segment, member, rows, cols = geometry(height, width, TOK_DEV)

        def forward(weights, inputs):
            return block_forward(weights, inputs, cond, member, segment, rows, cols)
        output, pull = jax.vjp(forward, params, block)
        grads, back = pull(cot)
        return (jax.tree.map(jnp.add, total, grads), (output, back))
    zeros = jax.tree.map(jnp.zeros_like, params)
    grads, (outputs, backs) = lax.scan(one_pack, zeros, (blocks, cond_all, heights, widths, cots))
    squares = jnp.float32(0.0)
    for grad in grads:
        squares = squares + jnp.sum(grad * grad)
    grad_norm = jnp.sqrt(squares)
    factor = CLIP_NORM / jnp.maximum(grad_norm, CLIP_NORM)
    means = (mix_mean, proj_mean, cond_mean, bias_mean, feed_mean, down_mean)
    squares_old = (mix_square, proj_square, cond_square, bias_square, feed_square, down_square)
    updates = [adam(w, m, v, g * factor) for w, m, v, g in zip(params, means, squares_old, grads)]
    block_output = outputs.reshape(TOKENS, D).astype(jnp.bfloat16)
    input_grad = backs.reshape(TOKENS, D)
    return (block_output, input_grad, grad_norm, updates[0][0], updates[1][0], updates[2][0], updates[3][0], updates[4][0], updates[5][0], updates[0][1], updates[1][1], updates[2][1], updates[3][1], updates[4][1], updates[5][1], updates[0][2], updates[1][2], updates[2][2], updates[3][2], updates[4][2], updates[5][2])
```

```python
import jax
import jax.numpy as jnp
from jax import lax
from jax.sharding import PartitionSpec as P

HEADS = 16
HEAD = 72
SLOTS = 4
STEP = 10


BETA_ONE = 0.9
BETA_TWO = 0.95
ADAM_EPS = 1e-08
RATE = 0.08
DECAY = 0.01
CLIP_NORM = 1.0
NORM_EPS = 1e-06
MASKED = -1e30
HIGH = lax.Precision.HIGHEST


def layer_norm(value):
    centered = value - jnp.mean(value, axis=-1, keepdims=True)
    spread = jnp.mean(centered * centered, axis=-1, keepdims=True)
    return centered * lax.rsqrt(spread + NORM_EPS)


def modulate(value, shift, scale):
    return layer_norm(value) * (1.0 + scale) + shift


def geometry(height, width, count):
    lengths = height * width
    ends = jnp.cumsum(lengths)
    starts = ends - lengths
    places = jnp.arange(count, dtype=jnp.int32)
    segment = jnp.sum((places[:, None] >= ends[None, :]).astype(jnp.int32), axis=1)
    member = segment[:, None] == jnp.arange(height.shape[0], dtype=jnp.int32)[None, :]
    start_tok = jnp.sum(jnp.where(member, starts[None, :], 0), axis=1)
    width_tok = jnp.maximum(jnp.sum(jnp.where(member, width[None, :], 0), axis=1), 1)
    offset = places - start_tok
    return (segment, member.astype(jnp.float32), offset // width_tok, offset % width_tok)


def rope(value, rows, cols):
    quarter = value.shape[-1] // 4
    freq = 10000.0 ** (-jnp.arange(quarter, dtype=jnp.float32) / quarter)
    angle = jnp.concatenate(
        [
            rows.astype(jnp.float32)[:, None] * freq[None, :],
            cols.astype(jnp.float32)[:, None] * freq[None, :],
        ],
        axis=1,
    )[:, None, :]
    cosine = jnp.cos(angle)
    sine = jnp.sin(angle)
    first = jnp.concatenate([value[..., :quarter], value[..., 2 * quarter : 3 * quarter]], axis=-1)
    second = jnp.concatenate(
        [value[..., quarter : 2 * quarter], value[..., 3 * quarter :]], axis=-1
    )
    new_first = first * cosine - second * sine
    new_second = second * cosine + first * sine
    return jnp.concatenate(
        [
            new_first[..., :quarter],
            new_second[..., :quarter],
            new_first[..., quarter:],
            new_second[..., quarter:],
        ],
        axis=-1,
    )


def across(left, right, precision=None):
    return lax.dot_general(
        left,
        right,
        (((0,), (0,)), ((), ())),
        preferred_element_type=jnp.float32,
        precision=precision,
    )


def against(left, right):
    return lax.dot_general(
        left, right, (((1,), (1,)), ((), ())), preferred_element_type=jnp.float32
    )


def adam(weight, mean, square, grad):
    mean_new = BETA_ONE * mean + (1.0 - BETA_ONE) * grad
    square_new = BETA_TWO * square + (1.0 - BETA_TWO) * grad * grad
    fixed_mean = mean_new / (1.0 - BETA_ONE**STEP)
    fixed_square = square_new / (1.0 - BETA_TWO**STEP)
    weight_new = weight - RATE * (fixed_mean / (jnp.sqrt(fixed_square) + ADAM_EPS) + DECAY * weight)
    return (mean_new, square_new, weight_new)


AXES = {16: (2, 2, 4), 128: (8, 4, 4)}


def factors(count):
    sizes = AXES.get(count, (count,))
    strides = []
    stride = 1
    for size in sizes:
        strides.append((size, stride))
        stride *= size
    return strides


def shift(factor, step, count):
    size, stride = factor
    pairs = []
    for place in range(count):
        digit = (place // stride) % size
        pairs.append((place, place + ((digit + step) % size - digit) * stride))
    return pairs


def digit_of(factor):
    size, stride = factor
    return (lax.axis_index("tok") // stride) % size


def plan(count):
    parts = factors(count)
    canon = parts[::-1]
    longest = max(canon, key=lambda part: part[0])
    rest = [part for part in canon if part is not longest]
    return canon, [longest] + rest, [longest] + rest[::-1]


def swap(value):
    return lax.ppermute(value, "mlp", [(0, 1), (1, 0)])


def gather_stage(value, factor, axis, count):
    size = factor[0]
    if size == 1:
        return value
    digit = digit_of(factor)
    shape = list(value.shape)
    shape[axis] *= size
    pieces = [value] + [
        lax.ppermute(value, "tok", shift(factor, step, count)) for step in range(1, size)
    ]
    out = jnp.zeros(shape, value.dtype)
    for step, piece in enumerate(pieces):
        start = [0] * value.ndim
        start[axis] = (digit - step) % size
        out = lax.dynamic_update_slice(out, piece, tuple(start))
    return out


def scatter_stage(value, factor, axis, count, kept):
    size = factor[0]
    if size == 1:
        return value.astype(kept)
    digit = digit_of(factor)

    def part(place):
        return lax.dynamic_slice_in_dim(value, place % size, 1, axis)

    out = part(digit).astype(jnp.float32)
    for step in range(1, size):
        sent = part(digit + step).astype(jnp.bfloat16)
        out = out + lax.ppermute(sent, "tok", shift(factor, step, count)).astype(jnp.float32)
    return out.astype(kept)


def split_rows(value, canon):
    sizes = [part[0] for part in canon]
    total = 1
    for size in sizes:
        total *= size
    return value.reshape(*sizes, value.shape[0] // total, value.shape[1])


def gather_small(value, count):
    canon, order, _ = plan(count)
    out = value.reshape((1,) * len(canon) + value.shape)
    for factor in order:
        out = gather_stage(out, factor, canon.index(factor), count)
    return out.reshape((count,) + value.shape)


def scatter_small(value, count):
    canon, order, _ = plan(count)
    out = split_rows(value, canon)
    for factor in order[::-1]:
        kept = jnp.float32
        out = scatter_stage(out, factor, canon.index(factor), count, kept)
    return out.reshape(out.shape[-2:])


def sum_all(value, count):
    value = value + swap(value)
    for factor in factors(count):
        size = factor[0]
        if size == 2:
            value = value + lax.ppermute(value, "tok", shift(factor, 1, count))
            continue
        digit = digit_of(factor)
        places = jnp.arange(size)
        line = jnp.where(places == digit, value, 0.0)
        for step in range(1, size):
            moved = lax.ppermute(value, "tok", shift(factor, step, count))
            line = jnp.where(places == (digit - step) % size, moved, line)
        value = jnp.sum(line)
    return value


def pick(segment, table):
    out = jnp.zeros((segment.shape[0], table.shape[1]), jnp.float32)
    for slot in range(SLOTS):
        out = jnp.where(segment[:, None] == slot, table[slot][None, :], out)
    return out


def body(
    block_input,
    out_grad,
    class_table,
    time_table,
    class_label,
    time_index,
    grid_height,
    grid_width,
    mix_weight,
    proj_weight,
    cond_weight,
    cond_bias,
    feed_weight,
    down_weight,
    mix_mean,
    proj_mean,
    cond_mean,
    bias_mean,
    feed_mean,
    down_mean,
    mix_square,
    proj_square,
    cond_square,
    bias_square,
    feed_square,
    down_square,
):
    half = jnp.bfloat16
    count = block_input.shape[0]
    width = block_input.shape[1]
    chips = lax.axis_size("tok")
    tok = lax.axis_index("tok")
    side = lax.axis_index("mlp")
    first_side = side == 0
    canon, order_a, order_b = plan(chips)
    rows_own = mix_weight.shape[0]
    mix_cols = mix_weight.shape[1]
    proj_cols = proj_weight.shape[1]
    hidden_cols = feed_weight.shape[2]
    cond_cols = cond_weight.shape[1]

    def expand(value):
        return value.reshape((1,) * len(canon) + value.shape)

    def stage(value, factor):
        return gather_stage(value, factor, canon.index(factor), chips)

    near = jnp.concatenate([mix_weight.astype(half), proj_weight.astype(half)], axis=1)
    near = stage(expand(near), order_a[0])
    down_turned = down_weight.T
    mid = hidden_cols // 2
    far = jnp.concatenate(
        [
            feed_weight[0].astype(half),
            down_turned[:, :mid].astype(half),
            feed_weight[1].astype(half),
            down_turned[:, mid:].astype(half),
        ],
        axis=1,
    )
    near, far = lax.optimization_barrier((near, far))
    far = stage(expand(far), order_a[0])
    cut = near.shape[-1] // 2
    near_a, near_b = near[..., :cut], near[..., cut:]
    for one, two in zip(order_a[1:], order_b[1:]):
        near_a, near_b = stage(near_a, one), stage(near_b, two)
    near_a, near_b, far = lax.optimization_barrier((near_a, near_b, far))
    cut = far.shape[-1] // 2
    far_a, far_b = far[..., :cut], far[..., cut:]
    for one, two in zip(order_a[1:], order_b[1:]):
        far_a, far_b = stage(far_a, one), stage(far_b, two)
    near_a, near_b, far_a, far_b = (
        value.reshape(width, value.shape[-1]) for value in (near_a, near_b, far_a, far_b)
    )
    far_gate, far_up = far_a[:, :hidden_cols], far_b[:, :hidden_cols]
    down_a, down_b = far_a[:, hidden_cols:], far_b[:, hidden_cols:]
    near_own = jnp.concatenate([near_a, near_b], axis=1)
    near_other = jnp.concatenate([swap(near_a), swap(near_b)], axis=1)
    mix_own, proj_own = near_own[:, :mix_cols], near_own[:, mix_cols:]
    mix_other, proj_other = near_other[:, :mix_cols], near_other[:, mix_cols:]

    def joined(own, other):
        low = jnp.where(first_side, own, other)
        high = jnp.where(first_side, other, own)
        return jnp.concatenate([low, high], axis=1)

    def parted(value):
        size = value.shape[1] // 2
        low, high = value[:, :size], value[:, size:]
        return jnp.where(first_side, low, high), jnp.where(first_side, high, low)

    codes = jnp.stack([class_label, time_index])
    codes = gather_small(jnp.concatenate([codes, swap(codes)], axis=1), chips)
    labels = codes[:, 0].reshape(-1)
    times = codes[:, 1].reshape(-1)
    start = tok * rows_own
    class_part = lax.dynamic_slice_in_dim(class_table, start, rows_own, 1)
    time_part = lax.dynamic_slice_in_dim(time_table, start, rows_own, 1)
    class_hot = (labels[:, None] == jnp.arange(class_table.shape[0])[None, :]).astype(half)
    time_hot = (times[:, None] == jnp.arange(time_table.shape[0])[None, :]).astype(half)
    embed = jnp.dot(class_hot, class_part, preferred_element_type=jnp.float32) + jnp.dot(
        time_hot, time_part, preferred_element_type=jnp.float32
    )
    cond_low = jax.nn.silu(embed).astype(half)
    partial_mod = jnp.dot(cond_low, cond_weight.astype(half), preferred_element_type=jnp.float32)
    bias_low = cond_bias.astype(half).astype(jnp.float32)
    bias_pair = joined(bias_low[None, :], swap(bias_low)[None, :])[0]
    bias_start = tok * bias_pair.shape[0]
    bias_side = bias_start // cond_cols
    bias_pair = jnp.where(bias_side == side, bias_pair, 0.0)
    bias_row = lax.dynamic_update_slice(
        jnp.zeros((cond_cols,), jnp.float32), bias_pair, (bias_start - bias_side * cond_cols,)
    )
    mod_half = scatter_small(partial_mod + bias_row[None, :], chips)
    slots = class_label.shape[0]
    modulation = joined(mod_half[:slots], swap(mod_half[slots:]))

    segment, member, rows, cols = geometry(grid_height, grid_width, count)
    valid = (segment < SLOTS).astype(jnp.float32)[:, None]
    shift_a, scale_a, gate_a, shift_b, scale_b, gate_b = (
        pick(segment, table) for table in jnp.split(modulation, 6, axis=1)
    )
    inputs = block_input.astype(jnp.float32)
    first_in = modulate(inputs, shift_a, scale_a).astype(half)
    first_other = swap(first_in)
    mixed = joined(
        jnp.dot(first_in, mix_own, preferred_element_type=jnp.float32),
        jnp.dot(first_in, mix_other, preferred_element_type=jnp.float32),
    )
    query_raw, key_raw, value_raw = jnp.split(mixed, 3, axis=1)
    shape = (count, HEADS, HEAD)
    query_raw = query_raw.reshape(shape)
    key_raw = key_raw.reshape(shape)
    query = rope(query_raw, rows, cols).astype(half)
    key = rope(key_raw, rows, cols).astype(half)
    value = value_raw.reshape(shape).astype(half)
    scale = HEAD ** (-0.5)
    same = segment[:, None] == segment[None, :]

    def scores_of():
        raw = jnp.einsum("qhd,khd->hqk", query, key, preferred_element_type=jnp.float32) * scale
        return jnp.where(same[None], raw, MASKED)

    scores = scores_of()
    top = jnp.max(scores, axis=-1, keepdims=True)
    weights = jnp.exp(scores - top)
    totals = jnp.sum(weights, axis=-1, keepdims=True)
    probs_low = (weights / totals).astype(half)
    log_total = top + jnp.log(totals)
    attended = (
        jnp.einsum("hqk,khd->qhd", probs_low, value, preferred_element_type=jnp.float32)
        .reshape(count, width)
        .astype(half)
    )
    attended_other = swap(attended)
    branch = joined(
        jnp.dot(attended, proj_own, preferred_element_type=jnp.float32),
        jnp.dot(attended, proj_other, preferred_element_type=jnp.float32),
    )
    middle = inputs + gate_a * branch
    second_in = modulate(middle, shift_b, scale_b).astype(half)
    second_pair = jnp.concatenate([second_in, swap(second_in)], axis=0)
    gate_pre = jnp.dot(second_pair, far_gate, preferred_element_type=jnp.float32)
    up_pre = jnp.dot(second_pair, far_up, preferred_element_type=jnp.float32)
    hidden = (jax.nn.silu(gate_pre) * up_pre).astype(half)
    partial_value = against(hidden[:, :mid], down_a) + against(hidden[:, mid:], down_b)
    result = partial_value[:count] + swap(partial_value[count:].astype(half)).astype(jnp.float32)
    block_output = (valid * (middle + gate_b * result)).astype(half)

    grad_out = valid * out_grad.astype(jnp.float32)
    d_gate_b = grad_out * result
    result_grad = (gate_b * grad_out).astype(half)
    result_pair = jnp.concatenate([result_grad, swap(result_grad)], axis=0)
    d_down = across(result_pair, hidden).astype(half)
    d_hidden = jnp.concatenate(
        [
            jnp.dot(result_pair, down_a, preferred_element_type=jnp.float32),
            jnp.dot(result_pair, down_b, preferred_element_type=jnp.float32),
        ],
        axis=1,
    )
    sig = jax.nn.sigmoid(gate_pre)
    gate_grad = (d_hidden * up_pre * sig * (1.0 + gate_pre * (1.0 - sig))).astype(half)
    up_grad = (d_hidden * gate_pre * sig).astype(half)
    d_gate = across(second_pair, gate_grad).astype(half)
    d_up = across(second_pair, up_grad).astype(half)

    def unstage(value, factor, kept=jnp.bfloat16):
        return scatter_stage(value, factor, canon.index(factor), chips, kept)

    far_a = split_rows(jnp.concatenate([d_gate, d_down[:, :mid]], axis=1), canon)
    far_b = split_rows(jnp.concatenate([d_up, d_down[:, mid:]], axis=1), canon)
    for one, two in zip(order_a[:0:-1], order_b[:0:-1]):
        far_a, far_b = unstage(far_a, one), unstage(far_b, two)
    far_grad = unstage(jnp.concatenate([far_a, far_b], axis=-1), order_a[0], jnp.float32)
    far_grad = far_grad.reshape(far_grad.shape[-2:])
    feed_grad = jnp.stack(
        [
            far_grad[:, :hidden_cols],
            far_grad[:, hidden_cols + mid : 2 * hidden_cols + mid],
        ]
    )
    down_grad = jnp.concatenate(
        [far_grad[:, hidden_cols : hidden_cols + mid], far_grad[:, 2 * hidden_cols + mid :]], axis=1
    ).T

    second_part = against(gate_grad, far_gate) + against(up_grad, far_up)
    second_grad = second_part[:count] + swap(second_part[count:].astype(half)).astype(jnp.float32)
    pull_second = jax.vjp(modulate, middle, shift_b, scale_b)[1]
    d_middle, d_shift_b, d_scale_b = pull_second(second_grad)
    d_middle = d_middle + grad_out
    d_gate_a = d_middle * branch
    branch_grad = (gate_a * d_middle).astype(half)
    branch_grad_own, branch_grad_other = parted(branch_grad)
    d_proj = across(
        jnp.concatenate([attended, attended_other], axis=0),
        jnp.concatenate([branch_grad_own, swap(branch_grad_other)], axis=0),
    ).astype(half)
    attended_grad = (
        (against(branch_grad_own, proj_own) + against(branch_grad_other, proj_other))
        .astype(half)
        .reshape(shape)
    )
    probs_again = jnp.exp(scores_of() - log_total)
    d_value = jnp.einsum(
        "hqk,qhd->khd", probs_again.astype(half), attended_grad, preferred_element_type=jnp.float32
    )
    d_probs = jnp.einsum("qhd,khd->hqk", attended_grad, value, preferred_element_type=jnp.float32)
    d_scores = (
        probs_again * (d_probs - jnp.sum(probs_again * d_probs, axis=-1, keepdims=True)) * scale
    ).astype(half)
    d_query = jnp.einsum("hqk,khd->qhd", d_scores, key, preferred_element_type=jnp.float32)
    d_key = jnp.einsum("hqk,qhd->khd", d_scores, query, preferred_element_type=jnp.float32)
    unturn = jax.vjp(
        lambda left, right: (rope(left, rows, cols), rope(right, rows, cols)), query_raw, key_raw
    )[1]
    d_query_raw, d_key_raw = unturn((d_query, d_key))
    mixed_grad = jnp.concatenate(
        [
            d_query_raw.reshape(count, width),
            d_key_raw.reshape(count, width),
            d_value.reshape(count, width),
        ],
        axis=1,
    ).astype(half)
    mixed_grad_own, mixed_grad_other = parted(mixed_grad)
    d_mix = across(
        jnp.concatenate([first_in, first_other], axis=0),
        jnp.concatenate([mixed_grad_own, swap(mixed_grad_other)], axis=0),
    ).astype(half)
    near_grad = jnp.concatenate([d_mix, d_proj], axis=1)
    cut = near_grad.shape[1] // 2
    near_a = split_rows(near_grad[:, :cut], canon)
    near_b = split_rows(near_grad[:, cut:], canon)
    for one, two in zip(order_a[:0:-1], order_b[:0:-1]):
        near_a, near_b = unstage(near_a, one), unstage(near_b, two)
    near_grad = unstage(jnp.concatenate([near_a, near_b], axis=-1), order_a[0], jnp.float32)
    near_grad = near_grad.reshape(near_grad.shape[-2:])
    mix_grad, proj_grad = near_grad[:, :mix_cols], near_grad[:, mix_cols:]

    first_grad = against(mixed_grad_own, mix_own) + against(mixed_grad_other, mix_other)
    pull_first = jax.vjp(modulate, inputs, shift_a, scale_a)[1]
    d_inputs, d_shift_a, d_scale_a = pull_first(first_grad)
    input_grad = d_inputs + d_middle
    member_low = member.astype(half)
    d_modulation = jnp.concatenate(
        [
            across(member_low, piece.astype(half))
            for piece in (d_shift_a, d_scale_a, d_gate_a, d_shift_b, d_scale_b, d_gate_b)
        ],
        axis=1,
    ).astype(half)
    mod_own, mod_other = parted(d_modulation)
    mod_all = gather_small(jnp.concatenate([mod_own, swap(mod_other)], axis=0), chips)
    mod_all = mod_all.reshape(-1, cond_cols)
    cond_grad = across(cond_low, mod_all)
    bias_half = jnp.sum(mod_all.astype(jnp.float32), axis=0)[None, :]
    bias_full = joined(bias_half, swap(bias_half))[0]
    bias_size = cond_bias.shape[0]
    bias_grad = lax.dynamic_slice_in_dim(bias_full, (2 * tok + side) * bias_size, bias_size, 0)

    grads = (mix_grad, proj_grad, cond_grad, bias_grad, feed_grad, down_grad)
    local_squares = jnp.float32(0.0)
    for grad in grads:
        local_squares = local_squares + jnp.sum(grad * grad)
    grad_norm = jnp.sqrt(sum_all(local_squares, chips))
    factor = CLIP_NORM / jnp.maximum(grad_norm, CLIP_NORM)
    params = (mix_weight, proj_weight, cond_weight, cond_bias, feed_weight, down_weight)
    means = (mix_mean, proj_mean, cond_mean, bias_mean, feed_mean, down_mean)
    squares_old = (mix_square, proj_square, cond_square, bias_square, feed_square, down_square)
    updates = [adam(w, m, v, g * factor) for w, m, v, g in zip(params, means, squares_old, grads)]
    return (
        block_output,
        input_grad,
        grad_norm,
        updates[0][0],
        updates[1][0],
        updates[2][0],
        updates[3][0],
        updates[4][0],
        updates[5][0],
        updates[0][1],
        updates[1][1],
        updates[2][1],
        updates[3][1],
        updates[4][1],
        updates[5][1],
        updates[0][2],
        updates[1][2],
        updates[2][2],
        updates[3][2],
        updates[4][2],
        updates[5][2],
    )


def solution(mesh):
    placed = (
        P(("tok", "mlp"), None),
        P(("tok", "mlp"), None),
        P(),
        P(),
        P(("tok", "mlp")),
        P(("tok", "mlp")),
        P(("tok", "mlp")),
        P(("tok", "mlp")),
        P("tok", "mlp"),
        P("tok", "mlp"),
        P("tok", "mlp"),
        P(("tok", "mlp")),
        P(None, "tok", "mlp"),
        P("mlp", "tok"),
        P("tok", "mlp"),
        P("tok", "mlp"),
        P("tok", "mlp"),
        P(("tok", "mlp")),
        P(None, "tok", "mlp"),
        P("mlp", "tok"),
        P("tok", "mlp"),
        P("tok", "mlp"),
        P("tok", "mlp"),
        P(("tok", "mlp")),
        P(None, "tok", "mlp"),
        P("mlp", "tok"),
    )
    return jax.shard_map(
        body,
        mesh=mesh,
        in_specs=placed,
        out_specs=(
            P(("tok", "mlp"), None),
            P(("tok", "mlp"), None),
            P(),
            P("tok", "mlp"),
            P("tok", "mlp"),
            P("tok", "mlp"),
            P(("tok", "mlp")),
            P(None, "tok", "mlp"),
            P("mlp", "tok"),
            P("tok", "mlp"),
            P("tok", "mlp"),
            P("tok", "mlp"),
            P(("tok", "mlp")),
            P(None, "tok", "mlp"),
            P("mlp", "tok"),
            P("tok", "mlp"),
            P("tok", "mlp"),
            P("tok", "mlp"),
            P(("tok", "mlp")),
            P(None, "tok", "mlp"),
            P("mlp", "tok"),
        ),
        check_vma=False,
    )
```

```python
import jax
import jax.numpy as jnp
from jax import lax
from jax.experimental import pallas as pl
from jax.experimental.pallas import tpu as pltpu
from jax.experimental.layout import Layout, with_layout_constraint
from jax.sharding import PartitionSpec as P

HEADS = 16
HEAD = 72
SLOTS = 4
STEP = 10


BETA_ONE = 0.9
BETA_TWO = 0.95
ADAM_EPS = 1e-08
RATE = 0.08
DECAY = 0.01
CLIP_NORM = 1.0
NORM_EPS = 1e-06
MASKED = -1e30
HIGH = lax.Precision.HIGHEST


def layer_norm(value):
    centered = value - jnp.mean(value, axis=-1, keepdims=True)
    spread = jnp.mean(centered * centered, axis=-1, keepdims=True)
    return centered * lax.rsqrt(spread + NORM_EPS)


def modulate(value, shift, scale):
    return layer_norm(value) * (1.0 + scale) + shift


def geometry(height, width, count):
    lengths = height * width
    ends = jnp.cumsum(lengths)
    starts = ends - lengths
    places = jnp.arange(count, dtype=jnp.int32)
    segment = jnp.sum((places[:, None] >= ends[None, :]).astype(jnp.int32), axis=1)
    member = segment[:, None] == jnp.arange(height.shape[0], dtype=jnp.int32)[None, :]
    start_tok = jnp.sum(jnp.where(member, starts[None, :], 0), axis=1)
    width_tok = jnp.maximum(jnp.sum(jnp.where(member, width[None, :], 0), axis=1), 1)
    offset = places - start_tok
    return (segment, member.astype(jnp.float32), offset // width_tok, offset % width_tok)


def across(left, right, precision=None):
    return lax.dot_general(
        left,
        right,
        (((0,), (0,)), ((), ())),
        preferred_element_type=jnp.float32,
        precision=precision,
    )


def against(left, right):
    return lax.dot_general(
        left, right, (((1,), (1,)), ((), ())), preferred_element_type=jnp.float32
    )


def adam(weight, mean, square, grad):
    mean_new = BETA_ONE * mean + (1.0 - BETA_ONE) * grad
    square_new = BETA_TWO * square + (1.0 - BETA_TWO) * grad * grad
    fixed_mean = mean_new / (1.0 - BETA_ONE**STEP)
    fixed_square = square_new / (1.0 - BETA_TWO**STEP)
    weight_new = weight - RATE * (fixed_mean / (jnp.sqrt(fixed_square) + ADAM_EPS) + DECAY * weight)
    return (mean_new, square_new, weight_new)


BITS = {16: ((3, 2), ((0,), (1,))), 128: ((2, 1, 0), ((3, 4), (5, 6)))}


def orders(count):
    first, (one, two) = BITS[count]
    return first, one + two, two + one


def bit_of(bit):
    return (lax.axis_index("tok") >> bit) & 1


def trade(value, bit, count):
    return lax.ppermute(value, "tok", [(place, place ^ (1 << bit)) for place in range(count)])


def axis_of(bit, count):
    return count.bit_length() - 2 - bit


def swap(value):
    return lax.ppermute(value, "mlp", [(0, 1), (1, 0)])


def swap_rows(value, count):
    blocks = value.reshape((2,) * (count.bit_length() - 1) + (-1, value.shape[-1]))
    return swap(blocks).reshape(value.shape)


def split_rows(value, count):
    axes = (2,) * (count.bit_length() - 1)
    return value.reshape(*axes, value.shape[0] // count, value.shape[1])


def put(out, value, places, count):
    start = [0] * out.ndim
    for axis, place in places.items():
        start[axis] = place
    return lax.dynamic_update_slice(out, value, tuple(start))


def doubled(value, bit, count):
    axis = axis_of(bit, count)
    out = jnp.concatenate([value, value], axis=axis)
    return put(out, trade(value, bit, count), {axis: 1 - bit_of(bit)}, count)


SCORE_SCALE = HEAD ** (-0.5)


def cost(micros):
    return pl.CostEstimate(flops=int(micros * 0.460e9), bytes_accessed=1000, transcendentals=0)


def turn(value, cosine, up, down):
    quarter = HEAD // 4
    above = pltpu.roll(value, HEAD - quarter, 0)
    below = pltpu.roll(value, quarter, 0)
    return value * cosine + above * up + below * down


def dots(left, right, left_axis, right_axis):
    return lax.dot_general(
        left,
        right,
        (((left_axis,), (right_axis,)), ((), ())),
        preferred_element_type=jnp.float32,
    )


def attend_kernel(
    q_ref, k_ref, v_ref, cos_ref, up_ref, down_ref, row_ref, col_ref,
    out_ref, log_ref, q_out, k_out, v_out,
):
    cosine, up, down = cos_ref[...], up_ref[...], down_ref[...]
    query = turn(q_ref[0, 0], cosine, up, down).astype(jnp.bfloat16)
    key = turn(k_ref[0, 0], cosine, up, down).astype(jnp.bfloat16)
    value = v_ref[0, 0].astype(jnp.bfloat16)
    q_out[0], k_out[0], v_out[0] = query, key, value
    scores = dots(key, query, 0, 0) * SCORE_SCALE
    scores = jnp.where(col_ref[...] == row_ref[...], scores, MASKED)
    top = jnp.max(scores, axis=0, keepdims=True)
    weights = jnp.exp(scores - top)
    total = jnp.sum(weights, axis=0, keepdims=True)
    mixed = dots(value, weights.astype(jnp.bfloat16), 1, 0)
    out_ref[0] = (mixed * (1.0 / total)).astype(jnp.bfloat16)
    log_ref[0] = top + jnp.log(total)


def whole(value):
    return pl.BlockSpec(value.shape, lambda i: (0,) * value.ndim)


def attend(mixed, tables):
    _, heads, _, tokens = mixed.shape

    def part(place):
        return pl.BlockSpec((1, 1, HEAD, tokens), lambda i: (place, i, 0, 0))

    block = pl.BlockSpec((1, HEAD, tokens), lambda i: (i, 0, 0))
    line = pl.BlockSpec((1, 1, tokens), lambda i: (i, 0, 0))
    shape = jax.ShapeDtypeStruct((heads, HEAD, tokens), jnp.bfloat16)
    return pl.pallas_call(
        attend_kernel,
        grid=(heads,),
        in_specs=[part(0), part(1), part(2)] + [whole(value) for value in tables],
        out_specs=[block, line, block, block, block],
        out_shape=[
            shape,
            jax.ShapeDtypeStruct((heads, 1, tokens), jnp.float32),
            shape,
            shape,
            shape,
        ],
        compiler_params=pltpu.CompilerParams(vmem_limit_bytes=32 << 20),
        cost_estimate=cost(6),
        name="attend",
    )(mixed, mixed, mixed, *tables)


def attend_back_kernel(
    q_ref, k_ref, v_ref, g_ref, log_ref, cos_ref, up_ref, down_ref, row_ref, col_ref, out_ref
):
    query, key, value, grad = q_ref[0], k_ref[0], v_ref[0], g_ref[0]
    scores = dots(key, query, 0, 0) * SCORE_SCALE
    scores = jnp.where(col_ref[...] == row_ref[...], scores, MASKED)
    probs = jnp.exp(scores - log_ref[0])
    d_probs = dots(value, grad, 0, 0)
    inner = jnp.sum(probs * d_probs, axis=0, keepdims=True)
    d_scores = (probs * (d_probs - inner) * SCORE_SCALE).astype(jnp.bfloat16)
    d_value = dots(grad, probs.astype(jnp.bfloat16), 1, 1)
    d_key = dots(query, d_scores, 1, 1)
    d_query = dots(key, d_scores, 1, 0)
    cosine, up, down = cos_ref[...], -up_ref[...], -down_ref[...]
    out_ref[0, 0] = turn(d_query, cosine, up, down).astype(jnp.bfloat16)
    out_ref[1, 0] = turn(d_key, cosine, up, down).astype(jnp.bfloat16)
    out_ref[2, 0] = d_value.astype(jnp.bfloat16)


def attend_back(query, key, value, grad, logs, tables):
    heads, _, tokens = query.shape
    block = pl.BlockSpec((1, HEAD, tokens), lambda i: (i, 0, 0))
    line = pl.BlockSpec((1, 1, tokens), lambda i: (i, 0, 0))
    return pl.pallas_call(
        attend_back_kernel,
        grid=(heads,),
        in_specs=[block] * 4 + [line] + [whole(item) for item in tables],
        out_specs=pl.BlockSpec((3, 1, HEAD, tokens), lambda i: (0, i, 0, 0)),
        out_shape=jax.ShapeDtypeStruct((3, heads, HEAD, tokens), jnp.bfloat16),
        compiler_params=pltpu.CompilerParams(vmem_limit_bytes=32 << 20),
        cost_estimate=cost(10),
        name="attend_back",
    )(query, key, value, grad, logs, *tables)


def turn_tables(rows, cols):
    quarter = HEAD // 4
    freq = 10000.0 ** (-jnp.arange(quarter, dtype=jnp.float32) / quarter)
    row_angle = freq[:, None] * rows.astype(jnp.float32)[None, :]
    col_angle = freq[:, None] * cols.astype(jnp.float32)[None, :]
    zero = jnp.zeros_like(row_angle)
    cosine = jnp.concatenate([jnp.cos(row_angle)] * 2 + [jnp.cos(col_angle)] * 2, axis=0)
    up = jnp.concatenate([-jnp.sin(row_angle), zero, -jnp.sin(col_angle), zero], axis=0)
    down = jnp.concatenate([zero, jnp.sin(row_angle), zero, jnp.sin(col_angle)], axis=0)
    return cosine, up, down


def heads_kernel(x_ref, w_ref, *refs):
    out_ref = refs[-1]
    step = min(256, x_ref.shape[0])
    for start in range(0, x_ref.shape[0], step):
        rows = slice(start, start + step)
        product = dots(x_ref[rows, :], w_ref[:, : out_ref.shape[0]], 1, 0)
        out_ref[:, rows] = product.T


def heads_of(value, weight, columns, *others):
    shape = (columns, value.shape[0])
    return pl.pallas_call(
        heads_kernel,
        in_specs=[pl.BlockSpec(memory_space=pltpu.VMEM)] * 2
        + [pl.BlockSpec(memory_space=pl.ANY)] * len(others),
        out_shape=jax.ShapeDtypeStruct(shape, jnp.float32),
        compiler_params=pltpu.CompilerParams(vmem_limit_bytes=48 << 20),
        cost_estimate=cost(5),
        name="heads_of",
    )(value, weight, *others)


def back_kernel(one_ref, two_ref, w_one_ref, w_two_ref, out_ref, one_turn, two_turn):
    @pl.when(pl.program_id(0) == 0)
    def _():
        for ref, turn_ref in ((one_ref, one_turn), (two_ref, two_turn)):
            for start in range(0, ref.shape[1], 128):
                turn_ref[start : start + 128, :] = ref[:, start : start + 128].T

    size = one_turn.shape[1]
    out_ref[...] = dots(one_turn[...], w_one_ref[:, :size], 1, 1) + dots(
        two_turn[...], w_two_ref[:, :size], 1, 1
    )


def back_through(one, two, weight_one, weight_two):
    columns, tokens = one.shape
    rows = weight_one.shape[0]
    block = 384
    fixed = pl.BlockSpec((columns, tokens), lambda i: (0, 0))
    moving = pl.BlockSpec((block, weight_one.shape[1]), lambda i: (i, 0))
    return pl.pallas_call(
        back_kernel,
        grid=(rows // block,),
        in_specs=[fixed, fixed, moving, moving],
        out_specs=pl.BlockSpec((tokens, block), lambda i: (0, i)),
        out_shape=jax.ShapeDtypeStruct((tokens, rows), jnp.float32),
        scratch_shapes=[pltpu.VMEM((tokens, columns), jnp.bfloat16)] * 2,
        compiler_params=pltpu.CompilerParams(vmem_limit_bytes=48 << 20),
        cost_estimate=cost(9),
        name="back_through",
    )(one, two, weight_one, weight_two)


def block_index(chip, bits):
    place = 0
    for bit in bits:
        place = place * 2 + ((chip >> bit) & 1)
    return place


def other_bits(bits, count):
    return [bit for bit in range(count.bit_length() - 2, -1, -1) if bit not in bits]


def grad_parts(terms, turned, columns, parts, count, *others):
    left = terms[0][0][0][0]
    rows = left.shape[1] if turned else left.shape[0]
    size = rows // count
    chunk = rows // 4
    flat = [pair for term, _ in terms for pair in term]
    lefts = []
    for pair in flat:
        if not any(pair[0] is other for other in lefts):
            lefts.append(pair[0])

    def kernel(tok_ref, *refs):
        left_refs = refs[: len(lefts)]
        right_refs = refs[len(lefts) : len(lefts) + len(flat)]
        outs = refs[len(lefts) + len(flat) + len(others) :]
        outs, scratch = outs[: len(parts)], outs[len(parts) :]
        step = pl.program_id(0)
        tok = tok_ref[0]
        if turned:

            @pl.when(step == 0)
            def _():
                for left_ref, turn_ref in zip(left_refs, scratch):
                    for start in range(0, rows, 128):
                        turn_ref[start : start + 128, :] = left_ref[:, start : start + 128].T

        place = 0
        for term, start in terms:
            total = None
            for left, right, axis in term:
                which = [left is other for other in lefts].index(True)
                if turned:
                    part = scratch[which][pl.ds(pl.multiple_of(step * chunk, chunk), chunk), :]
                else:
                    part = left_refs[which][...]
                product = dots(part, right_refs[place][...], 1, axis)
                total = product if total is None else total + product
                place += 1
            width = total.shape[1]
            for block in range(chunk // size):
                value = total[block * size : (block + 1) * size, :].astype(jnp.bfloat16)
                mine = (step * (chunk // size) + block) ^ tok
                for out, fixed_bits in zip(outs, parts):
                    index = block_index(mine, other_bits(fixed_bits, count))
                    here = jnp.bool_(True)
                    for bit, wanted in fixed_bits.items():
                        here &= ((mine >> bit) & 1) == wanted

                    @pl.when(here)
                    def _():
                        out[index, :, start : start + width] = value

    def fixed(value):
        return pl.BlockSpec(value.shape, lambda i: (0,) * value.ndim)

    if turned:
        left_specs = [fixed(value) for value in lefts]
        scratch = [pltpu.VMEM(value.shape[::-1], value.dtype) for value in lefts]
    else:
        left_specs = [pl.BlockSpec((chunk, value.shape[1]), lambda i: (i, 0)) for value in lefts]
        scratch = []
    shapes = [(count >> len(part), size, columns) for part in parts]
    return pl.pallas_call(
        kernel,
        grid=(4,),
        in_specs=[pl.BlockSpec(memory_space=pltpu.SMEM)]
        + left_specs
        + [fixed(pair[1]) for pair in flat]
        + [pl.BlockSpec(memory_space=pl.ANY)] * len(others),
        out_specs=[pl.BlockSpec(shape, lambda i: (0, 0, 0)) for shape in shapes],
        out_shape=[jax.ShapeDtypeStruct(shape, jnp.bfloat16) for shape in shapes],
        scratch_shapes=scratch,
        compiler_params=pltpu.CompilerParams(vmem_limit_bytes=56 << 20),
        cost_estimate=cost(6 * columns // 1024),
        name="grad_parts",
    )(lax.axis_index("tok").reshape(1), *lefts, *[pair[1] for pair in flat], *others)


def scatter_on(value, left_bits, order, count, last=jnp.bfloat16):
    left_bits = list(left_bits)
    sent = []
    for bit in order:
        value = value.reshape((2,) * len(left_bits) + value.shape[-2:])
        axis = left_bits.index(bit)
        away = lax.index_in_dim(value, 1, axis, keepdims=False)
        sent.append(away)
        kept = last if bit == order[-1] else jnp.bfloat16
        value = add(lax.index_in_dim(value, 0, axis, keepdims=False), trade(away, bit, count), kept)
        left_bits.remove(bit)
    return value, sent


def plain_products(terms, turned, columns):
    pieces = []
    for place, (term, start) in enumerate(terms):
        total = sum(dots(one, two, 0 if turned else 1, axis) for one, two, axis in term)
        end = terms[place + 1][1] if place + 1 < len(terms) else columns
        total = jnp.pad(total, ((0, 0), (0, end - start - total.shape[1])))
        pieces.append(total.astype(jnp.bfloat16))
    return pieces


def row_size(terms, turned, count):
    left = terms[0][0][0][0]
    return (left.shape[1] if turned else left.shape[0]) // count


def chain_scatter(terms, turned, columns, count, *others):
    first, order, _ = orders(count)
    bits = first[::-1] + order
    if row_size(terms, turned, count) % 8:
        half, sent = half_scatter(plain_products(terms, turned, columns), count)
        return sent[:1], [half], lambda value: last_scatter(value[0], count)
    away, kept = grad_parts(terms, turned, columns, [{bits[0]: 1}, {bits[0]: 0}], count, *others)
    left_bits = other_bits(bits[:1], count)
    value = add(kept, trade(away, bits[0], count))
    value, sent = scatter_on(value, left_bits, bits[1 : len(first)], count)
    left_bits = [bit for bit in left_bits if bit in order]
    return (
        sent[:1],
        [value],
        lambda value: scatter_on(value[0], left_bits, order, count, jnp.float32)[0],
    )


def across_scatter(terms, turned, columns, count):
    first, order_a, order_b = orders(count)
    if row_size(terms, turned, count) % 8:
        half, sent = half_scatter(plain_products(terms, turned, columns), count)
        return [half], sent, [], [], lambda value: last_scatter(value[0], count)
    half_bit = first[-1]
    parts = [
        {half_bit: half, order[-1]: away}
        for half, order in enumerate((order_a, order_b))
        for away in (1, 0)
    ]
    blocks = grad_parts(terms, turned, columns, parts, count)
    halves, firsts, mids = [], [], []
    for place, order in enumerate((order_a, order_b)):
        away, kept = blocks[2 * place : 2 * place + 2]
        left_bits = other_bits((order[-1], half_bit), count)
        value = add(kept, trade(away, order[-1], count))
        firsts.append(value)
        value, sent = scatter_on(value, left_bits, order[-2::-1], count)
        halves.append(value)
        mids += sent[:1]

    def finish(halves):
        kept, away = halves
        value = add(kept, trade(away, half_bit, count))
        left_bits = [bit for bit in other_bits((), count) if bit in first[:-1]]
        return scatter_on(value, left_bits, first[-2::-1], count, jnp.float32)[0]

    return halves, [blocks[0], blocks[2]], firsts, mids, finish


def row_major(value):
    return with_layout_constraint(value, Layout(tuple(range(value.ndim))))


def add(one, two, kept=jnp.bfloat16):
    return (one.astype(jnp.float32) + two.astype(jnp.float32)).astype(kept)


def after(value, *others, micros=1):
    def keep(*refs):
        pass

    anywhere = pl.BlockSpec(memory_space=pl.ANY)
    return pl.pallas_call(
        keep,
        in_specs=[anywhere] * (1 + len(others)),
        out_specs=anywhere,
        out_shape=jax.ShapeDtypeStruct(value.shape, value.dtype),
        input_output_aliases={0: 0},
        cost_estimate=cost(micros),
        name="after",
    )(value, *others)


def first_gather(shard, count):
    first, _, _ = orders(count)
    value = shard.reshape((1,) * (count.bit_length() - 1) + shard.shape)
    for bit in first:
        value = doubled(value, bit, count)
    return value


def next_gather(value, count):
    first, order_a, order_b = orders(count)
    axis = axis_of(first[-1], count)
    halves = [
        lax.slice_in_dim(value, 0, 1, axis=axis),
        lax.slice_in_dim(value, 1, 2, axis=axis),
    ]
    for one, two in zip(order_a[:-1], order_b[:-1]):
        halves = [doubled(half, bit, count) for half, bit in zip(halves, (one, two))]
    return halves


def last_gather(halves, count):
    first, order_a, order_b = orders(count)
    axis = axis_of(first[-1], count)
    lasts = (order_a[-1], order_b[-1])
    moved = [trade(half, bit, count) for half, bit in zip(halves, lasts)]
    out = jnp.concatenate(
        [
            jnp.concatenate([half, half], axis=axis_of(bit, count))
            for half, bit in zip(halves, lasts)
        ],
        axis=axis,
    )
    for place, (bit, value) in enumerate(zip(lasts, moved)):
        out = put(out, value, {axis: place, axis_of(bit, count): 1 - bit_of(bit)}, count)
    return out.reshape(-1, out.shape[-1])


def halved(pieces, bit, count, kept):
    axis = axis_of(bit, count)
    digit = bit_of(bit)

    def part(place):
        parts = [lax.dynamic_slice_in_dim(piece, place, 1, axis) for piece in pieces]
        return parts[0] if len(parts) == 1 else jnp.concatenate(parts, axis=-1)

    sent = part(1 - digit).astype(jnp.bfloat16)
    total = part(digit).astype(jnp.float32) + trade(sent, bit, count).astype(jnp.float32)
    return total.astype(kept), sent


def half_scatter(values, count):
    first, order_a, order_b = orders(count)
    values = [split_rows(value, count) for value in values]
    axis = axis_of(first[-1], count)
    first_sent, out = [], []
    for place, order in enumerate((order_a[::-1], order_b[::-1])):
        pieces = [lax.slice_in_dim(value, place, place + 1, axis=axis) for value in values]
        for step, bit in enumerate(order):
            total, sent = halved(pieces, bit, count, jnp.bfloat16)
            if step == 0:
                first_sent.append(sent)
            pieces = [total]
        out.append(pieces[0])
    return jnp.concatenate(out, axis=axis), first_sent


def last_scatter(value, count):
    first, _, _ = orders(count)
    for bit in first[::-1]:
        value, _ = halved([value], bit, count, jnp.bfloat16 if bit != first[0] else jnp.float32)
    return value.reshape(value.shape[-2:])


def gather_small(value, count, bits):
    for bit in bits:
        value = jnp.concatenate([value, trade(value, bit, count)], axis=axis_of(bit, count))
    return value


def spread(value, count):
    return value.reshape((1,) * (count.bit_length() - 1) + value.shape)


def stacked(value, count):
    return value.reshape((-1,) + value.shape[count.bit_length() :])


def scatter_small(value, count, bits):
    for bit in bits:
        axis = axis_of(bit, count)
        sent = lax.slice_in_dim(value, 1, 2, axis=axis).astype(jnp.bfloat16)
        moved = trade(sent, bit, count).astype(jnp.float32)
        value = lax.slice_in_dim(value, 0, 1, axis=axis) + moved
    return value


def sum_all(value, count):
    value = value + swap(value)
    for bit in range(count.bit_length() - 1):
        value = value + trade(value, bit, count)
    return value


def pick(segment, table):
    out = jnp.zeros((segment.shape[0], table.shape[1]), jnp.float32)
    for slot in range(SLOTS):
        out = jnp.where(segment[:, None] == slot, table[slot][None, :], out)
    return out


def body(
    block_input,
    out_grad,
    class_table,
    time_table,
    class_label,
    time_index,
    grid_height,
    grid_width,
    mix_weight,
    proj_weight,
    cond_weight,
    cond_bias,
    feed_weight,
    down_weight,
    mix_mean,
    proj_mean,
    cond_mean,
    bias_mean,
    feed_mean,
    down_mean,
    mix_square,
    proj_square,
    cond_square,
    bias_square,
    feed_square,
    down_square,
):
    half = jnp.bfloat16
    count = block_input.shape[0]
    width = block_input.shape[1]
    chips = lax.axis_size("tok")
    tok = lax.axis_index("tok")
    side = lax.axis_index("mlp")
    first_side = side == 0
    rows_own = mix_weight.shape[0]
    mix_cols = mix_weight.shape[1]
    proj_cols = proj_weight.shape[1]
    hidden_cols = feed_weight.shape[2]
    cond_cols = cond_weight.shape[1]
    group = mix_cols // 3
    heads = HEADS // 2

    def joined(own, other, axis=1):
        low = jnp.where(first_side, own, other)
        high = jnp.where(first_side, other, own)
        return jnp.concatenate([low, high], axis=axis)

    def parted(value):
        size = value.shape[1] // 2
        low, high = value[:, :size], value[:, size:]
        return jnp.where(first_side, low, high), jnp.where(first_side, high, low)

    codes = jnp.stack([class_label, time_index], axis=1)
    first, order, _ = orders(chips)
    codes = spread(jnp.concatenate([codes, swap(codes)], axis=0), chips)
    codes = gather_small(codes, chips, first)

    mix_low = mix_weight.astype(half)
    mix_parts = [mix_low[:, :group], mix_low[:, group : 2 * group], mix_low[:, 2 * group :]]
    mix_moved = swap(mix_parts[1])
    mix_shard = jnp.where(
        first_side,
        jnp.concatenate([mix_parts[0], mix_parts[2], mix_moved], axis=1),
        jnp.concatenate([mix_moved, mix_parts[0], mix_parts[2]], axis=1),
    )
    mix_shard = jnp.concatenate([mix_shard, proj_weight.astype(half)], axis=1)
    mix_first = spread(after(mix_shard, codes), chips)
    mix_first = doubled(mix_first, first[0], chips)
    codes = gather_small(after(codes, mix_first), chips, order)
    codes = stacked(codes, chips)
    labels, times = codes[:, 0], codes[:, 1]
    for bit in first[1:]:
        mix_first = doubled(mix_first, bit, chips)

    start = tok * rows_own
    class_part = lax.dynamic_slice_in_dim(class_table, start, rows_own, 1)
    time_part = lax.dynamic_slice_in_dim(time_table, start, rows_own, 1)
    class_hot = (labels[:, None] == jnp.arange(class_table.shape[0])[None, :]).astype(half)
    time_hot = (times[:, None] == jnp.arange(time_table.shape[0])[None, :]).astype(half)
    embed = jnp.dot(class_hot, class_part, preferred_element_type=jnp.float32) + jnp.dot(
        time_hot, time_part, preferred_element_type=jnp.float32
    )
    cond_low = jax.nn.silu(embed).astype(half)
    partial_mod = jnp.dot(cond_low, cond_weight.astype(half), preferred_element_type=jnp.float32)
    bias_low = cond_bias.astype(half).astype(jnp.float32)
    bias_pair = joined(bias_low[None, :], swap(bias_low)[None, :])[0]
    bias_start = tok * bias_pair.shape[0]
    bias_side = bias_start // cond_cols
    bias_pair = jnp.where(bias_side == side, bias_pair, 0.0)
    bias_row = lax.dynamic_update_slice(
        jnp.zeros((cond_cols,), jnp.float32), bias_pair, (bias_start - bias_side * cond_cols,)
    )
    mod_half = split_rows(partial_mod + bias_row[None, :], chips)
    mod_half = scatter_small(mod_half, chips, order[:1])
    mod_half = scatter_small(after(mod_half, mix_first), chips, order[1:])
    far_down = spread(down_weight.T.astype(half), chips)
    for bit in order:
        far_down = doubled(far_down, bit, chips)
    mix_halves = next_gather(after(mix_first, mod_half, far_down), chips)
    mod_half = scatter_small(mod_half, chips, first[::-1])
    mod_half = mod_half.reshape(-1, cond_cols)
    slots = class_label.shape[0]
    modulation = joined(mod_half[:slots], swap(mod_half[slots:]))

    mix_own = last_gather(mix_halves, chips)
    far = jnp.concatenate([feed_weight[0].astype(half), feed_weight[1].astype(half)], axis=1)
    far = first_gather(after(far, mix_first), chips)
    far_down = after(far_down, far)
    for bit in first:
        far_down = doubled(far_down, bit, chips)
    far_down = far_down.reshape(width, hidden_cols)
    far = last_gather(next_gather(after(far, mix_own), chips), chips)
    far_gate, far_up = far[:, :hidden_cols], far[:, hidden_cols:]
    mix_other = swap_rows(mix_own, chips)
    proj_full = joined(mix_own[:, mix_cols:], mix_other[:, mix_cols:])

    segment, member, rows, cols = geometry(grid_height, grid_width, count)
    tables = turn_tables(rows, cols) + (segment[None, :], segment[:, None])
    valid = (segment < SLOTS).astype(jnp.float32)[:, None]
    shift_a, scale_a, gate_a, shift_b, scale_b, gate_b = (
        pick(segment, table) for table in jnp.split(modulation, 6, axis=1)
    )
    inputs = block_input.astype(jnp.float32)
    first_in = modulate(inputs, shift_a, scale_a).astype(half)
    first_turned = after(first_in.T, first_in)
    first_moved = swap(first_turned)

    shape = (3, heads, HEAD, count)
    att_own, log_own, *qkv_own = attend(
        heads_of(first_in, mix_own, mix_cols).reshape(shape), tables
    )
    att_other, log_other, *qkv_other = attend(
        heads_of(first_in, mix_other, mix_cols, first_moved).reshape(shape), tables
    )
    attended = joined(att_own, att_other, 0).reshape(width, count)
    attended_moved = swap(attended)
    branch = dots(attended, proj_full, 0, 0)
    middle = inputs + gate_a * branch
    second_in = modulate(middle, shift_b, scale_b).astype(half)
    second_pair = jnp.concatenate([second_in, swap(second_in)], axis=0)
    gate_pre = jnp.dot(second_pair, far_gate, preferred_element_type=jnp.float32)
    up_pre = jnp.dot(second_pair, far_up, preferred_element_type=jnp.float32)
    hidden = (jax.nn.silu(gate_pre) * up_pre).astype(half)
    partial_value = against(hidden, far_down)
    result = partial_value[:count] + swap(partial_value[count:].astype(half)).astype(jnp.float32)
    block_output = (valid * (middle + gate_b * result)).astype(half)

    grad_out = valid * out_grad.astype(jnp.float32)
    d_gate_b = grad_out * result
    result_grad = (gate_b * grad_out).astype(half)
    result_pair = jnp.concatenate([result_grad, swap(result_grad)], axis=0)
    down_sent, down_half, down_finish = chain_scatter(
        [([(result_pair, hidden, 0)], 0)], True, hidden_cols, chips, attended_moved
    )
    d_hidden = jnp.dot(result_pair, far_down, preferred_element_type=jnp.float32)
    sig = jax.nn.sigmoid(gate_pre)
    gate_grad = (d_hidden * up_pre * sig * (1.0 + gate_pre * (1.0 - sig))).astype(half)
    up_grad = (d_hidden * gate_pre * sig).astype(half)
    feed_half, _, _, feed_mids, feed_finish = across_scatter(
        [([(second_pair, gate_grad, 0)], 0), ([(second_pair, up_grad, 0)], hidden_cols)],
        True,
        2 * hidden_cols,
        chips,
    )
    second_part = against(gate_grad, far_gate) + against(up_grad, far_up)
    second_grad = second_part[:count] + swap(second_part[count:].astype(half)).astype(jnp.float32)
    pull_second = jax.vjp(modulate, middle, shift_b, scale_b)[1]
    d_middle, d_shift_b, d_scale_b = pull_second(second_grad)
    d_middle = d_middle + grad_out
    d_gate_a = d_middle * branch
    branch_grad = (gate_a * d_middle).astype(half)
    attended_grad = dots(proj_full, branch_grad, 1, 1).astype(half).reshape(HEADS, HEAD, count)
    grad_own = lax.dynamic_slice_in_dim(attended_grad, side * heads, heads, 0)
    grad_other = lax.dynamic_slice_in_dim(attended_grad, (1 - side) * heads, heads, 0)
    grad_other = after(grad_other, *down_sent)
    mg_other = attend_back(*qkv_other, grad_other, log_other, tables).reshape(mix_cols, count)
    mg_moved = swap(mg_other)
    grad_own = after(grad_own, mg_other, *feed_mids)
    mg_own = attend_back(*qkv_own, grad_own, log_own, tables).reshape(mix_cols, count)
    branch_grad_own, branch_grad_other = parted(branch_grad)
    proj_start = -(-mix_cols // 128) * 128
    near_half, near_sent, near_firsts, _, near_finish = across_scatter(
        [
            ([(first_turned, mg_own, 1), (first_moved, mg_moved, 1)], 0),
            ([(attended, branch_grad_own, 0), (attended_moved, swap_rows(branch_grad_other, chips), 0)], proj_start),
        ],
        False,
        proj_start + proj_cols,
        chips,
    )
    down_grad = down_finish(jax.tree.map(lambda value: after(value, *near_sent), down_half)).T
    feed_grad = feed_finish(jax.tree.map(lambda value: after(value, *near_sent), feed_half))
    feed_grad = jnp.stack([feed_grad[:, :hidden_cols], feed_grad[:, hidden_cols:]])
    near_grad = near_finish(near_half)
    proj_grad = near_grad[:, proj_start:]
    mix_parts = [near_grad[:, place * group : (place + 1) * group] for place in range(3)]
    mix_moved = swap(jnp.where(first_side, mix_parts[2], mix_parts[0]))
    mix_grad = jnp.where(
        first_side,
        jnp.concatenate([mix_parts[0], mix_moved, mix_parts[1]], axis=1),
        jnp.concatenate([mix_parts[1], mix_moved, mix_parts[2]], axis=1),
    )

    mg_own, mg_other = after(mg_own, *near_sent), after(mg_other, *near_sent)
    first_grad = back_through(mg_own, mg_other, mix_own, mix_other)
    pull_first = jax.vjp(modulate, inputs, shift_a, scale_a)[1]
    d_inputs, d_shift_a, d_scale_a = pull_first(first_grad)
    input_grad = d_inputs + d_middle
    member_low = member.astype(half)
    d_modulation = jnp.concatenate(
        [
            across(member_low, piece.astype(half))
            for piece in (d_shift_a, d_scale_a, d_gate_a, d_shift_b, d_scale_b, d_gate_b)
        ],
        axis=1,
    ).astype(half)
    mod_own, mod_other = parted(d_modulation)
    mod_all = spread(jnp.concatenate([mod_own, swap(mod_other)], axis=0), chips)
    mod_all = after(gather_small(mod_all, chips, first), *near_firsts)
    mod_all = stacked(gather_small(mod_all, chips, order), chips)
    cond_grad = across(cond_low, mod_all)
    bias_half = jnp.sum(mod_all.astype(jnp.float32), axis=0)[None, :]
    bias_full = joined(bias_half, swap(bias_half))[0]
    bias_size = cond_bias.shape[0]
    bias_grad = lax.dynamic_slice_in_dim(bias_full, (2 * tok + side) * bias_size, bias_size, 0)

    grads = (mix_grad, proj_grad, cond_grad, bias_grad, feed_grad, down_grad)
    local_squares = jnp.float32(0.0)
    for grad in grads:
        local_squares = local_squares + jnp.sum(grad * grad)
    grad_norm = jnp.sqrt(sum_all(local_squares, chips))
    factor = CLIP_NORM / jnp.maximum(grad_norm, CLIP_NORM)
    params = (mix_weight, proj_weight, cond_weight, cond_bias, feed_weight, down_weight)
    means = (mix_mean, proj_mean, cond_mean, bias_mean, feed_mean, down_mean)
    squares_old = (mix_square, proj_square, cond_square, bias_square, feed_square, down_square)
    updates = [adam(w, m, v, g * factor) for w, m, v, g in zip(params, means, squares_old, grads)]
    return (
        block_output,
        input_grad,
        grad_norm,
        updates[0][0],
        updates[1][0],
        updates[2][0],
        updates[3][0],
        updates[4][0],
        updates[5][0],
        updates[0][1],
        updates[1][1],
        updates[2][1],
        updates[3][1],
        updates[4][1],
        updates[5][1],
        updates[0][2],
        updates[1][2],
        updates[2][2],
        updates[3][2],
        updates[4][2],
        updates[5][2],
    )


def solution(mesh):
    placed = (
        P(("tok", "mlp"), None),
        P(("tok", "mlp"), None),
        P(),
        P(),
        P(("tok", "mlp")),
        P(("tok", "mlp")),
        P(("tok", "mlp")),
        P(("tok", "mlp")),
        P("tok", "mlp"),
        P("tok", "mlp"),
        P("tok", "mlp"),
        P(("tok", "mlp")),
        P(None, "tok", "mlp"),
        P("mlp", "tok"),
        P("tok", "mlp"),
        P("tok", "mlp"),
        P("tok", "mlp"),
        P(("tok", "mlp")),
        P(None, "tok", "mlp"),
        P("mlp", "tok"),
        P("tok", "mlp"),
        P("tok", "mlp"),
        P("tok", "mlp"),
        P(("tok", "mlp")),
        P(None, "tok", "mlp"),
        P("mlp", "tok"),
    )
    return jax.shard_map(
        body,
        mesh=mesh,
        in_specs=placed,
        out_specs=(
            P(("tok", "mlp"), None),
            P(("tok", "mlp"), None),
            P(),
            P("tok", "mlp"),
            P("tok", "mlp"),
            P("tok", "mlp"),
            P(("tok", "mlp")),
            P(None, "tok", "mlp"),
            P("mlp", "tok"),
            P("tok", "mlp"),
            P("tok", "mlp"),
            P("tok", "mlp"),
            P(("tok", "mlp")),
            P(None, "tok", "mlp"),
            P("mlp", "tok"),
            P("tok", "mlp"),
            P("tok", "mlp"),
            P("tok", "mlp"),
            P(("tok", "mlp")),
            P(None, "tok", "mlp"),
            P("mlp", "tok"),
        ),
        check_vma=False,
    )
```

```python
import jax
import jax.numpy as jnp
from jax import lax
from jax.experimental import pallas as pl
from jax.experimental.pallas import tpu as pltpu
from jax.experimental.layout import Layout, with_layout_constraint
from jax.sharding import PartitionSpec as P

HEADS = 16
HEAD = 72
SLOTS = 4
STEP = 10


BETA_ONE = 0.9
BETA_TWO = 0.95
ADAM_EPS = 1e-08
RATE = 0.08
DECAY = 0.01
CLIP_NORM = 1.0
NORM_EPS = 1e-06
MASKED = -1e30
HIGH = lax.Precision.HIGHEST


def layer_norm(value):
    centered = value - jnp.mean(value, axis=-1, keepdims=True)
    spread = jnp.mean(centered * centered, axis=-1, keepdims=True)
    return centered * lax.rsqrt(spread + NORM_EPS)


def modulate(value, shift, scale):
    return layer_norm(value) * (1.0 + scale) + shift


def geometry(height, width, count):
    lengths = height * width
    ends = jnp.cumsum(lengths)
    starts = ends - lengths
    places = jnp.arange(count, dtype=jnp.int32)
    segment = jnp.sum((places[:, None] >= ends[None, :]).astype(jnp.int32), axis=1)
    member = segment[:, None] == jnp.arange(height.shape[0], dtype=jnp.int32)[None, :]
    start_tok = jnp.sum(jnp.where(member, starts[None, :], 0), axis=1)
    width_tok = jnp.maximum(jnp.sum(jnp.where(member, width[None, :], 0), axis=1), 1)
    offset = places - start_tok
    return (segment, member.astype(jnp.float32), offset // width_tok, offset % width_tok)


def across(left, right, precision=None):
    return lax.dot_general(
        left,
        right,
        (((0,), (0,)), ((), ())),
        preferred_element_type=jnp.float32,
        precision=precision,
    )


def against(left, right):
    return lax.dot_general(
        left, right, (((1,), (1,)), ((), ())), preferred_element_type=jnp.float32
    )


def adam(weight, mean, square, grad):
    mean_new = BETA_ONE * mean + (1.0 - BETA_ONE) * grad
    square_new = BETA_TWO * square + (1.0 - BETA_TWO) * grad * grad
    fixed_mean = mean_new / (1.0 - BETA_ONE**STEP)
    fixed_square = square_new / (1.0 - BETA_TWO**STEP)
    weight_new = weight - RATE * (fixed_mean / (jnp.sqrt(fixed_square) + ADAM_EPS) + DECAY * weight)
    return (mean_new, square_new, weight_new)


BITS = {16: ((3, 2), ((0,), (1,))), 128: ((2, 1, 0), ((3, 4), (5, 6)))}


def orders(count):
    first, (one, two) = BITS[count]
    return first, one + two, two + one


def bit_of(bit):
    return (lax.axis_index("tok") >> bit) & 1


def trade(value, bit, count):
    return lax.ppermute(value, "tok", [(place, place ^ (1 << bit)) for place in range(count)])


def axis_of(bit, count):
    return count.bit_length() - 2 - bit


def swap(value):
    return lax.ppermute(value, "mlp", [(0, 1), (1, 0)])


def swap_rows(value, count):
    blocks = value.reshape((2,) * (count.bit_length() - 1) + (-1, value.shape[-1]))
    return swap(blocks).reshape(value.shape)


def split_rows(value, count):
    axes = (2,) * (count.bit_length() - 1)
    return value.reshape(*axes, value.shape[0] // count, value.shape[1])


def put(out, value, places, count):
    start = [0] * out.ndim
    for axis, place in places.items():
        start[axis] = place
    return lax.dynamic_update_slice(out, value, tuple(start))


def doubled(value, bit, count):
    axis = axis_of(bit, count)
    out = jnp.concatenate([value, value], axis=axis)
    return put(out, trade(value, bit, count), {axis: 1 - bit_of(bit)}, count)


SCORE_SCALE = HEAD ** (-0.5)


def cost(micros):
    return pl.CostEstimate(flops=int(micros * 0.460e9), bytes_accessed=1000, transcendentals=0)


def turn(value, cosine, up, down):
    quarter = HEAD // 4
    above = pltpu.roll(value, HEAD - quarter, 0)
    below = pltpu.roll(value, quarter, 0)
    return value * cosine + above * up + below * down


def dots(left, right, left_axis, right_axis):
    return lax.dot_general(
        left,
        right,
        (((left_axis,), (right_axis,)), ((), ())),
        preferred_element_type=jnp.float32,
    )


def attend_kernel(
    q_ref, k_ref, v_ref, cos_ref, up_ref, down_ref, row_ref, col_ref,
    out_ref, log_ref, q_out, k_out, v_out,
):
    cosine, up, down = cos_ref[...], up_ref[...], down_ref[...]
    query = turn(q_ref[0, 0], cosine, up, down).astype(jnp.bfloat16)
    key = turn(k_ref[0, 0], cosine, up, down).astype(jnp.bfloat16)
    value = v_ref[0, 0].astype(jnp.bfloat16)
    q_out[0], k_out[0], v_out[0] = query, key, value
    scores = dots(key, query, 0, 0) * SCORE_SCALE
    scores = jnp.where(col_ref[...] == row_ref[...], scores, MASKED)
    top = jnp.max(scores, axis=0, keepdims=True)
    weights = jnp.exp(scores - top)
    total = jnp.sum(weights, axis=0, keepdims=True)
    mixed = dots(value, weights.astype(jnp.bfloat16), 1, 0)
    out_ref[0] = (mixed * (1.0 / total)).astype(jnp.bfloat16)
    log_ref[0] = top + jnp.log(total)


def whole(value):
    return pl.BlockSpec(value.shape, lambda i: (0,) * value.ndim)


def attend(mixed, tables):
    _, heads, _, tokens = mixed.shape

    def part(place):
        return pl.BlockSpec((1, 1, HEAD, tokens), lambda i: (place, i, 0, 0))

    block = pl.BlockSpec((1, HEAD, tokens), lambda i: (i, 0, 0))
    line = pl.BlockSpec((1, 1, tokens), lambda i: (i, 0, 0))
    shape = jax.ShapeDtypeStruct((heads, HEAD, tokens), jnp.bfloat16)
    return pl.pallas_call(
        attend_kernel,
        grid=(heads,),
        in_specs=[part(0), part(1), part(2)] + [whole(value) for value in tables],
        out_specs=[block, line, block, block, block],
        out_shape=[
            shape,
            jax.ShapeDtypeStruct((heads, 1, tokens), jnp.float32),
            shape,
            shape,
            shape,
        ],
        compiler_params=pltpu.CompilerParams(vmem_limit_bytes=32 << 20),
        cost_estimate=cost(6),
        name="attend",
    )(mixed, mixed, mixed, *tables)


def attend_back_kernel(
    q_ref, k_ref, v_ref, g_ref, log_ref, cos_ref, up_ref, down_ref, row_ref, col_ref, out_ref
):
    query, key, value, grad = q_ref[0], k_ref[0], v_ref[0], g_ref[0]
    scores = dots(key, query, 0, 0) * SCORE_SCALE
    scores = jnp.where(col_ref[...] == row_ref[...], scores, MASKED)
    probs = jnp.exp(scores - log_ref[0])
    d_probs = dots(value, grad, 0, 0)
    inner = jnp.sum(probs * d_probs, axis=0, keepdims=True)
    d_scores = (probs * (d_probs - inner) * SCORE_SCALE).astype(jnp.bfloat16)
    d_value = dots(grad, probs.astype(jnp.bfloat16), 1, 1)
    d_key = dots(query, d_scores, 1, 1)
    d_query = dots(key, d_scores, 1, 0)
    cosine, up, down = cos_ref[...], -up_ref[...], -down_ref[...]
    out_ref[0, 0] = turn(d_query, cosine, up, down).astype(jnp.bfloat16)
    out_ref[1, 0] = turn(d_key, cosine, up, down).astype(jnp.bfloat16)
    out_ref[2, 0] = d_value.astype(jnp.bfloat16)


def attend_back(query, key, value, grad, logs, tables):
    heads, _, tokens = query.shape
    block = pl.BlockSpec((1, HEAD, tokens), lambda i: (i, 0, 0))
    line = pl.BlockSpec((1, 1, tokens), lambda i: (i, 0, 0))
    return pl.pallas_call(
        attend_back_kernel,
        grid=(heads,),
        in_specs=[block] * 4 + [line] + [whole(item) for item in tables],
        out_specs=pl.BlockSpec((3, 1, HEAD, tokens), lambda i: (0, i, 0, 0)),
        out_shape=jax.ShapeDtypeStruct((3, heads, HEAD, tokens), jnp.bfloat16),
        compiler_params=pltpu.CompilerParams(vmem_limit_bytes=32 << 20),
        cost_estimate=cost(10),
        name="attend_back",
    )(query, key, value, grad, logs, *tables)


def turn_tables(rows, cols):
    quarter = HEAD // 4
    freq = 10000.0 ** (-jnp.arange(quarter, dtype=jnp.float32) / quarter)
    row_angle = freq[:, None] * rows.astype(jnp.float32)[None, :]
    col_angle = freq[:, None] * cols.astype(jnp.float32)[None, :]
    zero = jnp.zeros_like(row_angle)
    cosine = jnp.concatenate([jnp.cos(row_angle)] * 2 + [jnp.cos(col_angle)] * 2, axis=0)
    up = jnp.concatenate([-jnp.sin(row_angle), zero, -jnp.sin(col_angle), zero], axis=0)
    down = jnp.concatenate([zero, jnp.sin(row_angle), zero, jnp.sin(col_angle)], axis=0)
    return cosine, up, down


def heads_kernel(x_ref, w_ref, *refs):
    out_ref, turned_ref = refs[-2:]
    step = min(256, x_ref.shape[0])
    for start in range(0, x_ref.shape[0], step):
        rows = slice(start, start + step)
        product = dots(x_ref[rows, :], w_ref[:, : out_ref.shape[0]], 1, 0)
        out_ref[:, rows] = product.T
        turned_ref[:, rows] = x_ref[rows, :].T


def heads_of(value, weight, columns, *others):
    shape = (columns, value.shape[0])
    return pl.pallas_call(
        heads_kernel,
        in_specs=[pl.BlockSpec(memory_space=pltpu.VMEM)] * 2
        + [pl.BlockSpec(memory_space=pl.ANY)] * len(others),
        out_shape=[
            jax.ShapeDtypeStruct(shape, jnp.float32),
            jax.ShapeDtypeStruct(value.shape[::-1], value.dtype),
        ],
        compiler_params=pltpu.CompilerParams(vmem_limit_bytes=48 << 20),
        cost_estimate=cost(5),
        name="heads_of",
    )(value, weight, *others)


def back_kernel(one_ref, two_ref, w_one_ref, w_two_ref, out_ref, one_turn, two_turn):
    @pl.when(pl.program_id(0) == 0)
    def _():
        for ref, turn_ref in ((one_ref, one_turn), (two_ref, two_turn)):
            for start in range(0, ref.shape[1], 128):
                turn_ref[start : start + 128, :] = ref[:, start : start + 128].T

    size = one_turn.shape[1]
    out_ref[...] = dots(one_turn[...], w_one_ref[:, :size], 1, 1) + dots(
        two_turn[...], w_two_ref[:, :size], 1, 1
    )


def back_through(one, two, weight_one, weight_two):
    columns, tokens = one.shape
    rows = weight_one.shape[0]
    block = 384
    fixed = pl.BlockSpec((columns, tokens), lambda i: (0, 0))
    moving = pl.BlockSpec((block, weight_one.shape[1]), lambda i: (i, 0))
    return pl.pallas_call(
        back_kernel,
        grid=(rows // block,),
        in_specs=[fixed, fixed, moving, moving],
        out_specs=pl.BlockSpec((tokens, block), lambda i: (0, i)),
        out_shape=jax.ShapeDtypeStruct((tokens, rows), jnp.float32),
        scratch_shapes=[pltpu.VMEM((tokens, columns), jnp.bfloat16)] * 2,
        compiler_params=pltpu.CompilerParams(vmem_limit_bytes=48 << 20),
        cost_estimate=cost(9),
        name="back_through",
    )(one, two, weight_one, weight_two)


def block_index(chip, bits):
    place = 0
    for bit in bits:
        place = place * 2 + ((chip >> bit) & 1)
    return place


def other_bits(bits, count):
    return [bit for bit in range(count.bit_length() - 2, -1, -1) if bit not in bits]


def grad_parts(terms, turned, columns, parts, count, *others):
    left = terms[0][0][0][0]
    rows = left.shape[1] if turned else left.shape[0]
    size = rows // count
    chunk = rows // 4
    flat = [pair for term, _ in terms for pair in term]
    lefts = []
    for pair in flat:
        if not any(pair[0] is other for other in lefts):
            lefts.append(pair[0])

    def kernel(tok_ref, *refs):
        left_refs = refs[: len(lefts)]
        right_refs = refs[len(lefts) : len(lefts) + len(flat)]
        outs = refs[len(lefts) + len(flat) + len(others) :]
        outs, scratch = outs[: len(parts)], outs[len(parts) :]
        step = pl.program_id(0)
        tok = tok_ref[0]
        if turned:

            @pl.when(step == 0)
            def _():
                for left_ref, turn_ref in zip(left_refs, scratch):
                    for start in range(0, rows, 128):
                        turn_ref[start : start + 128, :] = left_ref[:, start : start + 128].T

        place = 0
        for term, start in terms:
            total = None
            for left, right, axis in term:
                which = [left is other for other in lefts].index(True)
                if turned:
                    part = scratch[which][pl.ds(pl.multiple_of(step * chunk, chunk), chunk), :]
                else:
                    part = left_refs[which][...]
                product = dots(part, right_refs[place][...], 1, axis)
                total = product if total is None else total + product
                place += 1
            width = total.shape[1]
            for block in range(chunk // size):
                value = total[block * size : (block + 1) * size, :].astype(jnp.bfloat16)
                mine = (step * (chunk // size) + block) ^ tok
                for out, fixed_bits in zip(outs, parts):
                    index = block_index(mine, other_bits(fixed_bits, count))
                    here = jnp.bool_(True)
                    for bit, wanted in fixed_bits.items():
                        here &= ((mine >> bit) & 1) == wanted

                    @pl.when(here)
                    def _():
                        out[index, :, start : start + width] = value

    def fixed(value):
        return pl.BlockSpec(value.shape, lambda i: (0,) * value.ndim)

    if turned:
        left_specs = [fixed(value) for value in lefts]
        scratch = [pltpu.VMEM(value.shape[::-1], value.dtype) for value in lefts]
    else:
        left_specs = [pl.BlockSpec((chunk, value.shape[1]), lambda i: (i, 0)) for value in lefts]
        scratch = []
    shapes = [(count >> len(part), size, columns) for part in parts]
    return pl.pallas_call(
        kernel,
        grid=(4,),
        in_specs=[pl.BlockSpec(memory_space=pltpu.SMEM)]
        + left_specs
        + [fixed(pair[1]) for pair in flat]
        + [pl.BlockSpec(memory_space=pl.ANY)] * len(others),
        out_specs=[pl.BlockSpec(shape, lambda i: (0, 0, 0)) for shape in shapes],
        out_shape=[jax.ShapeDtypeStruct(shape, jnp.bfloat16) for shape in shapes],
        scratch_shapes=scratch,
        compiler_params=pltpu.CompilerParams(vmem_limit_bytes=56 << 20),
        cost_estimate=cost(6 * columns // 1024),
        name="grad_parts",
    )(lax.axis_index("tok").reshape(1), *lefts, *[pair[1] for pair in flat], *others)


def scatter_on(value, left_bits, order, count, last=jnp.bfloat16, hold=()):
    left_bits = list(left_bits)
    sent = []
    for bit in order:
        value = value.reshape((2,) * len(left_bits) + value.shape[-2:])
        axis = left_bits.index(bit)
        away = lax.index_in_dim(value, 1, axis, keepdims=False)
        sent.append(away)
        kept = last if bit == order[-1] else jnp.bfloat16
        stay = lax.index_in_dim(value, 0, axis, keepdims=False)
        if hold and bit == order[-1]:
            stay = after(stay, *hold)
        value = add(stay, trade(away, bit, count), kept)
        left_bits.remove(bit)
    return value, sent


def plain_products(terms, turned, columns):
    pieces = []
    for place, (term, start) in enumerate(terms):
        total = sum(dots(one, two, 0 if turned else 1, axis) for one, two, axis in term)
        end = terms[place + 1][1] if place + 1 < len(terms) else columns
        total = jnp.pad(total, ((0, 0), (0, end - start - total.shape[1])))
        pieces.append(total.astype(jnp.bfloat16))
    return pieces


def row_size(terms, turned, count):
    left = terms[0][0][0][0]
    return (left.shape[1] if turned else left.shape[0]) // count


def chain_scatter(terms, turned, columns, count, *others):
    first, order, _ = orders(count)
    bits = first[::-1] + order
    if row_size(terms, turned, count) % 8:
        half, sent = half_scatter(plain_products(terms, turned, columns), count)
        return sent[:1], [half], lambda value, _: last_scatter(value[0], count)
    away, kept = grad_parts(terms, turned, columns, [{bits[0]: 1}, {bits[0]: 0}], count, *others)
    left_bits = other_bits(bits[:1], count)
    value = add(kept, trade(away, bits[0], count))
    value, sent = scatter_on(value, left_bits, bits[1 : len(first)], count)
    left_bits = [bit for bit in left_bits if bit in order]
    return (
        sent[:1],
        [value],
        lambda value, hold: scatter_on(value[0], left_bits, order, count, jnp.float32, hold)[0],
    )


def across_scatter(terms, turned, columns, count, hold=()):
    first, order_a, order_b = orders(count)
    if row_size(terms, turned, count) % 8:
        half, sent = half_scatter(plain_products(terms, turned, columns), count)
        return [half], sent, [], [], lambda value, *_: value, lambda value, *_: last_scatter(value[0], count)
    half_bit = first[-1]
    parts = [
        {half_bit: half, order[-1]: away}
        for half, order in enumerate((order_a, order_b))
        for away in (1, 0)
    ]
    blocks = grad_parts(terms, turned, columns, parts, count)
    halves, firsts, mids = [], [], []
    for place, order in enumerate((order_a, order_b)):
        away, kept = blocks[2 * place : 2 * place + 2]
        left_bits = other_bits((order[-1], half_bit), count)
        moved = trade(away, order[-1], count)
        value = add(after(kept, *hold) if hold else kept, moved)
        firsts.append(value)
        halves.append((value, left_bits, order[-2::-1]))
        mids += scatter_on(value, left_bits, order[-2::-1], count)[1][:1]

    def begin(halves, before=()):
        return [scatter_on(*half, count, hold=before)[0] for half in halves]

    def finish(halves, between=()):
        kept, away = halves
        kept = after(kept, *between[:2]) if between else kept
        value = add(kept, trade(away, half_bit, count))
        left_bits = [bit for bit in other_bits((), count) if bit in first[:-1]]
        return scatter_on(value, left_bits, first[-2::-1], count, jnp.float32, between[2:])[0]

    return halves, [blocks[0], blocks[2]], firsts, mids, begin, finish


def row_major(value):
    return with_layout_constraint(value, Layout(tuple(range(value.ndim))))


def add(one, two, kept=jnp.bfloat16):
    return (one.astype(jnp.float32) + two.astype(jnp.float32)).astype(kept)


def after(value, *others, micros=1):
    def keep(*refs):
        pass

    anywhere = pl.BlockSpec(memory_space=pl.ANY)
    return pl.pallas_call(
        keep,
        in_specs=[anywhere] * (1 + len(others)),
        out_specs=anywhere,
        out_shape=jax.ShapeDtypeStruct(value.shape, value.dtype),
        input_output_aliases={0: 0},
        cost_estimate=cost(micros),
        name="after",
    )(value, *others)


def first_gather(shard, count):
    first, _, _ = orders(count)
    value = shard.reshape((1,) * (count.bit_length() - 1) + shard.shape)
    for bit in first:
        value = doubled(value, bit, count)
    return value


def next_gather(value, count):
    first, order_a, order_b = orders(count)
    axis = axis_of(first[-1], count)
    halves = [
        lax.slice_in_dim(value, 0, 1, axis=axis),
        lax.slice_in_dim(value, 1, 2, axis=axis),
    ]
    for one, two in zip(order_a[:-1], order_b[:-1]):
        halves = [doubled(half, bit, count) for half, bit in zip(halves, (one, two))]
    return halves


def last_gather(halves, count, *others):
    first, order_a, order_b = orders(count)
    axis = axis_of(first[-1], count)
    lasts = (order_a[-1], order_b[-1])
    moved = [trade(half, bit, count) for half, bit in zip(halves, lasts)]
    out = jnp.concatenate(
        [
            jnp.concatenate([half, half], axis=axis_of(bit, count))
            for half, bit in zip(halves, lasts)
        ],
        axis=axis,
    )
    out = after(out, *others) if others else out
    for place, (bit, value) in enumerate(zip(lasts, moved)):
        out = put(out, value, {axis: place, axis_of(bit, count): 1 - bit_of(bit)}, count)
    return out.reshape(-1, out.shape[-1])


def halved(pieces, bit, count, kept):
    axis = axis_of(bit, count)
    digit = bit_of(bit)

    def part(place):
        parts = [lax.dynamic_slice_in_dim(piece, place, 1, axis) for piece in pieces]
        return parts[0] if len(parts) == 1 else jnp.concatenate(parts, axis=-1)

    sent = part(1 - digit).astype(jnp.bfloat16)
    total = part(digit).astype(jnp.float32) + trade(sent, bit, count).astype(jnp.float32)
    return total.astype(kept), sent


def half_scatter(values, count):
    first, order_a, order_b = orders(count)
    values = [split_rows(value, count) for value in values]
    axis = axis_of(first[-1], count)
    first_sent, out = [], []
    for place, order in enumerate((order_a[::-1], order_b[::-1])):
        pieces = [lax.slice_in_dim(value, place, place + 1, axis=axis) for value in values]
        for step, bit in enumerate(order):
            total, sent = halved(pieces, bit, count, jnp.bfloat16)
            if step == 0:
                first_sent.append(sent)
            pieces = [total]
        out.append(pieces[0])
    return jnp.concatenate(out, axis=axis), first_sent


def last_scatter(value, count):
    first, _, _ = orders(count)
    for bit in first[::-1]:
        value, _ = halved([value], bit, count, jnp.bfloat16 if bit != first[0] else jnp.float32)
    return value.reshape(value.shape[-2:])


def gather_small(value, count, bits):
    for bit in bits:
        value = jnp.concatenate([value, trade(value, bit, count)], axis=axis_of(bit, count))
    return value


def spread(value, count):
    return value.reshape((1,) * (count.bit_length() - 1) + value.shape)


def stacked(value, count):
    return value.reshape((-1,) + value.shape[count.bit_length() :])


def scatter_small(value, count, bits):
    for bit in bits:
        axis = axis_of(bit, count)
        sent = lax.slice_in_dim(value, 1, 2, axis=axis).astype(jnp.bfloat16)
        moved = trade(sent, bit, count).astype(jnp.float32)
        value = lax.slice_in_dim(value, 0, 1, axis=axis) + moved
    return value


def sum_all(value, count):
    value = value + swap(value)
    for bit in range(count.bit_length() - 1):
        value = value + trade(value, bit, count)
    return value


def pick(segment, table):
    out = jnp.zeros((segment.shape[0], table.shape[1]), jnp.float32)
    for slot in range(SLOTS):
        out = jnp.where(segment[:, None] == slot, table[slot][None, :], out)
    return out


def body(
    block_input,
    out_grad,
    class_table,
    time_table,
    class_label,
    time_index,
    grid_height,
    grid_width,
    mix_weight,
    proj_weight,
    cond_weight,
    cond_bias,
    feed_weight,
    down_weight,
    mix_mean,
    proj_mean,
    cond_mean,
    bias_mean,
    feed_mean,
    down_mean,
    mix_square,
    proj_square,
    cond_square,
    bias_square,
    feed_square,
    down_square,
):
    half = jnp.bfloat16
    count = block_input.shape[0]
    width = block_input.shape[1]
    chips = lax.axis_size("tok")
    tok = lax.axis_index("tok")
    side = lax.axis_index("mlp")
    first_side = side == 0
    rows_own = mix_weight.shape[0]
    mix_cols = mix_weight.shape[1]
    proj_cols = proj_weight.shape[1]
    hidden_cols = feed_weight.shape[2]
    cond_cols = cond_weight.shape[1]
    group = mix_cols // 3
    heads = HEADS // 2

    def joined(own, other, axis=1):
        low = jnp.where(first_side, own, other)
        high = jnp.where(first_side, other, own)
        return jnp.concatenate([low, high], axis=axis)

    def parted(value):
        size = value.shape[1] // 2
        low, high = value[:, :size], value[:, size:]
        return jnp.where(first_side, low, high), jnp.where(first_side, high, low)

    codes = jnp.stack([class_label, time_index], axis=1)
    first, order, _ = orders(chips)
    codes = spread(jnp.concatenate([codes, swap(codes)], axis=0), chips)
    codes = gather_small(codes, chips, order)

    mix_low = mix_weight.astype(half)
    mix_parts = [mix_low[:, :group], mix_low[:, group : 2 * group], mix_low[:, 2 * group :]]
    mix_moved = swap(mix_parts[1])
    mix_shard = jnp.where(
        first_side,
        jnp.concatenate([mix_parts[0], mix_parts[2], mix_moved], axis=1),
        jnp.concatenate([mix_moved, mix_parts[0], mix_parts[2]], axis=1),
    )
    mix_shard = jnp.concatenate([mix_shard, proj_weight.astype(half)], axis=1)
    codes = gather_small(codes, chips, first)
    mix_first = after(spread(mix_shard, chips), codes)
    mix_first = doubled(mix_first, first[0], chips)
    nothing = jnp.minimum(jnp.abs(mix_first.reshape(-1)[0].astype(jnp.float32)), 0.0)
    codes = stacked(codes, chips)
    labels, times = codes[:, 0], codes[:, 1]
    for bit in first[1:]:
        mix_first = doubled(mix_first, bit, chips)

    start = tok * rows_own
    class_part = lax.dynamic_slice_in_dim(class_table, start, rows_own, 1)
    time_part = lax.dynamic_slice_in_dim(time_table, start, rows_own, 1)
    class_hot = (labels[:, None] == jnp.arange(class_table.shape[0])[None, :]).astype(half)
    time_hot = (times[:, None] == jnp.arange(time_table.shape[0])[None, :]).astype(half)
    embed = jnp.dot(class_hot, class_part, preferred_element_type=jnp.float32) + jnp.dot(
        time_hot, time_part, preferred_element_type=jnp.float32
    )
    cond_low = jax.nn.silu(embed).astype(half)
    partial_mod = jnp.dot(cond_low, cond_weight.astype(half), preferred_element_type=jnp.float32)
    bias_low = cond_bias.astype(half).astype(jnp.float32)
    bias_pair = joined(bias_low[None, :], swap(bias_low)[None, :])[0]
    bias_start = tok * bias_pair.shape[0]
    bias_side = bias_start // cond_cols
    bias_pair = jnp.where(bias_side == side, bias_pair, 0.0)
    bias_row = lax.dynamic_update_slice(
        jnp.zeros((cond_cols,), jnp.float32), bias_pair, (bias_start - bias_side * cond_cols,)
    )
    mod_half = split_rows(partial_mod + bias_row[None, :], chips)
    mod_half = scatter_small(mod_half, chips, order[:1])
    mod_half = scatter_small(mod_half, chips, order[1:])
    mix_halves = next_gather(mix_first, chips)
    mod_half = scatter_small(after(mod_half, mix_first), chips, first[::-1])
    mod_half = mod_half.reshape(-1, cond_cols)
    slots = class_label.shape[0]
    modulation = joined(mod_half[:slots], swap(mod_half[slots:]))

    later = nothing.astype(jnp.int32)
    segment, member, rows, cols = geometry(grid_height + later, grid_width + later, count)
    tables = turn_tables(rows, cols) + (segment[None, :], segment[:, None])
    valid = (segment < SLOTS).astype(jnp.float32)[:, None]
    shift_a, scale_a, gate_a, shift_b, scale_b, gate_b = (
        pick(segment, table) for table in jnp.split(modulation, 6, axis=1)
    )
    inputs = block_input.astype(jnp.float32) + nothing
    first_in = modulate(inputs, shift_a, scale_a).astype(half)

    mix_own = last_gather(mix_halves, chips, first_in)
    far = jnp.concatenate(
        [(value + nothing).astype(half) for value in (feed_weight[0], feed_weight[1], down_weight.T)],
        axis=1,
    )
    far = first_gather(after(far, mix_first, mod_half), chips)
    far = last_gather(next_gather(after(far, first_in), chips), chips)
    far_gate, far_up, far_down = (
        far[:, place * hidden_cols : (place + 1) * hidden_cols] for place in range(3)
    )
    mix_other = swap_rows(mix_own, chips)
    proj_full = joined(mix_own[:, mix_cols:], mix_other[:, mix_cols:])

    shape = (3, heads, HEAD, count)
    raw_own, first_turned = heads_of(first_in, mix_own, mix_cols)
    first_moved = swap(first_turned)
    att_own, log_own, *qkv_own = attend(raw_own.reshape(shape), tables)
    att_other, log_other, *qkv_other = attend(
        heads_of(first_in, mix_other, mix_cols, first_moved)[0].reshape(shape), tables
    )
    attended = joined(att_own, att_other, 0).reshape(width, count)
    attended_moved = swap(attended)
    branch = dots(attended, proj_full, 0, 0)
    middle = inputs + gate_a * branch
    second_in = modulate(middle, shift_b, scale_b).astype(half)
    second_pair = jnp.concatenate([second_in, swap(second_in)], axis=0)
    gate_pre = jnp.dot(second_pair, far_gate, preferred_element_type=jnp.float32)
    up_pre = jnp.dot(second_pair, far_up, preferred_element_type=jnp.float32)
    hidden = (jax.nn.silu(gate_pre) * up_pre).astype(half)
    grad_out = valid * out_grad.astype(jnp.float32)
    result_grad = (gate_b * grad_out).astype(half)
    result_pair = jnp.concatenate([result_grad, swap(result_grad)], axis=0)
    down_sent, down_half, down_finish = chain_scatter(
        [([(result_pair, hidden, 0)], 0)], True, hidden_cols, chips, attended_moved
    )
    d_hidden = jnp.dot(result_pair, far_down, preferred_element_type=jnp.float32)
    sig = jax.nn.sigmoid(gate_pre)
    gate_grad = (d_hidden * up_pre * sig * (1.0 + gate_pre * (1.0 - sig))).astype(half)
    up_grad = (d_hidden * gate_pre * sig).astype(half)
    second_part = against(gate_grad, far_gate) + against(up_grad, far_up)
    second_grad = second_part[:count] + swap(second_part[count:].astype(half)).astype(jnp.float32)
    pull_second = jax.vjp(modulate, middle, shift_b, scale_b)[1]
    d_middle, d_shift_b, d_scale_b = pull_second(second_grad)
    d_middle = d_middle + grad_out
    d_gate_a = d_middle * branch
    branch_grad = (gate_a * d_middle).astype(half)
    attended_grad = dots(proj_full, branch_grad, 1, 1).astype(half).reshape(HEADS, HEAD, count)
    grad_own = lax.dynamic_slice_in_dim(attended_grad, side * heads, heads, 0)
    grad_other = lax.dynamic_slice_in_dim(attended_grad, (1 - side) * heads, heads, 0)
    grad_other = after(grad_other, *down_sent)
    mg_other = attend_back(*qkv_other, grad_other, log_other, tables).reshape(mix_cols, count)
    mg_moved = swap(mg_other)
    feed_half, _, _, feed_mids, feed_begin, feed_finish = across_scatter(
        [([(second_pair, gate_grad, 0)], 0), ([(second_pair, up_grad, 0)], hidden_cols)],
        True,
        2 * hidden_cols,
        chips,
        (mg_other,),
    )
    grad_own = after(grad_own, *feed_mids) if feed_mids else grad_own
    mg_own = attend_back(*qkv_own, grad_own, log_own, tables).reshape(mix_cols, count)
    branch_grad_own, branch_grad_other = parted(branch_grad)
    proj_start = -(-mix_cols // 128) * 128
    near_half, near_sent, _, near_mids, near_begin, near_finish = across_scatter(
        [
            ([(first_turned, mg_own, 1), (first_moved, mg_moved, 1)], 0),
            ([(attended, branch_grad_own, 0), (attended_moved, swap_rows(branch_grad_other, chips), 0)], proj_start),
        ],
        False,
        proj_start + proj_cols,
        chips,
    )
    down_grad = down_finish([after(value, *near_sent) for value in down_half], near_mids).T
    feed_half = feed_begin(feed_half, near_sent)
    near_half = near_begin(near_half)
    feed_grad = feed_finish(feed_half, [*near_mids, near_half[-1]])
    feed_grad = jnp.stack([feed_grad[:, :hidden_cols], feed_grad[:, hidden_cols:]])
    near_grad = near_finish(near_half)
    proj_grad = near_grad[:, proj_start:]
    mix_parts = [near_grad[:, place * group : (place + 1) * group] for place in range(3)]
    mix_moved = swap(jnp.where(first_side, mix_parts[2], mix_parts[0]))
    mix_grad = jnp.where(
        first_side,
        jnp.concatenate([mix_parts[0], mix_moved, mix_parts[1]], axis=1),
        jnp.concatenate([mix_parts[1], mix_moved, mix_parts[2]], axis=1),
    )

    partial_value = against(after(hidden, *near_sent), far_down)
    result = partial_value[:count] + swap(partial_value[count:].astype(half)).astype(jnp.float32)
    block_output = (valid * (middle + gate_b * result)).astype(half)
    d_gate_b = grad_out * result
    held = [*near_sent, feed_half[-1]]
    mg_own, mg_other = after(mg_own, *held), after(mg_other, *held)
    first_grad = back_through(mg_own, mg_other, mix_own, mix_other)
    pull_first = jax.vjp(modulate, inputs, shift_a, scale_a)[1]
    d_inputs, d_shift_a, d_scale_a = pull_first(first_grad)
    input_grad = d_inputs + d_middle
    member_low = after(member.astype(half), *near_sent)
    d_modulation = jnp.concatenate(
        [
            across(member_low, piece.astype(half))
            for piece in (d_shift_a, d_scale_a, d_gate_a, d_shift_b, d_scale_b, d_gate_b)
        ],
        axis=1,
    ).astype(half)
    mod_own, mod_other = parted(d_modulation)
    mod_all = spread(jnp.concatenate([mod_own, swap(mod_other)], axis=0), chips)
    mod_all = gather_small(after(mod_all, *near_mids), chips, first + order)
    mod_all = stacked(mod_all, chips)
    cond_grad = across(cond_low, mod_all)
    bias_half = jnp.sum(mod_all.astype(jnp.float32), axis=0)[None, :]
    bias_full = joined(bias_half, swap(bias_half))[0]
    bias_size = cond_bias.shape[0]
    bias_grad = lax.dynamic_slice_in_dim(bias_full, (2 * tok + side) * bias_size, bias_size, 0)

    grads = (mix_grad, proj_grad, cond_grad, bias_grad, feed_grad, down_grad)
    local_squares = jnp.float32(0.0)
    for grad in (near_grad[:, :mix_cols], *grads[1:]):
        local_squares = local_squares + jnp.sum(grad * grad)
    grad_norm = jnp.sqrt(sum_all(local_squares, chips))
    factor = CLIP_NORM / jnp.maximum(grad_norm, CLIP_NORM)
    params = (mix_weight, proj_weight, cond_weight, cond_bias, feed_weight, down_weight)
    means = (mix_mean, proj_mean, cond_mean, bias_mean, feed_mean, down_mean)
    squares_old = (mix_square, proj_square, cond_square, bias_square, feed_square, down_square)
    updates = [adam(w, m, v, g * factor) for w, m, v, g in zip(params, means, squares_old, grads)]
    return (
        block_output,
        input_grad,
        grad_norm,
        updates[0][0],
        updates[1][0],
        updates[2][0],
        updates[3][0],
        updates[4][0],
        updates[5][0],
        updates[0][1],
        updates[1][1],
        updates[2][1],
        updates[3][1],
        updates[4][1],
        updates[5][1],
        updates[0][2],
        updates[1][2],
        updates[2][2],
        updates[3][2],
        updates[4][2],
        updates[5][2],
    )


def solution(mesh):
    placed = (
        P(("tok", "mlp"), None),
        P(("tok", "mlp"), None),
        P(),
        P(),
        P(("tok", "mlp")),
        P(("tok", "mlp")),
        P(("tok", "mlp")),
        P(("tok", "mlp")),
        P("tok", "mlp"),
        P("tok", "mlp"),
        P("tok", "mlp"),
        P(("tok", "mlp")),
        P(None, "tok", "mlp"),
        P("mlp", "tok"),
        P("tok", "mlp"),
        P("tok", "mlp"),
        P("tok", "mlp"),
        P(("tok", "mlp")),
        P(None, "tok", "mlp"),
        P("mlp", "tok"),
        P("tok", "mlp"),
        P("tok", "mlp"),
        P("tok", "mlp"),
        P(("tok", "mlp")),
        P(None, "tok", "mlp"),
        P("mlp", "tok"),
    )
    return jax.shard_map(
        body,
        mesh=mesh,
        in_specs=placed,
        out_specs=(
            P(("tok", "mlp"), None),
            P(("tok", "mlp"), None),
            P(),
            P("tok", "mlp"),
            P("tok", "mlp"),
            P("tok", "mlp"),
            P(("tok", "mlp")),
            P(None, "tok", "mlp"),
            P("mlp", "tok"),
            P("tok", "mlp"),
            P("tok", "mlp"),
            P("tok", "mlp"),
            P(("tok", "mlp")),
            P(None, "tok", "mlp"),
            P("mlp", "tok"),
            P("tok", "mlp"),
            P("tok", "mlp"),
            P("tok", "mlp"),
            P(("tok", "mlp")),
            P(None, "tok", "mlp"),
            P("mlp", "tok"),
        ),
        check_vma=False,
    )
```

```python
import jax
import jax.numpy as jnp
from jax import lax
from jax.experimental import pallas as pl
from jax.experimental.pallas import tpu as pltpu
from jax.experimental.layout import Layout, with_layout_constraint
from jax.sharding import PartitionSpec as P

HEADS = 16
HEAD = 72
SLOTS = 4
STEP = 10


BETA_ONE = 0.9
BETA_TWO = 0.95
ADAM_EPS = 1e-08
RATE = 0.08
DECAY = 0.01
CLIP_NORM = 1.0
NORM_EPS = 1e-06
MASKED = -1e30
HIGH = lax.Precision.HIGHEST


def layer_norm(value):
    centered = value - jnp.mean(value, axis=-1, keepdims=True)
    spread = jnp.mean(centered * centered, axis=-1, keepdims=True)
    return centered * lax.rsqrt(spread + NORM_EPS)


def modulate(value, shift, scale):
    return layer_norm(value) * (1.0 + scale) + shift


def geometry(height, width, count):
    lengths = height * width
    ends = jnp.cumsum(lengths)
    starts = ends - lengths
    places = jnp.arange(count, dtype=jnp.int32)
    segment = jnp.sum((places[:, None] >= ends[None, :]).astype(jnp.int32), axis=1)
    member = segment[:, None] == jnp.arange(height.shape[0], dtype=jnp.int32)[None, :]
    start_tok = jnp.sum(jnp.where(member, starts[None, :], 0), axis=1)
    width_tok = jnp.maximum(jnp.sum(jnp.where(member, width[None, :], 0), axis=1), 1)
    offset = places - start_tok
    return (segment, member.astype(jnp.float32), offset // width_tok, offset % width_tok)


def across(left, right, precision=None):
    return lax.dot_general(
        left,
        right,
        (((0,), (0,)), ((), ())),
        preferred_element_type=jnp.float32,
        precision=precision,
    )


def against(left, right):
    return lax.dot_general(
        left, right, (((1,), (1,)), ((), ())), preferred_element_type=jnp.float32
    )


def adam(weight, mean, square, grad):
    mean_new = BETA_ONE * mean + (1.0 - BETA_ONE) * grad
    square_new = BETA_TWO * square + (1.0 - BETA_TWO) * grad * grad
    fixed_mean = mean_new / (1.0 - BETA_ONE**STEP)
    fixed_square = square_new / (1.0 - BETA_TWO**STEP)
    weight_new = weight - RATE * (fixed_mean / (jnp.sqrt(fixed_square) + ADAM_EPS) + DECAY * weight)
    return (mean_new, square_new, weight_new)


BITS = {16: ((3, 2), ((0,), (1,))), 128: ((2, 1, 0), ((3, 4), (5, 6)))}


def orders(count):
    first, (one, two) = BITS[count]
    return first, one + two, two + one


def bit_of(bit):
    return (lax.axis_index("tok") >> bit) & 1


def trade(value, bit, count):
    return lax.ppermute(value, "tok", [(place, place ^ (1 << bit)) for place in range(count)])


def axis_of(bit, count):
    return count.bit_length() - 2 - bit


def swap(value):
    return lax.ppermute(value, "mlp", [(0, 1), (1, 0)])


def swap_rows(value, count):
    blocks = value.reshape((2,) * (count.bit_length() - 1) + (-1, value.shape[-1]))
    return swap(blocks).reshape(value.shape)


def split_rows(value, count):
    axes = (2,) * (count.bit_length() - 1)
    return value.reshape(*axes, value.shape[0] // count, value.shape[1])


def put(out, value, places, count):
    start = [0] * out.ndim
    for axis, place in places.items():
        start[axis] = place
    return lax.dynamic_update_slice(out, value, tuple(start))


def doubled(value, bit, count):
    axis = axis_of(bit, count)
    out = jnp.concatenate([value, value], axis=axis)
    return put(out, trade(value, bit, count), {axis: 1 - bit_of(bit)}, count)


SCORE_SCALE = HEAD ** (-0.5)
FEED_BLOCK = 512
FEED_ROWS = 512
TURN_BLOCK = 768
TURN_CHUNKS = 1
NEAR_CHUNKS = 2


def cost(micros):
    return pl.CostEstimate(flops=int(micros * 0.460e9), bytes_accessed=1000, transcendentals=0)


def turn(value, cosine, up, down):
    quarter = HEAD // 4
    above = pltpu.roll(value, HEAD - quarter, 0)
    below = pltpu.roll(value, quarter, 0)
    return value * cosine + above * up + below * down


def dots(left, right, left_axis, right_axis):
    return lax.dot_general(
        left,
        right,
        (((left_axis,), (right_axis,)), ((), ())),
        preferred_element_type=jnp.float32,
    )


def attend_kernel(
    q_ref, k_ref, v_ref, cos_ref, up_ref, down_ref, row_ref, col_ref,
    out_ref, log_ref, q_out, k_out, v_out,
):
    cosine, up, down = cos_ref[...], up_ref[...], down_ref[...]
    query = turn(q_ref[0, 0], cosine, up, down).astype(jnp.bfloat16)
    key = turn(k_ref[0, 0], cosine, up, down).astype(jnp.bfloat16)
    value = v_ref[0, 0].astype(jnp.bfloat16)
    q_out[0], k_out[0], v_out[0] = query, key, value
    scores = dots(key, query, 0, 0) * SCORE_SCALE
    scores = jnp.where(col_ref[...] == row_ref[...], scores, MASKED)
    top = jnp.max(scores, axis=0, keepdims=True)
    weights = jnp.exp(scores - top)
    total = jnp.sum(weights, axis=0, keepdims=True)
    mixed = dots(value, weights.astype(jnp.bfloat16), 1, 0)
    out_ref[0] = (mixed * (1.0 / total)).astype(jnp.bfloat16)
    log_ref[0] = top + jnp.log(total)


def whole(value):
    return pl.BlockSpec(value.shape, lambda i: (0,) * value.ndim)


def attend(mixed, tables):
    _, heads, _, tokens = mixed.shape

    def part(place):
        return pl.BlockSpec((1, 1, HEAD, tokens), lambda i: (place, i, 0, 0))

    block = pl.BlockSpec((1, HEAD, tokens), lambda i: (i, 0, 0))
    line = pl.BlockSpec((1, 1, tokens), lambda i: (i, 0, 0))
    shape = jax.ShapeDtypeStruct((heads, HEAD, tokens), jnp.bfloat16)
    return pl.pallas_call(
        attend_kernel,
        grid=(heads,),
        in_specs=[part(0), part(1), part(2)] + [whole(value) for value in tables],
        out_specs=[block, line, block, block, block],
        out_shape=[
            shape,
            jax.ShapeDtypeStruct((heads, 1, tokens), jnp.float32),
            shape,
            shape,
            shape,
        ],
        compiler_params=pltpu.CompilerParams(vmem_limit_bytes=32 << 20),
        cost_estimate=cost(6),
        name="attend",
    )(mixed, mixed, mixed, *tables)


def attend_back_kernel(
    q_ref, k_ref, v_ref, g_ref, log_ref, cos_ref, up_ref, down_ref, row_ref, col_ref, out_ref
):
    query, key, value, grad = q_ref[0], k_ref[0], v_ref[0], g_ref[0]
    scores = dots(key, query, 0, 0) * SCORE_SCALE
    scores = jnp.where(col_ref[...] == row_ref[...], scores, MASKED)
    probs = jnp.exp(scores - log_ref[0])
    d_probs = dots(value, grad, 0, 0)
    inner = jnp.sum(probs * d_probs, axis=0, keepdims=True)
    d_scores = (probs * (d_probs - inner) * SCORE_SCALE).astype(jnp.bfloat16)
    d_value = dots(grad, probs.astype(jnp.bfloat16), 1, 1)
    d_key = dots(query, d_scores, 1, 1)
    d_query = dots(key, d_scores, 1, 0)
    cosine, up, down = cos_ref[...], -up_ref[...], -down_ref[...]
    out_ref[0, 0] = turn(d_query, cosine, up, down).astype(jnp.bfloat16)
    out_ref[1, 0] = turn(d_key, cosine, up, down).astype(jnp.bfloat16)
    out_ref[2, 0] = d_value.astype(jnp.bfloat16)


def attend_back(query, key, value, grad, logs, tables):
    heads, _, tokens = query.shape
    block = pl.BlockSpec((1, HEAD, tokens), lambda i: (i, 0, 0))
    line = pl.BlockSpec((1, 1, tokens), lambda i: (i, 0, 0))
    return pl.pallas_call(
        attend_back_kernel,
        grid=(heads,),
        in_specs=[block] * 4 + [line] + [whole(item) for item in tables],
        out_specs=pl.BlockSpec((3, 1, HEAD, tokens), lambda i: (0, i, 0, 0)),
        out_shape=jax.ShapeDtypeStruct((3, heads, HEAD, tokens), jnp.bfloat16),
        compiler_params=pltpu.CompilerParams(vmem_limit_bytes=32 << 20),
        cost_estimate=cost(10),
        name="attend_back",
    )(query, key, value, grad, logs, *tables)


def turn_tables(rows, cols):
    quarter = HEAD // 4
    freq = 10000.0 ** (-jnp.arange(quarter, dtype=jnp.float32) / quarter)
    row_angle = freq[:, None] * rows.astype(jnp.float32)[None, :]
    col_angle = freq[:, None] * cols.astype(jnp.float32)[None, :]
    zero = jnp.zeros_like(row_angle)
    cosine = jnp.concatenate([jnp.cos(row_angle)] * 2 + [jnp.cos(col_angle)] * 2, axis=0)
    up = jnp.concatenate([-jnp.sin(row_angle), zero, -jnp.sin(col_angle), zero], axis=0)
    down = jnp.concatenate([zero, jnp.sin(row_angle), zero, jnp.sin(col_angle)], axis=0)
    return cosine, up, down


def heads_kernel(x_ref, w_ref, *refs):
    out_ref, turned_ref = refs[-2:]
    step = min(256, x_ref.shape[0])
    for start in range(0, x_ref.shape[0], step):
        rows = slice(start, start + step)
        product = dots(x_ref[rows, :], w_ref[:, : out_ref.shape[0]], 1, 0)
        out_ref[:, rows] = product.T
        turned_ref[:, rows] = x_ref[rows, :].T


def heads_of(value, weight, columns, *others):
    shape = (columns, value.shape[0])
    return pl.pallas_call(
        heads_kernel,
        in_specs=[pl.BlockSpec(memory_space=pltpu.VMEM)] * 2
        + [pl.BlockSpec(memory_space=pl.ANY)] * len(others),
        out_shape=[
            jax.ShapeDtypeStruct(shape, jnp.float32),
            jax.ShapeDtypeStruct(value.shape[::-1], value.dtype),
        ],
        compiler_params=pltpu.CompilerParams(vmem_limit_bytes=48 << 20),
        cost_estimate=cost(5),
        name="heads_of",
    )(value, weight, *others)


def back_kernel(one_ref, two_ref, w_one_ref, w_two_ref, out_ref, one_turn, two_turn):
    @pl.when(pl.program_id(0) == 0)
    def _():
        for ref, turn_ref in ((one_ref, one_turn), (two_ref, two_turn)):
            for start in range(0, ref.shape[1], 128):
                turn_ref[start : start + 128, :] = ref[:, start : start + 128].T

    size = one_turn.shape[1]
    out_ref[...] = dots(one_turn[...], w_one_ref[:, :size], 1, 1) + dots(
        two_turn[...], w_two_ref[:, :size], 1, 1
    )


def back_through(one, two, weight_one, weight_two):
    columns, tokens = one.shape
    rows = weight_one.shape[0]
    block = 384
    fixed = pl.BlockSpec((columns, tokens), lambda i: (0, 0))
    moving = pl.BlockSpec((block, weight_one.shape[1]), lambda i: (i, 0))
    return pl.pallas_call(
        back_kernel,
        grid=(rows // block,),
        in_specs=[fixed, fixed, moving, moving],
        out_specs=pl.BlockSpec((tokens, block), lambda i: (0, i)),
        out_shape=jax.ShapeDtypeStruct((tokens, rows), jnp.float32),
        scratch_shapes=[pltpu.VMEM((tokens, columns), jnp.bfloat16)] * 2,
        compiler_params=pltpu.CompilerParams(vmem_limit_bytes=48 << 20),
        cost_estimate=cost(9),
        name="back_through",
    )(one, two, weight_one, weight_two)


def feed_kernel(
    x_one, x_two, r_one, r_two, gate_ref, up_ref, down_ref,
    hidden_ref, gate_out, up_out, own_ref, sent_ref, total_ref,
):
    step = pl.program_id(0)
    count = x_one.shape[0]
    rows = min(FEED_ROWS, count)
    low = jnp.bfloat16

    @pl.when(step == 0)
    def _():
        total_ref[...] = jnp.zeros_like(total_ref)

    for half, (x_ref, r_ref) in enumerate(((x_one, r_one), (x_two, r_two))):
        for start in range(0, count, rows):
            here = slice(start, start + rows)
            place = slice(half * count + start, half * count + start + rows)
            gate = dots(x_ref[here, :], gate_ref[...], 1, 0)
            up = dots(x_ref[here, :], up_ref[...], 1, 0)
            d_hidden = dots(r_ref[here, :], down_ref[...], 1, 0)
            sig = 1.0 / (1.0 + jnp.exp(-gate))
            active = gate * sig
            hidden_ref[place, :] = (active * up).astype(low)
            d_gate = (d_hidden * up * sig * (1.0 + gate * (1.0 - sig))).astype(low)
            d_up = (d_hidden * active).astype(low)
            gate_out[place, :] = d_gate
            up_out[place, :] = d_up
            total_ref[place, :] += dots(d_gate, gate_ref[...], 1, 1) + dots(
                d_up, up_ref[...], 1, 1
            )

    @pl.when(step == pl.num_programs(0) - 1)
    def _():
        own_ref[...] = total_ref[:count, :]
        sent_ref[...] = total_ref[count:, :].astype(low)


def feed_both_ways(x_one, x_two, r_one, r_two, far):
    count, width = x_one.shape
    size = far.shape[1] // 3
    block = FEED_BLOCK
    steps = size // block
    fixed = pl.BlockSpec((count, width), lambda i: (0, 0))

    def weight(place):
        return pl.BlockSpec((width, block), lambda i: (0, place * steps + i))

    moving = pl.BlockSpec((2 * count, block), lambda i: (0, i))
    wide = jax.ShapeDtypeStruct((2 * count, size), jnp.bfloat16)
    return pl.pallas_call(
        feed_kernel,
        grid=(steps,),
        in_specs=[fixed] * 4 + [weight(place) for place in range(3)],
        out_specs=[moving] * 3 + [fixed] * 2,
        out_shape=[wide] * 3
        + [
            jax.ShapeDtypeStruct((count, width), jnp.float32),
            jax.ShapeDtypeStruct((count, width), jnp.bfloat16),
        ],
        scratch_shapes=[pltpu.VMEM((2 * count, width), jnp.float32)],
        compiler_params=pltpu.CompilerParams(vmem_limit_bytes=56 << 20),
        cost_estimate=cost(22),
        name="feed_both_ways",
    )(x_one, x_two, r_one, r_two, far, far, far)


def hand_out(block_ref, outs, parts, count):
    for out, fixed_bits in zip(outs, parts):
        rest = other_bits(fixed_bits, count)
        for chip in range(count):
            if all((chip >> bit) & 1 == wanted for bit, wanted in fixed_bits.items()):
                out[block_index(chip, rest)] = block_ref[chip]


def turned_parts(lefts, rights, parts, count, *others):
    tokens, rows = lefts[0].shape
    columns = rights[0].shape[1]
    size = rows // count
    chunk = rows // TURN_CHUNKS
    block = TURN_BLOCK
    steps = columns // block

    def kernel(tok_ref, one_ref, two_ref, *refs):
        right_refs = refs[: len(rights)]
        outs = refs[len(rights) + len(others) :]
        outs, (turn_ref, block_ref) = outs[: len(parts)], outs[len(parts) :]
        step = pl.program_id(0)
        tok = tok_ref[0]

        @pl.when(step == 0)
        def _():
            for half, ref in enumerate((one_ref, two_ref)):
                for start in range(0, rows, 128):
                    turn_ref[start : start + 128, half * tokens : (half + 1) * tokens] = ref[
                        :, start : start + 128
                    ].T

        for place, right_ref in enumerate(right_refs):

            @pl.when(step // steps == place)
            def _():
                for piece in range(rows // chunk):
                    total = dots(turn_ref[piece * chunk : (piece + 1) * chunk, :], right_ref[...], 1, 0)
                    for inner in range(chunk // size):
                        value = total[inner * size : (inner + 1) * size, :].astype(jnp.bfloat16)
                        block_ref[(piece * (chunk // size) + inner) ^ tok] = value
                hand_out(block_ref, outs, parts, count)

    fixed = pl.BlockSpec((tokens, rows), lambda i: (0, 0))

    def moving(place):
        return pl.BlockSpec(
            (2 * tokens, block), lambda i: (0, jnp.clip(i - place * steps, 0, steps - 1))
        )

    shapes = [(count >> len(part), size) for part in parts]
    return pl.pallas_call(
        kernel,
        grid=(steps * len(rights),),
        in_specs=[pl.BlockSpec(memory_space=pltpu.SMEM), fixed, fixed]
        + [moving(place) for place in range(len(rights))]
        + [pl.BlockSpec(memory_space=pl.ANY)] * len(others),
        out_specs=[pl.BlockSpec(shape + (block,), lambda i: (0, 0, i)) for shape in shapes],
        out_shape=[
            jax.ShapeDtypeStruct(shape + (columns * len(rights),), jnp.bfloat16) for shape in shapes
        ],
        scratch_shapes=[
            pltpu.VMEM((rows, 2 * tokens), jnp.bfloat16),
            pltpu.VMEM((count, size, block), jnp.bfloat16),
        ],
        compiler_params=pltpu.CompilerParams(vmem_limit_bytes=48 << 20),
        cost_estimate=cost(6 * len(rights)),
        name="turned_parts",
    )(lax.axis_index("tok").reshape(1), *lefts, *rights, *others)


def block_index(chip, bits):
    place = 0
    for bit in bits:
        place = place * 2 + ((chip >> bit) & 1)
    return place


def other_bits(bits, count):
    return [bit for bit in range(count.bit_length() - 2, -1, -1) if bit not in bits]


def grad_parts(terms, columns, parts, count):
    left = terms[0][0][0][0]
    rows = left.shape[0]
    size = rows // count
    chunk = rows // NEAR_CHUNKS
    flat = [pair for term, _ in terms for pair in term]
    lefts = []
    for pair in flat:
        if not any(pair[0] is other for other in lefts):
            lefts.append(pair[0])

    def kernel(tok_ref, *refs):
        left_refs = refs[: len(lefts)]
        right_refs = refs[len(lefts) : len(lefts) + len(flat)]
        outs = refs[len(lefts) + len(flat) :]
        step = pl.program_id(0)
        tok = tok_ref[0]
        place = 0
        for term, start in terms:
            total = None
            for left, right, axis in term:
                which = [left is other for other in lefts].index(True)
                product = dots(left_refs[which][...], right_refs[place][...], 1, axis)
                total = product if total is None else total + product
                place += 1
            width = total.shape[1]
            for block in range(chunk // size):
                value = total[block * size : (block + 1) * size, :].astype(jnp.bfloat16)
                mine = (step * (chunk // size) + block) ^ tok
                for out, fixed_bits in zip(outs, parts):
                    index = block_index(mine, other_bits(fixed_bits, count))
                    here = jnp.bool_(True)
                    for bit, wanted in fixed_bits.items():
                        here &= ((mine >> bit) & 1) == wanted

                    @pl.when(here)
                    def _():
                        out[index, :, start : start + width] = value

    def fixed(value):
        return pl.BlockSpec(value.shape, lambda i: (0,) * value.ndim)

    left_specs = [pl.BlockSpec((chunk, value.shape[1]), lambda i: (i, 0)) for value in lefts]
    shapes = [(count >> len(part), size, columns) for part in parts]
    return pl.pallas_call(
        kernel,
        grid=(rows // chunk,),
        in_specs=[pl.BlockSpec(memory_space=pltpu.SMEM)]
        + left_specs
        + [fixed(pair[1]) for pair in flat],
        out_specs=[pl.BlockSpec(shape, lambda i: (0, 0, 0)) for shape in shapes],
        out_shape=[jax.ShapeDtypeStruct(shape, jnp.bfloat16) for shape in shapes],
        compiler_params=pltpu.CompilerParams(vmem_limit_bytes=56 << 20),
        cost_estimate=cost(6 * columns // 1024),
        name="grad_parts",
    )(lax.axis_index("tok").reshape(1), *lefts, *[pair[1] for pair in flat])


def scatter_on(value, left_bits, order, count, last=jnp.bfloat16, hold=()):
    left_bits = list(left_bits)
    sent = []
    for bit in order:
        value = value.reshape((2,) * len(left_bits) + value.shape[-2:])
        axis = left_bits.index(bit)
        away = lax.index_in_dim(value, 1, axis, keepdims=False)
        sent.append(away)
        kept = last if bit == order[-1] else jnp.bfloat16
        stay = lax.index_in_dim(value, 0, axis, keepdims=False)
        if hold and bit == order[-1]:
            stay = after(stay, *hold)
        value = add(stay, trade(away, bit, count), kept)
        left_bits.remove(bit)
    return value, sent


def plain_products(terms, columns):
    pieces = []
    for place, (term, start) in enumerate(terms):
        total = sum(dots(one, two, 1, axis) for one, two, axis in term)
        end = terms[place + 1][1] if place + 1 < len(terms) else columns
        total = jnp.pad(total, ((0, 0), (0, end - start - total.shape[1])))
        pieces.append(total.astype(jnp.bfloat16))
    return pieces


def near_scatter(terms, columns, count, hold=()):
    return across_scatter(
        lambda parts: grad_parts(terms, columns, parts, count),
        lambda: plain_products(terms, columns),
        terms[0][0][0][0].shape[0],
        count,
        hold,
    )


def turned_products(lefts, rights):
    left = jnp.concatenate(lefts, axis=0)
    return [across(left, right).astype(jnp.bfloat16) for right in rights]


def feed_scatter(lefts, rights, count, hold=()):
    return across_scatter(
        lambda parts: turned_parts(lefts, rights, parts, count),
        lambda: turned_products(lefts, rights),
        lefts[0].shape[1],
        count,
        hold,
    )


def chain_scatter(lefts, rights, count, *others):
    first, order, _ = orders(count)
    bits = first[::-1] + order
    if (lefts[0].shape[1] // count) % 8:
        half, sent = half_scatter(turned_products(lefts, rights), count)
        return sent[:1], [half], lambda value, *_: last_scatter(value[0], count)
    away, kept = turned_parts(lefts, rights, [{bits[0]: 1}, {bits[0]: 0}], count, *others)
    left_bits = other_bits(bits[:1], count)
    value = add(kept, trade(away, bits[0], count))
    value = value.reshape((2,) * len(left_bits) + value.shape[-2:])
    axis = left_bits.index(bits[1])
    away = lax.index_in_dim(value, 1, axis, keepdims=False)
    stay = lax.index_in_dim(value, 0, axis, keepdims=False)
    moved = trade(away, bits[1], count)
    left_bits.remove(bits[1])

    def finish(_, before, hold):
        value = add(after(stay, *before), moved)
        return scatter_on(value, left_bits, bits[2:], count, jnp.float32, hold)[0]

    return [away], [], finish


def across_scatter(make_parts, make_plain, rows, count, hold=()):
    first, order_a, order_b = orders(count)
    if (rows // count) % 8:
        half, sent = half_scatter(make_plain(), count)
        return [half], sent, [], lambda value, *_: value, lambda value, *_: last_scatter(value[0], count)
    half_bit = first[-1]
    parts = [
        {half_bit: half, order[-1]: away}
        for half, order in enumerate((order_a, order_b))
        for away in (1, 0)
    ]
    blocks = make_parts(parts)
    halves, mids = [], []
    for place, order in enumerate((order_a, order_b)):
        away, kept = blocks[2 * place : 2 * place + 2]
        left_bits = other_bits((order[-1], half_bit), count)
        moved = trade(away, order[-1], count)
        value = add(after(kept, *hold) if hold else kept, moved)
        halves.append((value, left_bits, order[-2::-1]))
        mids += scatter_on(value, left_bits, order[-2::-1], count)[1][:1]

    def begin(halves, before=()):
        return [scatter_on(*half, count, hold=before)[0] for half in halves]

    def finish(halves, between=()):
        kept, away = halves
        kept = after(kept, *between[:2]) if between else kept
        value = add(kept, trade(away, half_bit, count))
        left_bits = [bit for bit in other_bits((), count) if bit in first[:-1]]
        return scatter_on(value, left_bits, first[-2::-1], count, jnp.float32, between[2:])[0]

    return halves, [blocks[0], blocks[2]], mids, begin, finish


def row_major(value):
    return with_layout_constraint(value, Layout(tuple(range(value.ndim))))


def add(one, two, kept=jnp.bfloat16):
    return (one.astype(jnp.float32) + two.astype(jnp.float32)).astype(kept)


def after(value, *others, micros=1):
    def keep(*refs):
        pass

    anywhere = pl.BlockSpec(memory_space=pl.ANY)
    return pl.pallas_call(
        keep,
        in_specs=[anywhere] * (1 + len(others)),
        out_specs=anywhere,
        out_shape=jax.ShapeDtypeStruct(value.shape, value.dtype),
        input_output_aliases={0: 0},
        cost_estimate=cost(micros),
        name="after",
    )(value, *others)


def first_gather(shard, count):
    first, _, _ = orders(count)
    value = shard.reshape((1,) * (count.bit_length() - 1) + shard.shape)
    for bit in first:
        value = doubled(value, bit, count)
    return value


def next_gather(value, count):
    first, order_a, order_b = orders(count)
    axis = axis_of(first[-1], count)
    halves = [
        lax.slice_in_dim(value, 0, 1, axis=axis),
        lax.slice_in_dim(value, 1, 2, axis=axis),
    ]
    for one, two in zip(order_a[:-1], order_b[:-1]):
        halves = [doubled(half, bit, count) for half, bit in zip(halves, (one, two))]
    return halves


def last_gather(halves, count, *others):
    first, order_a, order_b = orders(count)
    axis = axis_of(first[-1], count)
    lasts = (order_a[-1], order_b[-1])
    moved = [trade(half, bit, count) for half, bit in zip(halves, lasts)]
    out = jnp.concatenate(
        [
            jnp.concatenate([half, half], axis=axis_of(bit, count))
            for half, bit in zip(halves, lasts)
        ],
        axis=axis,
    )
    out = after(out, *others) if others else out
    for place, (bit, value) in enumerate(zip(lasts, moved)):
        out = put(out, value, {axis: place, axis_of(bit, count): 1 - bit_of(bit)}, count)
    return out.reshape(-1, out.shape[-1])


def halved(pieces, bit, count, kept):
    axis = axis_of(bit, count)
    digit = bit_of(bit)

    def part(place):
        parts = [lax.dynamic_slice_in_dim(piece, place, 1, axis) for piece in pieces]
        return parts[0] if len(parts) == 1 else jnp.concatenate(parts, axis=-1)

    sent = part(1 - digit).astype(jnp.bfloat16)
    total = part(digit).astype(jnp.float32) + trade(sent, bit, count).astype(jnp.float32)
    return total.astype(kept), sent


def half_scatter(values, count):
    first, order_a, order_b = orders(count)
    values = [split_rows(value, count) for value in values]
    axis = axis_of(first[-1], count)
    first_sent, out = [], []
    for place, order in enumerate((order_a[::-1], order_b[::-1])):
        pieces = [lax.slice_in_dim(value, place, place + 1, axis=axis) for value in values]
        for step, bit in enumerate(order):
            total, sent = halved(pieces, bit, count, jnp.bfloat16)
            if step == 0:
                first_sent.append(sent)
            pieces = [total]
        out.append(pieces[0])
    return jnp.concatenate(out, axis=axis), first_sent


def last_scatter(value, count):
    first, _, _ = orders(count)
    for bit in first[::-1]:
        value, _ = halved([value], bit, count, jnp.bfloat16 if bit != first[0] else jnp.float32)
    return value.reshape(value.shape[-2:])


def gather_small(value, count, bits):
    for bit in bits:
        value = jnp.concatenate([value, trade(value, bit, count)], axis=axis_of(bit, count))
    return value


def spread(value, count):
    return value.reshape((1,) * (count.bit_length() - 1) + value.shape)


def stacked(value, count):
    return value.reshape((-1,) + value.shape[count.bit_length() :])


def scatter_small(value, count, bits):
    for bit in bits:
        axis = axis_of(bit, count)
        sent = lax.slice_in_dim(value, 1, 2, axis=axis).astype(jnp.bfloat16)
        moved = trade(sent, bit, count).astype(jnp.float32)
        value = lax.slice_in_dim(value, 0, 1, axis=axis) + moved
    return value


def sum_all(value, count):
    value = value + swap(value)
    for bit in range(count.bit_length() - 1):
        value = value + trade(value, bit, count)
    return value


def pick(segment, table):
    out = jnp.zeros((segment.shape[0], table.shape[1]), jnp.float32)
    for slot in range(SLOTS):
        out = jnp.where(segment[:, None] == slot, table[slot][None, :], out)
    return out


def body(
    block_input,
    out_grad,
    class_table,
    time_table,
    class_label,
    time_index,
    grid_height,
    grid_width,
    mix_weight,
    proj_weight,
    cond_weight,
    cond_bias,
    feed_weight,
    down_weight,
    mix_mean,
    proj_mean,
    cond_mean,
    bias_mean,
    feed_mean,
    down_mean,
    mix_square,
    proj_square,
    cond_square,
    bias_square,
    feed_square,
    down_square,
):
    half = jnp.bfloat16
    count = block_input.shape[0]
    width = block_input.shape[1]
    chips = lax.axis_size("tok")
    tok = lax.axis_index("tok")
    side = lax.axis_index("mlp")
    first_side = side == 0
    rows_own = mix_weight.shape[0]
    mix_cols = mix_weight.shape[1]
    proj_cols = proj_weight.shape[1]
    hidden_cols = feed_weight.shape[2]
    cond_cols = cond_weight.shape[1]
    group = mix_cols // 3
    heads = HEADS // 2

    def joined(own, other, axis=1):
        low = jnp.where(first_side, own, other)
        high = jnp.where(first_side, other, own)
        return jnp.concatenate([low, high], axis=axis)

    def parted(value):
        size = value.shape[1] // 2
        low, high = value[:, :size], value[:, size:]
        return jnp.where(first_side, low, high), jnp.where(first_side, high, low)

    codes = jnp.stack([class_label, time_index], axis=1)
    first, order, _ = orders(chips)
    codes = spread(jnp.concatenate([codes, swap(codes)], axis=0), chips)
    codes = gather_small(codes, chips, order)

    mix_low = mix_weight.astype(half)
    mix_parts = [mix_low[:, :group], mix_low[:, group : 2 * group], mix_low[:, 2 * group :]]
    mix_moved = swap(mix_parts[1])
    mix_shard = jnp.where(
        first_side,
        jnp.concatenate([mix_parts[0], mix_parts[2], mix_moved], axis=1),
        jnp.concatenate([mix_moved, mix_parts[0], mix_parts[2]], axis=1),
    )
    mix_shard = jnp.concatenate([mix_shard, proj_weight.astype(half)], axis=1)
    codes = gather_small(codes, chips, first)
    mix_first = after(spread(mix_shard, chips), codes)
    mix_first = doubled(mix_first, first[0], chips)
    nothing = jnp.minimum(jnp.abs(mix_first.reshape(-1)[0].astype(jnp.float32)), 0.0)
    codes = stacked(codes, chips)
    labels, times = codes[:, 0], codes[:, 1]
    for bit in first[1:]:
        mix_first = doubled(mix_first, bit, chips)

    start = tok * rows_own
    class_part = lax.dynamic_slice_in_dim(class_table, start, rows_own, 1)
    time_part = lax.dynamic_slice_in_dim(time_table, start, rows_own, 1)
    class_hot = (labels[:, None] == jnp.arange(class_table.shape[0])[None, :]).astype(half)
    time_hot = (times[:, None] == jnp.arange(time_table.shape[0])[None, :]).astype(half)
    embed = jnp.dot(class_hot, class_part, preferred_element_type=jnp.float32) + jnp.dot(
        time_hot, time_part, preferred_element_type=jnp.float32
    )
    cond_low = jax.nn.silu(embed).astype(half)
    partial_mod = jnp.dot(cond_low, cond_weight.astype(half), preferred_element_type=jnp.float32)
    bias_low = cond_bias.astype(half).astype(jnp.float32)
    bias_pair = joined(bias_low[None, :], swap(bias_low)[None, :])[0]
    bias_start = tok * bias_pair.shape[0]
    bias_side = bias_start // cond_cols
    bias_pair = jnp.where(bias_side == side, bias_pair, 0.0)
    bias_row = lax.dynamic_update_slice(
        jnp.zeros((cond_cols,), jnp.float32), bias_pair, (bias_start - bias_side * cond_cols,)
    )
    mod_half = split_rows(partial_mod + bias_row[None, :], chips)
    mod_half = scatter_small(mod_half, chips, order[:1])
    mod_half = scatter_small(mod_half, chips, order[1:])
    mix_halves = next_gather(mix_first, chips)
    mod_half = scatter_small(after(mod_half, *mix_halves), chips, first[::-1])
    mod_half = mod_half.reshape(-1, cond_cols)
    slots = class_label.shape[0]
    modulation = joined(mod_half[:slots], swap(mod_half[slots:]))

    later = nothing.astype(jnp.int32)
    segment, member, rows, cols = geometry(grid_height + later, grid_width + later, count)
    tables = turn_tables(rows, cols) + (segment[None, :], segment[:, None])
    valid = (segment < SLOTS).astype(jnp.float32)[:, None]
    shift_a, scale_a, gate_a, shift_b, scale_b, gate_b = (
        pick(segment, table) for table in jnp.split(modulation, 6, axis=1)
    )
    inputs = block_input.astype(jnp.float32) + nothing
    first_in = modulate(inputs, shift_a, scale_a).astype(half)

    mix_own = last_gather(mix_halves, chips, first_in)
    far = jnp.concatenate(
        [(value + nothing).astype(half) for value in (feed_weight[0], feed_weight[1], down_weight.T)],
        axis=1,
    )
    far = doubled(spread(after(far, mix_first), chips), first[0], chips)
    far = after(far, mod_half)
    for bit in first[1:]:
        far = doubled(far, bit, chips)
    far = last_gather(next_gather(after(far, first_in), chips), chips)
    mix_other = swap_rows(mix_own, chips)
    proj_full = joined(mix_own[:, mix_cols:], mix_other[:, mix_cols:])

    shape = (3, heads, HEAD, count)
    raw_own, first_turned = heads_of(first_in, mix_own, mix_cols)
    first_moved = swap(first_turned)
    att_own, log_own, *qkv_own = attend(raw_own.reshape(shape), tables)
    att_other, log_other, *qkv_other = attend(
        heads_of(first_in, mix_other, mix_cols, first_moved)[0].reshape(shape), tables
    )
    attended = joined(att_own, att_other, 0).reshape(width, count)
    attended_moved = swap(attended)
    branch = dots(attended, proj_full, 0, 0)
    middle = inputs + gate_a * branch
    second_in = modulate(middle, shift_b, scale_b).astype(half)
    grad_out = valid * out_grad.astype(jnp.float32)
    result_grad = (gate_b * grad_out).astype(half)
    second_other, result_other = swap(second_in), swap(result_grad)
    hidden, gate_grad, up_grad, second_own, second_sent = feed_both_ways(
        second_in, second_other, result_grad, result_other, far
    )
    down_sent, down_half, down_finish = chain_scatter(
        (result_grad, result_other), [hidden], chips, attended_moved
    )
    second_grad = second_own + swap(second_sent).astype(jnp.float32)
    pull_second = jax.vjp(modulate, middle, shift_b, scale_b)[1]
    d_middle, d_shift_b, d_scale_b = pull_second(second_grad)
    d_middle = d_middle + grad_out
    d_gate_a = d_middle * branch
    branch_grad = (gate_a * d_middle).astype(half)
    attended_grad = dots(proj_full, branch_grad, 1, 1).astype(half).reshape(HEADS, HEAD, count)
    grad_own = lax.dynamic_slice_in_dim(attended_grad, side * heads, heads, 0)
    grad_other = lax.dynamic_slice_in_dim(attended_grad, (1 - side) * heads, heads, 0)
    mg_other = attend_back(*qkv_other, grad_other, log_other, tables).reshape(mix_cols, count)
    mg_moved = swap(mg_other)
    grad_own = after(grad_own, mg_other, *down_sent)
    mg_own = attend_back(*qkv_own, grad_own, log_own, tables).reshape(mix_cols, count)
    feed_half, _, feed_mids, feed_begin, feed_finish = feed_scatter(
        (second_in, second_other), [gate_grad, up_grad], chips, (mg_own,)
    )
    mg_moved = after(mg_moved, *feed_mids) if feed_mids else mg_moved
    branch_grad_own, branch_grad_other = parted(branch_grad)
    proj_start = -(-mix_cols // 128) * 128
    near_half, near_sent, near_mids, near_begin, near_finish = near_scatter(
        [
            ([(first_turned, mg_own, 1), (first_moved, mg_moved, 1)], 0),
            ([(attended, branch_grad_own, 0), (attended_moved, swap_rows(branch_grad_other, chips), 0)], proj_start),
        ],
        proj_start + proj_cols,
        chips,
    )
    down_grad = down_finish(down_half, near_mids, near_mids).T
    feed_half = feed_begin(feed_half, near_sent)
    near_half = near_begin(near_half)
    feed_grad = feed_finish(feed_half, [*near_mids, near_half[-1]])
    feed_grad = jnp.stack([feed_grad[:, :hidden_cols], feed_grad[:, hidden_cols:]])
    near_grad = near_finish(near_half)
    proj_grad = near_grad[:, proj_start:]
    mix_parts = [near_grad[:, place * group : (place + 1) * group] for place in range(3)]
    mix_moved = swap(jnp.where(first_side, mix_parts[2], mix_parts[0]))
    mix_grad = jnp.where(
        first_side,
        jnp.concatenate([mix_parts[0], mix_moved, mix_parts[1]], axis=1),
        jnp.concatenate([mix_parts[1], mix_moved, mix_parts[2]], axis=1),
    )

    partial_value = against(after(hidden, *near_sent, *near_mids), far[:, 2 * hidden_cols :])
    result = partial_value[:count] + swap(partial_value[count:].astype(half)).astype(jnp.float32)
    block_output = (valid * (middle + gate_b * result)).astype(half)
    d_gate_b = grad_out * result
    held = [*near_sent, feed_half[-1]]
    mg_own, mg_other = after(mg_own, *held), after(mg_other, *held)
    first_grad = back_through(mg_own, mg_other, mix_own, mix_other)
    pull_first = jax.vjp(modulate, inputs, shift_a, scale_a)[1]
    d_inputs, d_shift_a, d_scale_a = pull_first(first_grad)
    input_grad = d_inputs + d_middle
    member_low = after(member.astype(half), *near_sent, *near_mids)
    d_modulation = jnp.concatenate(
        [
            across(member_low, piece.astype(half))
            for piece in (d_shift_a, d_scale_a, d_gate_a, d_shift_b, d_scale_b, d_gate_b)
        ],
        axis=1,
    ).astype(half)
    mod_own, mod_other = parted(d_modulation)
    mod_all = spread(jnp.concatenate([mod_own, swap(mod_other)], axis=0), chips)
    mod_all = gather_small(after(mod_all, *near_mids), chips, first + order)
    mod_all = stacked(mod_all, chips)
    cond_grad = across(cond_low, mod_all)
    bias_half = jnp.sum(mod_all.astype(jnp.float32), axis=0)[None, :]
    bias_full = joined(bias_half, swap(bias_half))[0]
    bias_size = cond_bias.shape[0]
    bias_grad = lax.dynamic_slice_in_dim(bias_full, (2 * tok + side) * bias_size, bias_size, 0)

    grads = (mix_grad, proj_grad, cond_grad, bias_grad, feed_grad, down_grad)
    local_squares = jnp.float32(0.0)
    for grad in (near_grad[:, :mix_cols], *grads[1:]):
        local_squares = local_squares + jnp.sum(grad * grad)
    grad_norm = jnp.sqrt(sum_all(local_squares, chips))
    factor = CLIP_NORM / jnp.maximum(grad_norm, CLIP_NORM)
    params = (mix_weight, proj_weight, cond_weight, cond_bias, feed_weight, down_weight)
    means = (mix_mean, proj_mean, cond_mean, bias_mean, feed_mean, down_mean)
    squares_old = (mix_square, proj_square, cond_square, bias_square, feed_square, down_square)
    updates = [adam(w, m, v, g * factor) for w, m, v, g in zip(params, means, squares_old, grads)]
    return (
        block_output,
        input_grad,
        grad_norm,
        updates[0][0],
        updates[1][0],
        updates[2][0],
        updates[3][0],
        updates[4][0],
        updates[5][0],
        updates[0][1],
        updates[1][1],
        updates[2][1],
        updates[3][1],
        updates[4][1],
        updates[5][1],
        updates[0][2],
        updates[1][2],
        updates[2][2],
        updates[3][2],
        updates[4][2],
        updates[5][2],
    )


def solution(mesh):
    placed = (
        P(("tok", "mlp"), None),
        P(("tok", "mlp"), None),
        P(),
        P(),
        P(("tok", "mlp")),
        P(("tok", "mlp")),
        P(("tok", "mlp")),
        P(("tok", "mlp")),
        P("tok", "mlp"),
        P("tok", "mlp"),
        P("tok", "mlp"),
        P(("tok", "mlp")),
        P(None, "tok", "mlp"),
        P("mlp", "tok"),
        P("tok", "mlp"),
        P("tok", "mlp"),
        P("tok", "mlp"),
        P(("tok", "mlp")),
        P(None, "tok", "mlp"),
        P("mlp", "tok"),
        P("tok", "mlp"),
        P("tok", "mlp"),
        P("tok", "mlp"),
        P(("tok", "mlp")),
        P(None, "tok", "mlp"),
        P("mlp", "tok"),
    )
    return jax.shard_map(
        body,
        mesh=mesh,
        in_specs=placed,
        out_specs=(
            P(("tok", "mlp"), None),
            P(("tok", "mlp"), None),
            P(),
            P("tok", "mlp"),
            P("tok", "mlp"),
            P("tok", "mlp"),
            P(("tok", "mlp")),
            P(None, "tok", "mlp"),
            P("mlp", "tok"),
            P("tok", "mlp"),
            P("tok", "mlp"),
            P("tok", "mlp"),
            P(("tok", "mlp")),
            P(None, "tok", "mlp"),
            P("mlp", "tok"),
            P("tok", "mlp"),
            P("tok", "mlp"),
            P("tok", "mlp"),
            P(("tok", "mlp")),
            P(None, "tok", "mlp"),
            P("mlp", "tok"),
        ),
        check_vma=False,
    )
```

```python
import jax
import jax.numpy as jnp
from jax import lax
from jax.experimental import pallas as pl
from jax.experimental.pallas import tpu as pltpu
from jax.experimental.layout import Layout, with_layout_constraint
from jax.sharding import PartitionSpec as P

HEADS = 16
HEAD = 72
SLOTS = 4
STEP = 10


BETA_ONE = 0.9
BETA_TWO = 0.95
ADAM_EPS = 1e-08
RATE = 0.08
DECAY = 0.01
CLIP_NORM = 1.0
NORM_EPS = 1e-06
MASKED = -1e30
HIGH = lax.Precision.HIGHEST


def layer_norm(value):
    centered = value - jnp.mean(value, axis=-1, keepdims=True)
    spread = jnp.mean(centered * centered, axis=-1, keepdims=True)
    return centered * lax.rsqrt(spread + NORM_EPS)


def modulate(value, shift, scale):
    return layer_norm(value) * (1.0 + scale) + shift


def geometry(height, width, count):
    lengths = height * width
    ends = jnp.cumsum(lengths)
    starts = ends - lengths
    places = jnp.arange(count, dtype=jnp.int32)
    segment = jnp.sum((places[:, None] >= ends[None, :]).astype(jnp.int32), axis=1)
    member = segment[:, None] == jnp.arange(height.shape[0], dtype=jnp.int32)[None, :]
    start_tok = jnp.sum(jnp.where(member, starts[None, :], 0), axis=1)
    width_tok = jnp.maximum(jnp.sum(jnp.where(member, width[None, :], 0), axis=1), 1)
    offset = places - start_tok
    return (segment, member.astype(jnp.float32), offset // width_tok, offset % width_tok)


def across(left, right, precision=None):
    return lax.dot_general(
        left,
        right,
        (((0,), (0,)), ((), ())),
        preferred_element_type=jnp.float32,
        precision=precision,
    )


def against(left, right):
    return lax.dot_general(
        left, right, (((1,), (1,)), ((), ())), preferred_element_type=jnp.float32
    )


def adam(weight, mean, square, grad):
    mean_new = BETA_ONE * mean + (1.0 - BETA_ONE) * grad
    square_new = BETA_TWO * square + (1.0 - BETA_TWO) * grad * grad
    fixed_mean = mean_new / (1.0 - BETA_ONE**STEP)
    fixed_square = square_new / (1.0 - BETA_TWO**STEP)
    weight_new = weight - RATE * (fixed_mean / (jnp.sqrt(fixed_square) + ADAM_EPS) + DECAY * weight)
    return (mean_new, square_new, weight_new)


BITS = {16: ((3, 2), ((0,), (1,))), 128: ((2, 1, 0), ((3, 4), (5, 6)))}


def orders(count):
    first, (one, two) = BITS[count]
    return first, one + two, two + one


def bit_of(bit):
    return (lax.axis_index("tok") >> bit) & 1


def trade(value, bit, count):
    return lax.ppermute(value, "tok", [(place, place ^ (1 << bit)) for place in range(count)])


def axis_of(bit, count):
    return count.bit_length() - 2 - bit


def swap(value):
    return lax.ppermute(value, "mlp", [(0, 1), (1, 0)])


def swap_rows(value, count):
    blocks = value.reshape((2,) * (count.bit_length() - 1) + (-1, value.shape[-1]))
    return swap(blocks).reshape(value.shape)


def split_rows(value, count):
    axes = (2,) * (count.bit_length() - 1)
    return value.reshape(*axes, value.shape[0] // count, value.shape[1])


def put(out, value, places, count):
    start = [0] * out.ndim
    for axis, place in places.items():
        start[axis] = place
    return lax.dynamic_update_slice(out, value, tuple(start))


def doubled(value, bit, count):
    axis = axis_of(bit, count)
    out = jnp.concatenate([value, value], axis=axis)
    return put(out, trade(value, bit, count), {axis: 1 - bit_of(bit)}, count)


SCORE_SCALE = HEAD ** (-0.5)
FEED_BLOCK = 512
FEED_ROWS = 512
TURN_BLOCK = 768
TURN_CHUNKS = 1
NEAR_CHUNKS = 2


def cost(micros):
    return pl.CostEstimate(flops=int(micros * 0.460e9), bytes_accessed=1000, transcendentals=0)


def turn(value, cosine, up, down):
    quarter = HEAD // 4
    above = pltpu.roll(value, HEAD - quarter, 0)
    below = pltpu.roll(value, quarter, 0)
    return value * cosine + above * up + below * down


def dots(left, right, left_axis, right_axis):
    return lax.dot_general(
        left,
        right,
        (((left_axis,), (right_axis,)), ((), ())),
        preferred_element_type=jnp.float32,
    )


def attend_kernel(
    q_ref, k_ref, v_ref, cos_ref, up_ref, down_ref, row_ref, col_ref,
    out_ref, log_ref, q_out, k_out, v_out,
):
    cosine, up, down = cos_ref[...], up_ref[...], down_ref[...]
    query = turn(q_ref[0, 0], cosine, up, down).astype(jnp.bfloat16)
    key = turn(k_ref[0, 0], cosine, up, down).astype(jnp.bfloat16)
    value = v_ref[0, 0].astype(jnp.bfloat16)
    q_out[0], k_out[0], v_out[0] = query, key, value
    scores = dots(key, query, 0, 0) * SCORE_SCALE
    scores = jnp.where(col_ref[...] == row_ref[...], scores, MASKED)
    top = jnp.max(scores, axis=0, keepdims=True)
    weights = jnp.exp(scores - top)
    total = jnp.sum(weights, axis=0, keepdims=True)
    mixed = dots(value, weights.astype(jnp.bfloat16), 1, 0)
    out_ref[0] = (mixed * (1.0 / total)).astype(jnp.bfloat16)
    log_ref[0] = top + jnp.log(total)


def whole(value):
    return pl.BlockSpec(value.shape, lambda i: (0,) * value.ndim)


def attend(mixed, tables):
    _, heads, _, tokens = mixed.shape

    def part(place):
        return pl.BlockSpec((1, 1, HEAD, tokens), lambda i: (place, i, 0, 0))

    block = pl.BlockSpec((1, HEAD, tokens), lambda i: (i, 0, 0))
    line = pl.BlockSpec((1, 1, tokens), lambda i: (i, 0, 0))
    shape = jax.ShapeDtypeStruct((heads, HEAD, tokens), jnp.bfloat16)
    return pl.pallas_call(
        attend_kernel,
        grid=(heads,),
        in_specs=[part(0), part(1), part(2)] + [whole(value) for value in tables],
        out_specs=[block, line, block, block, block],
        out_shape=[
            shape,
            jax.ShapeDtypeStruct((heads, 1, tokens), jnp.float32),
            shape,
            shape,
            shape,
        ],
        compiler_params=pltpu.CompilerParams(vmem_limit_bytes=32 << 20),
        cost_estimate=cost(6),
        name="attend",
    )(mixed, mixed, mixed, *tables)


def attend_back_kernel(
    q_ref, k_ref, v_ref, g_ref, log_ref, cos_ref, up_ref, down_ref, row_ref, col_ref, out_ref
):
    query, key, value, grad = q_ref[0], k_ref[0], v_ref[0], g_ref[0]
    scores = dots(key, query, 0, 0) * SCORE_SCALE
    scores = jnp.where(col_ref[...] == row_ref[...], scores, MASKED)
    probs = jnp.exp(scores - log_ref[0])
    d_probs = dots(value, grad, 0, 0)
    inner = jnp.sum(probs * d_probs, axis=0, keepdims=True)
    d_scores = (probs * (d_probs - inner) * SCORE_SCALE).astype(jnp.bfloat16)
    d_value = dots(grad, probs.astype(jnp.bfloat16), 1, 1)
    d_key = dots(query, d_scores, 1, 1)
    d_query = dots(key, d_scores, 1, 0)
    cosine, up, down = cos_ref[...], -up_ref[...], -down_ref[...]
    out_ref[0, 0] = turn(d_query, cosine, up, down).astype(jnp.bfloat16)
    out_ref[1, 0] = turn(d_key, cosine, up, down).astype(jnp.bfloat16)
    out_ref[2, 0] = d_value.astype(jnp.bfloat16)


def attend_back(query, key, value, grad, logs, tables):
    heads, _, tokens = query.shape
    block = pl.BlockSpec((1, HEAD, tokens), lambda i: (i, 0, 0))
    line = pl.BlockSpec((1, 1, tokens), lambda i: (i, 0, 0))
    return pl.pallas_call(
        attend_back_kernel,
        grid=(heads,),
        in_specs=[block] * 4 + [line] + [whole(item) for item in tables],
        out_specs=pl.BlockSpec((3, 1, HEAD, tokens), lambda i: (0, i, 0, 0)),
        out_shape=jax.ShapeDtypeStruct((3, heads, HEAD, tokens), jnp.bfloat16),
        compiler_params=pltpu.CompilerParams(vmem_limit_bytes=32 << 20),
        cost_estimate=cost(10),
        name="attend_back",
    )(query, key, value, grad, logs, *tables)


def turn_tables(rows, cols):
    quarter = HEAD // 4
    freq = 10000.0 ** (-jnp.arange(quarter, dtype=jnp.float32) / quarter)
    row_angle = freq[:, None] * rows.astype(jnp.float32)[None, :]
    col_angle = freq[:, None] * cols.astype(jnp.float32)[None, :]
    zero = jnp.zeros_like(row_angle)
    cosine = jnp.concatenate([jnp.cos(row_angle)] * 2 + [jnp.cos(col_angle)] * 2, axis=0)
    up = jnp.concatenate([-jnp.sin(row_angle), zero, -jnp.sin(col_angle), zero], axis=0)
    down = jnp.concatenate([zero, jnp.sin(row_angle), zero, jnp.sin(col_angle)], axis=0)
    return cosine, up, down


def heads_kernel(x_ref, w_ref, *refs):
    out_ref, turned_ref = refs[-2:]
    step = min(256, x_ref.shape[0])
    for start in range(0, x_ref.shape[0], step):
        rows = slice(start, start + step)
        product = dots(x_ref[rows, :], w_ref[:, : out_ref.shape[0]], 1, 0)
        out_ref[:, rows] = product.T
        turned_ref[:, rows] = x_ref[rows, :].T


def heads_of(value, weight, columns, *others):
    shape = (columns, value.shape[0])
    return pl.pallas_call(
        heads_kernel,
        in_specs=[pl.BlockSpec(memory_space=pltpu.VMEM)] * 2
        + [pl.BlockSpec(memory_space=pl.ANY)] * len(others),
        out_shape=[
            jax.ShapeDtypeStruct(shape, jnp.float32),
            jax.ShapeDtypeStruct(value.shape[::-1], value.dtype),
        ],
        compiler_params=pltpu.CompilerParams(vmem_limit_bytes=48 << 20),
        cost_estimate=cost(5),
        name="heads_of",
    )(value, weight, *others)


def back_kernel(one_ref, two_ref, w_one_ref, w_two_ref, out_ref, one_turn, two_turn):
    @pl.when(pl.program_id(0) == 0)
    def _():
        for ref, turn_ref in ((one_ref, one_turn), (two_ref, two_turn)):
            for start in range(0, ref.shape[1], 128):
                turn_ref[start : start + 128, :] = ref[:, start : start + 128].T

    size = one_turn.shape[1]
    out_ref[...] = dots(one_turn[...], w_one_ref[:, :size], 1, 1) + dots(
        two_turn[...], w_two_ref[:, :size], 1, 1
    )


def back_through(one, two, weight_one, weight_two):
    columns, tokens = one.shape
    rows = weight_one.shape[0]
    block = 384
    fixed = pl.BlockSpec((columns, tokens), lambda i: (0, 0))
    moving = pl.BlockSpec((block, weight_one.shape[1]), lambda i: (i, 0))
    return pl.pallas_call(
        back_kernel,
        grid=(rows // block,),
        in_specs=[fixed, fixed, moving, moving],
        out_specs=pl.BlockSpec((tokens, block), lambda i: (0, i)),
        out_shape=jax.ShapeDtypeStruct((tokens, rows), jnp.float32),
        scratch_shapes=[pltpu.VMEM((tokens, columns), jnp.bfloat16)] * 2,
        compiler_params=pltpu.CompilerParams(vmem_limit_bytes=48 << 20),
        cost_estimate=cost(9),
        name="back_through",
    )(one, two, weight_one, weight_two)


def feed_kernel(
    x_one, x_two, r_one, r_two, gate_ref, up_ref, down_ref,
    hidden_ref, gate_out, up_out, own_ref, sent_ref, total_ref,
):
    step = pl.program_id(0)
    count = x_one.shape[0]
    rows = min(FEED_ROWS, count)
    low = jnp.bfloat16

    @pl.when(step == 0)
    def _():
        total_ref[...] = jnp.zeros_like(total_ref)

    for half, (x_ref, r_ref) in enumerate(((x_one, r_one), (x_two, r_two))):
        for start in range(0, count, rows):
            here = slice(start, start + rows)
            place = slice(half * count + start, half * count + start + rows)
            gate = dots(x_ref[here, :], gate_ref[...], 1, 0)
            up = dots(x_ref[here, :], up_ref[...], 1, 0)
            d_hidden = dots(r_ref[here, :], down_ref[...], 1, 0)
            sig = 1.0 / (1.0 + jnp.exp(-gate))
            active = gate * sig
            hidden_ref[place, :] = (active * up).astype(low)
            d_gate = (d_hidden * up * sig * (1.0 + gate * (1.0 - sig))).astype(low)
            d_up = (d_hidden * active).astype(low)
            gate_out[place, :] = d_gate
            up_out[place, :] = d_up
            total_ref[place, :] += dots(d_gate, gate_ref[...], 1, 1) + dots(
                d_up, up_ref[...], 1, 1
            )

    @pl.when(step == pl.num_programs(0) - 1)
    def _():
        own_ref[...] = total_ref[:count, :]
        sent_ref[...] = total_ref[count:, :].astype(low)


def feed_both_ways(x_one, x_two, r_one, r_two, far):
    count, width = x_one.shape
    size = far.shape[1] // 3
    block = FEED_BLOCK
    steps = size // block
    fixed = pl.BlockSpec((count, width), lambda i: (0, 0))

    def weight(place):
        return pl.BlockSpec((width, block), lambda i: (0, place * steps + i))

    moving = pl.BlockSpec((2 * count, block), lambda i: (0, i))
    wide = jax.ShapeDtypeStruct((2 * count, size), jnp.bfloat16)
    return pl.pallas_call(
        feed_kernel,
        grid=(steps,),
        in_specs=[fixed] * 4 + [weight(place) for place in range(3)],
        out_specs=[moving] * 3 + [fixed] * 2,
        out_shape=[wide] * 3
        + [
            jax.ShapeDtypeStruct((count, width), jnp.float32),
            jax.ShapeDtypeStruct((count, width), jnp.bfloat16),
        ],
        scratch_shapes=[pltpu.VMEM((2 * count, width), jnp.float32)],
        compiler_params=pltpu.CompilerParams(vmem_limit_bytes=56 << 20),
        cost_estimate=cost(22),
        name="feed_both_ways",
    )(x_one, x_two, r_one, r_two, far, far, far)


def hand_out(block_ref, outs, parts, count):
    for out, fixed_bits in zip(outs, parts):
        rest = other_bits(fixed_bits, count)
        for chip in range(count):
            if all((chip >> bit) & 1 == wanted for bit, wanted in fixed_bits.items()):
                out[block_index(chip, rest)] = block_ref[chip]


def turned_parts(lefts, rights, parts, count, *others):
    tokens, rows = lefts[0].shape
    columns = rights[0].shape[1]
    size = rows // count
    chunk = rows // TURN_CHUNKS
    block = TURN_BLOCK
    steps = columns // block

    def kernel(tok_ref, one_ref, two_ref, *refs):
        right_refs = refs[: len(rights)]
        outs = refs[len(rights) + len(others) :]
        outs, (turn_ref, block_ref) = outs[: len(parts)], outs[len(parts) :]
        step = pl.program_id(0)
        tok = tok_ref[0]

        @pl.when(step == 0)
        def _():
            for half, ref in enumerate((one_ref, two_ref)):
                for start in range(0, rows, 128):
                    turn_ref[start : start + 128, half * tokens : (half + 1) * tokens] = ref[
                        :, start : start + 128
                    ].T

        for place, right_ref in enumerate(right_refs):

            @pl.when(step // steps == place)
            def _():
                for piece in range(rows // chunk):
                    total = dots(turn_ref[piece * chunk : (piece + 1) * chunk, :], right_ref[...], 1, 0)
                    for inner in range(chunk // size):
                        value = total[inner * size : (inner + 1) * size, :].astype(jnp.bfloat16)
                        block_ref[(piece * (chunk // size) + inner) ^ tok] = value
                hand_out(block_ref, outs, parts, count)

    fixed = pl.BlockSpec((tokens, rows), lambda i: (0, 0))

    def moving(place):
        return pl.BlockSpec(
            (2 * tokens, block), lambda i: (0, jnp.clip(i - place * steps, 0, steps - 1))
        )

    shapes = [(count >> len(part), size) for part in parts]
    return pl.pallas_call(
        kernel,
        grid=(steps * len(rights),),
        in_specs=[pl.BlockSpec(memory_space=pltpu.SMEM), fixed, fixed]
        + [moving(place) for place in range(len(rights))]
        + [pl.BlockSpec(memory_space=pl.ANY)] * len(others),
        out_specs=[pl.BlockSpec(shape + (block,), lambda i: (0, 0, i)) for shape in shapes],
        out_shape=[
            jax.ShapeDtypeStruct(shape + (columns * len(rights),), jnp.bfloat16) for shape in shapes
        ],
        scratch_shapes=[
            pltpu.VMEM((rows, 2 * tokens), jnp.bfloat16),
            pltpu.VMEM((count, size, block), jnp.bfloat16),
        ],
        compiler_params=pltpu.CompilerParams(vmem_limit_bytes=48 << 20),
        cost_estimate=cost(6 * len(rights)),
        name="turned_parts",
    )(lax.axis_index("tok").reshape(1), *lefts, *rights, *others)


def block_index(chip, bits):
    place = 0
    for bit in bits:
        place = place * 2 + ((chip >> bit) & 1)
    return place


def other_bits(bits, count):
    return [bit for bit in range(count.bit_length() - 2, -1, -1) if bit not in bits]


def grad_parts(terms, columns, parts, count):
    left = terms[0][0][0][0]
    rows = left.shape[0]
    size = rows // count
    chunk = rows // NEAR_CHUNKS
    flat = [pair for term, _ in terms for pair in term]
    lefts = []
    for pair in flat:
        if not any(pair[0] is other for other in lefts):
            lefts.append(pair[0])

    def kernel(tok_ref, *refs):
        left_refs = refs[: len(lefts)]
        right_refs = refs[len(lefts) : len(lefts) + len(flat)]
        outs = refs[len(lefts) + len(flat) :]
        step = pl.program_id(0)
        tok = tok_ref[0]
        place = 0
        for term, start in terms:
            total = None
            for left, right, axis in term:
                which = [left is other for other in lefts].index(True)
                product = dots(left_refs[which][...], right_refs[place][...], 1, axis)
                total = product if total is None else total + product
                place += 1
            width = total.shape[1]
            for block in range(chunk // size):
                value = total[block * size : (block + 1) * size, :].astype(jnp.bfloat16)
                mine = (step * (chunk // size) + block) ^ tok
                for out, fixed_bits in zip(outs, parts):
                    index = block_index(mine, other_bits(fixed_bits, count))
                    here = jnp.bool_(True)
                    for bit, wanted in fixed_bits.items():
                        here &= ((mine >> bit) & 1) == wanted

                    @pl.when(here)
                    def _():
                        out[index, :, start : start + width] = value

    def fixed(value):
        return pl.BlockSpec(value.shape, lambda i: (0,) * value.ndim)

    left_specs = [pl.BlockSpec((chunk, value.shape[1]), lambda i: (i, 0)) for value in lefts]
    shapes = [(count >> len(part), size, columns) for part in parts]
    return pl.pallas_call(
        kernel,
        grid=(rows // chunk,),
        in_specs=[pl.BlockSpec(memory_space=pltpu.SMEM)]
        + left_specs
        + [fixed(pair[1]) for pair in flat],
        out_specs=[pl.BlockSpec(shape, lambda i: (0, 0, 0)) for shape in shapes],
        out_shape=[jax.ShapeDtypeStruct(shape, jnp.bfloat16) for shape in shapes],
        compiler_params=pltpu.CompilerParams(vmem_limit_bytes=56 << 20),
        cost_estimate=cost(6 * columns // 1024),
        name="grad_parts",
    )(lax.axis_index("tok").reshape(1), *lefts, *[pair[1] for pair in flat])


def scatter_on(value, left_bits, order, count, last=jnp.bfloat16, hold=()):
    left_bits = list(left_bits)
    sent = []
    for bit in order:
        value = value.reshape((2,) * len(left_bits) + value.shape[-2:])
        axis = left_bits.index(bit)
        away = lax.index_in_dim(value, 1, axis, keepdims=False)
        sent.append(away)
        kept = last if bit == order[-1] else jnp.bfloat16
        stay = lax.index_in_dim(value, 0, axis, keepdims=False)
        if hold and bit == order[-1]:
            stay = after(stay, *hold)
        value = add(stay, trade(away, bit, count), kept)
        left_bits.remove(bit)
    return value, sent


def plain_products(terms, columns):
    pieces = []
    for place, (term, start) in enumerate(terms):
        total = sum(dots(one, two, 1, axis) for one, two, axis in term)
        end = terms[place + 1][1] if place + 1 < len(terms) else columns
        total = jnp.pad(total, ((0, 0), (0, end - start - total.shape[1])))
        pieces.append(total.astype(jnp.bfloat16))
    return pieces


def near_scatter(terms, columns, count, hold=()):
    return across_scatter(
        lambda parts: grad_parts(terms, columns, parts, count),
        lambda: plain_products(terms, columns),
        terms[0][0][0][0].shape[0],
        count,
        hold,
    )


def turned_products(lefts, rights):
    left = jnp.concatenate(lefts, axis=0)
    return [across(left, right).astype(jnp.bfloat16) for right in rights]


def feed_scatter(lefts, rights, count, hold=()):
    return across_scatter(
        lambda parts: turned_parts(lefts, rights, parts, count),
        lambda: turned_products(lefts, rights),
        lefts[0].shape[1],
        count,
        hold,
    )


def chain_scatter(lefts, rights, count, *others):
    first, order, _ = orders(count)
    bits = first[::-1] + order
    if (lefts[0].shape[1] // count) % 8:
        half, sent = half_scatter(turned_products(lefts, rights), count)
        return sent[:1], [half], lambda value, *_: last_scatter(value[0], count)
    away, kept = turned_parts(lefts, rights, [{bits[0]: 1}, {bits[0]: 0}], count, *others)
    left_bits = other_bits(bits[:1], count)
    value = add(kept, trade(away, bits[0], count))
    value = value.reshape((2,) * len(left_bits) + value.shape[-2:])
    axis = left_bits.index(bits[1])
    away = lax.index_in_dim(value, 1, axis, keepdims=False)
    stay = lax.index_in_dim(value, 0, axis, keepdims=False)
    moved = trade(away, bits[1], count)
    left_bits.remove(bits[1])

    def finish(_, before, hold):
        value = add(after(stay, *before), moved)
        return scatter_on(value, left_bits, bits[2:], count, jnp.float32, hold)[0]

    return [away], [], finish


def across_scatter(make_parts, make_plain, rows, count, hold=()):
    first, order_a, order_b = orders(count)
    if (rows // count) % 8:
        half, sent = half_scatter(make_plain(), count)
        return [half], sent, [], lambda value, *_: value, lambda value, *_: last_scatter(value[0], count)
    half_bit = first[-1]
    parts = [
        {half_bit: half, order[-1]: away}
        for half, order in enumerate((order_a, order_b))
        for away in (1, 0)
    ]
    blocks = make_parts(parts)
    halves, mids = [], []
    for place, order in enumerate((order_a, order_b)):
        away, kept = blocks[2 * place : 2 * place + 2]
        left_bits = other_bits((order[-1], half_bit), count)
        moved = trade(away, order[-1], count)
        value = add(after(kept, *hold) if hold else kept, moved)
        halves.append((value, left_bits, order[-2::-1]))
        mids += scatter_on(value, left_bits, order[-2::-1], count)[1][:1]

    def begin(halves, before=()):
        return [scatter_on(*half, count, hold=before)[0] for half in halves]

    def finish(halves, between=()):
        kept, away = halves
        kept = after(kept, *between[:2]) if between else kept
        value = add(kept, trade(away, half_bit, count))
        left_bits = [bit for bit in other_bits((), count) if bit in first[:-1]]
        return scatter_on(value, left_bits, first[-2::-1], count, jnp.float32, between[2:])[0]

    return halves, [blocks[0], blocks[2]], mids, begin, finish


def row_major(value):
    return with_layout_constraint(value, Layout(tuple(range(value.ndim))))


def add(one, two, kept=jnp.bfloat16):
    return (one.astype(jnp.float32) + two.astype(jnp.float32)).astype(kept)


def after(value, *others, micros=1):
    def keep(*refs):
        pass

    anywhere = pl.BlockSpec(memory_space=pl.ANY)
    return pl.pallas_call(
        keep,
        in_specs=[anywhere] * (1 + len(others)),
        out_specs=anywhere,
        out_shape=jax.ShapeDtypeStruct(value.shape, value.dtype),
        input_output_aliases={0: 0},
        cost_estimate=cost(micros),
        name="after",
    )(value, *others)


def first_gather(shard, count):
    first, _, _ = orders(count)
    value = shard.reshape((1,) * (count.bit_length() - 1) + shard.shape)
    for bit in first:
        value = doubled(value, bit, count)
    return value


def next_gather(value, count):
    first, order_a, order_b = orders(count)
    axis = axis_of(first[-1], count)
    halves = [
        lax.slice_in_dim(value, 0, 1, axis=axis),
        lax.slice_in_dim(value, 1, 2, axis=axis),
    ]
    for one, two in zip(order_a[:-1], order_b[:-1]):
        halves = [doubled(half, bit, count) for half, bit in zip(halves, (one, two))]
    return halves


def last_gather(halves, count, *others):
    first, order_a, order_b = orders(count)
    axis = axis_of(first[-1], count)
    lasts = (order_a[-1], order_b[-1])
    moved = [trade(half, bit, count) for half, bit in zip(halves, lasts)]
    out = jnp.concatenate(
        [
            jnp.concatenate([half, half], axis=axis_of(bit, count))
            for half, bit in zip(halves, lasts)
        ],
        axis=axis,
    )
    out = after(out, *others) if others else out
    for place, (bit, value) in enumerate(zip(lasts, moved)):
        out = put(out, value, {axis: place, axis_of(bit, count): 1 - bit_of(bit)}, count)
    return out.reshape(-1, out.shape[-1])


def halved(pieces, bit, count, kept):
    axis = axis_of(bit, count)
    digit = bit_of(bit)

    def part(place):
        parts = [lax.dynamic_slice_in_dim(piece, place, 1, axis) for piece in pieces]
        return parts[0] if len(parts) == 1 else jnp.concatenate(parts, axis=-1)

    sent = part(1 - digit).astype(jnp.bfloat16)
    total = part(digit).astype(jnp.float32) + trade(sent, bit, count).astype(jnp.float32)
    return total.astype(kept), sent


def half_scatter(values, count):
    first, order_a, order_b = orders(count)
    values = [split_rows(value, count) for value in values]
    axis = axis_of(first[-1], count)
    first_sent, out = [], []
    for place, order in enumerate((order_a[::-1], order_b[::-1])):
        pieces = [lax.slice_in_dim(value, place, place + 1, axis=axis) for value in values]
        for step, bit in enumerate(order):
            total, sent = halved(pieces, bit, count, jnp.bfloat16)
            if step == 0:
                first_sent.append(sent)
            pieces = [total]
        out.append(pieces[0])
    return jnp.concatenate(out, axis=axis), first_sent


def last_scatter(value, count):
    first, _, _ = orders(count)
    for bit in first[::-1]:
        value, _ = halved([value], bit, count, jnp.bfloat16 if bit != first[0] else jnp.float32)
    return value.reshape(value.shape[-2:])


def gather_small(value, count, bits):
    for bit in bits:
        value = jnp.concatenate([value, trade(value, bit, count)], axis=axis_of(bit, count))
    return value


def spread(value, count):
    return value.reshape((1,) * (count.bit_length() - 1) + value.shape)


def stacked(value, count):
    return value.reshape((-1,) + value.shape[count.bit_length() :])


def scatter_small(value, count, bits):
    for bit in bits:
        axis = axis_of(bit, count)
        sent = lax.slice_in_dim(value, 1, 2, axis=axis).astype(jnp.bfloat16)
        moved = trade(sent, bit, count).astype(jnp.float32)
        value = lax.slice_in_dim(value, 0, 1, axis=axis) + moved
    return value


def sum_all(value, count):
    value = value + swap(value)
    for bit in range(count.bit_length() - 1):
        value = value + trade(value, bit, count)
    return value


def pick(segment, table):
    out = jnp.zeros((segment.shape[0], table.shape[1]), jnp.float32)
    for slot in range(SLOTS):
        out = jnp.where(segment[:, None] == slot, table[slot][None, :], out)
    return out


def body(
    block_input,
    out_grad,
    class_table,
    time_table,
    class_label,
    time_index,
    grid_height,
    grid_width,
    mix_weight,
    proj_weight,
    cond_weight,
    cond_bias,
    feed_weight,
    down_weight,
    mix_mean,
    proj_mean,
    cond_mean,
    bias_mean,
    feed_mean,
    down_mean,
    mix_square,
    proj_square,
    cond_square,
    bias_square,
    feed_square,
    down_square,
):
    half = jnp.bfloat16
    count = block_input.shape[0]
    width = block_input.shape[1]
    chips = lax.axis_size("tok")
    tok = lax.axis_index("tok")
    side = lax.axis_index("mlp")
    first_side = side == 0
    rows_own = mix_weight.shape[0]
    mix_cols = mix_weight.shape[1]
    proj_cols = proj_weight.shape[1]
    hidden_cols = feed_weight.shape[2]
    cond_cols = cond_weight.shape[1]
    group = mix_cols // 3
    heads = HEADS // 2

    def joined(own, other, axis=1):
        low = jnp.where(first_side, own, other)
        high = jnp.where(first_side, other, own)
        return jnp.concatenate([low, high], axis=axis)

    def parted(value):
        size = value.shape[1] // 2
        low, high = value[:, :size], value[:, size:]
        return jnp.where(first_side, low, high), jnp.where(first_side, high, low)

    codes = jnp.stack([class_label, time_index], axis=1)
    first, order, _ = orders(chips)
    codes = spread(jnp.concatenate([codes, swap(codes)], axis=0), chips)
    codes = gather_small(codes, chips, order)

    mix_low = mix_weight.astype(half)
    mix_parts = [mix_low[:, :group], mix_low[:, group : 2 * group], mix_low[:, 2 * group :]]
    mix_moved = swap(mix_parts[1])
    mix_shard = jnp.where(
        first_side,
        jnp.concatenate([mix_parts[0], mix_parts[2], mix_moved], axis=1),
        jnp.concatenate([mix_moved, mix_parts[0], mix_parts[2]], axis=1),
    )
    mix_shard = jnp.concatenate([mix_shard, proj_weight.astype(half)], axis=1)
    codes = gather_small(after(codes, mix_shard), chips, first)
    mix_first = after(spread(mix_shard, chips), codes)
    mix_first = doubled(mix_first, first[0], chips)
    nothing = jnp.minimum(jnp.abs(mix_first.reshape(-1)[0].astype(jnp.float32)), 0.0)
    codes = stacked(codes, chips)
    labels, times = codes[:, 0], codes[:, 1]
    for bit in first[1:]:
        mix_first = doubled(mix_first, bit, chips)

    start = tok * rows_own
    class_part = lax.dynamic_slice_in_dim(class_table, start, rows_own, 1)
    time_part = lax.dynamic_slice_in_dim(time_table, start, rows_own, 1)
    class_hot = (labels[:, None] == jnp.arange(class_table.shape[0])[None, :]).astype(half)
    time_hot = (times[:, None] == jnp.arange(time_table.shape[0])[None, :]).astype(half)
    embed = jnp.dot(class_hot, class_part, preferred_element_type=jnp.float32) + jnp.dot(
        time_hot, time_part, preferred_element_type=jnp.float32
    )
    cond_low = jax.nn.silu(embed).astype(half)
    partial_mod = jnp.dot(cond_low, cond_weight.astype(half), preferred_element_type=jnp.float32)
    bias_low = cond_bias.astype(half).astype(jnp.float32)
    bias_pair = joined(bias_low[None, :], swap(bias_low)[None, :])[0]
    bias_start = tok * bias_pair.shape[0]
    bias_side = bias_start // cond_cols
    bias_pair = jnp.where(bias_side == side, bias_pair, 0.0)
    bias_row = lax.dynamic_update_slice(
        jnp.zeros((cond_cols,), jnp.float32), bias_pair, (bias_start - bias_side * cond_cols,)
    )
    mod_half = split_rows(partial_mod + bias_row[None, :], chips)
    mod_half = scatter_small(mod_half, chips, order[:1])
    mod_half = scatter_small(mod_half, chips, order[1:])
    mix_halves = next_gather(mix_first, chips)
    mod_half = scatter_small(after(mod_half, *mix_halves), chips, first[::-1])
    mod_half = mod_half.reshape(-1, cond_cols)
    slots = class_label.shape[0]
    modulation = joined(mod_half[:slots], swap(mod_half[slots:]))

    later = nothing.astype(jnp.int32)
    segment, member, rows, cols = geometry(grid_height + later, grid_width + later, count)
    tables = turn_tables(rows, cols) + (segment[None, :], segment[:, None])
    valid = (segment < SLOTS).astype(jnp.float32)[:, None]
    shift_a, scale_a, gate_a, shift_b, scale_b, gate_b = (
        pick(segment, table) for table in jnp.split(modulation, 6, axis=1)
    )
    inputs = block_input.astype(jnp.float32) + nothing
    first_in = modulate(inputs, shift_a, scale_a).astype(half)

    mix_own = last_gather(mix_halves, chips, first_in)
    far = jnp.concatenate(
        [(value + nothing).astype(half) for value in (feed_weight[0], feed_weight[1], down_weight.T)],
        axis=1,
    )
    far = doubled(spread(after(far, mix_first), chips), first[0], chips)
    far = after(far, mod_half)
    for bit in first[1:]:
        far = doubled(far, bit, chips)
    far = last_gather(next_gather(after(far, first_in), chips), chips)
    mix_other = swap_rows(mix_own, chips)
    proj_full = joined(mix_own[:, mix_cols:], mix_other[:, mix_cols:])

    shape = (3, heads, HEAD, count)
    raw_own, first_turned = heads_of(first_in, mix_own, mix_cols)
    first_moved = swap(first_turned)
    att_own, log_own, *qkv_own = attend(raw_own.reshape(shape), tables)
    att_other, log_other, *qkv_other = attend(
        heads_of(first_in, mix_other, mix_cols, first_moved)[0].reshape(shape), tables
    )
    attended = joined(att_own, att_other, 0).reshape(width, count)
    attended_moved = swap(attended)
    branch = dots(attended, proj_full, 0, 0)
    middle = inputs + gate_a * branch
    second_in = modulate(middle, shift_b, scale_b).astype(half)
    grad_out = valid * out_grad.astype(jnp.float32)
    result_grad = (gate_b * grad_out).astype(half)
    second_other, result_other = swap(second_in), swap(result_grad)
    hidden, gate_grad, up_grad, second_own, second_sent = feed_both_ways(
        second_in, second_other, result_grad, result_other, far
    )
    down_sent, down_half, down_finish = chain_scatter(
        (result_grad, result_other), [hidden], chips, attended_moved
    )
    second_grad = second_own + swap(second_sent).astype(jnp.float32)
    pull_second = jax.vjp(modulate, middle, shift_b, scale_b)[1]
    d_middle, d_shift_b, d_scale_b = pull_second(second_grad)
    d_middle = d_middle + grad_out
    d_gate_a = d_middle * branch
    branch_grad = (gate_a * d_middle).astype(half)
    attended_grad = dots(proj_full, branch_grad, 1, 1).astype(half).reshape(HEADS, HEAD, count)
    grad_own = lax.dynamic_slice_in_dim(attended_grad, side * heads, heads, 0)
    grad_other = lax.dynamic_slice_in_dim(attended_grad, (1 - side) * heads, heads, 0)
    mg_other = attend_back(*qkv_other, grad_other, log_other, tables).reshape(mix_cols, count)
    mg_moved = swap(mg_other)
    grad_own = after(grad_own, mg_other, *down_sent)
    mg_own = attend_back(*qkv_own, grad_own, log_own, tables).reshape(mix_cols, count)
    feed_half, _, feed_mids, feed_begin, feed_finish = feed_scatter(
        (second_in, second_other), [gate_grad, up_grad], chips, (mg_own,)
    )
    mg_moved = after(mg_moved, *feed_mids) if feed_mids else mg_moved
    branch_grad_own, branch_grad_other = parted(branch_grad)
    proj_start = -(-mix_cols // 128) * 128
    near_half, near_sent, near_mids, near_begin, near_finish = near_scatter(
        [
            ([(first_turned, mg_own, 1), (first_moved, mg_moved, 1)], 0),
            ([(attended, branch_grad_own, 0), (attended_moved, swap_rows(branch_grad_other, chips), 0)], proj_start),
        ],
        proj_start + proj_cols,
        chips,
    )
    feed_half = feed_begin(feed_half, near_sent)
    near_half = near_begin(near_half)
    down_grad = down_finish(down_half, near_half[-1:], near_half[-1:]).T
    feed_grad = feed_finish(feed_half, [*near_mids, near_half[-1]])
    feed_grad = jnp.stack([feed_grad[:, :hidden_cols], feed_grad[:, hidden_cols:]])
    near_grad = near_finish(near_half)
    proj_grad = near_grad[:, proj_start:]
    mix_parts = [near_grad[:, place * group : (place + 1) * group] for place in range(3)]
    mix_moved = swap(jnp.where(first_side, mix_parts[2], mix_parts[0]))
    mix_grad = jnp.where(
        first_side,
        jnp.concatenate([mix_parts[0], mix_moved, mix_parts[1]], axis=1),
        jnp.concatenate([mix_parts[1], mix_moved, mix_parts[2]], axis=1),
    )

    partial_value = against(after(hidden, *near_sent), far[:, 2 * hidden_cols :])
    result = partial_value[:count] + swap(partial_value[count:].astype(half)).astype(jnp.float32)
    block_output = (valid * (middle + gate_b * result)).astype(half)
    d_gate_b = grad_out * result
    held = [*near_sent, feed_half[-1]]
    mg_own, mg_other = after(mg_own, *held), after(mg_other, *held)
    first_grad = back_through(mg_own, mg_other, mix_own, mix_other)
    pull_first = jax.vjp(modulate, inputs, shift_a, scale_a)[1]
    d_inputs, d_shift_a, d_scale_a = pull_first(first_grad)
    input_grad = d_inputs + d_middle
    member_low = after(member.astype(half), *near_sent, *near_mids, near_half[-1])
    d_modulation = jnp.concatenate(
        [
            across(member_low, piece.astype(half))
            for piece in (d_shift_a, d_scale_a, d_gate_a, d_shift_b, d_scale_b, d_gate_b)
        ],
        axis=1,
    ).astype(half)
    mod_own, mod_other = parted(d_modulation)
    mod_all = spread(jnp.concatenate([mod_own, swap(mod_other)], axis=0), chips)
    mod_all = gather_small(after(mod_all, *near_mids), chips, first + order)
    mod_all = stacked(mod_all, chips)
    cond_grad = across(cond_low, mod_all)
    bias_half = jnp.sum(mod_all.astype(jnp.float32), axis=0)[None, :]
    bias_full = joined(bias_half, swap(bias_half))[0]
    bias_size = cond_bias.shape[0]
    bias_grad = lax.dynamic_slice_in_dim(bias_full, (2 * tok + side) * bias_size, bias_size, 0)

    grads = (mix_grad, proj_grad, cond_grad, bias_grad, feed_grad, down_grad)
    local_squares = jnp.float32(0.0)
    for grad in (near_grad[:, :mix_cols], *grads[1:]):
        local_squares = local_squares + jnp.sum(grad * grad)
    grad_norm = jnp.sqrt(sum_all(local_squares, chips))
    factor = CLIP_NORM / jnp.maximum(grad_norm, CLIP_NORM)
    params = (mix_weight, proj_weight, cond_weight, cond_bias, feed_weight, down_weight)
    means = (mix_mean, proj_mean, cond_mean, bias_mean, feed_mean, down_mean)
    squares_old = (mix_square, proj_square, cond_square, bias_square, feed_square, down_square)
    updates = [adam(w, m, v, g * factor) for w, m, v, g in zip(params, means, squares_old, grads)]
    return (
        block_output,
        input_grad,
        grad_norm,
        updates[0][0],
        updates[1][0],
        updates[2][0],
        updates[3][0],
        updates[4][0],
        updates[5][0],
        updates[0][1],
        updates[1][1],
        updates[2][1],
        updates[3][1],
        updates[4][1],
        updates[5][1],
        updates[0][2],
        updates[1][2],
        updates[2][2],
        updates[3][2],
        updates[4][2],
        updates[5][2],
    )


def solution(mesh):
    placed = (
        P(("tok", "mlp"), None),
        P(("tok", "mlp"), None),
        P(),
        P(),
        P(("tok", "mlp")),
        P(("tok", "mlp")),
        P(("tok", "mlp")),
        P(("tok", "mlp")),
        P("tok", "mlp"),
        P("tok", "mlp"),
        P("tok", "mlp"),
        P(("tok", "mlp")),
        P(None, "tok", "mlp"),
        P("mlp", "tok"),
        P("tok", "mlp"),
        P("tok", "mlp"),
        P("tok", "mlp"),
        P(("tok", "mlp")),
        P(None, "tok", "mlp"),
        P("mlp", "tok"),
        P("tok", "mlp"),
        P("tok", "mlp"),
        P("tok", "mlp"),
        P(("tok", "mlp")),
        P(None, "tok", "mlp"),
        P("mlp", "tok"),
    )
    return jax.shard_map(
        body,
        mesh=mesh,
        in_specs=placed,
        out_specs=(
            P(("tok", "mlp"), None),
            P(("tok", "mlp"), None),
            P(),
            P("tok", "mlp"),
            P("tok", "mlp"),
            P("tok", "mlp"),
            P(("tok", "mlp")),
            P(None, "tok", "mlp"),
            P("mlp", "tok"),
            P("tok", "mlp"),
            P("tok", "mlp"),
            P("tok", "mlp"),
            P(("tok", "mlp")),
            P(None, "tok", "mlp"),
            P("mlp", "tok"),
            P("tok", "mlp"),
            P("tok", "mlp"),
            P("tok", "mlp"),
            P(("tok", "mlp")),
            P(None, "tok", "mlp"),
            P("mlp", "tok"),
        ),
        check_vma=False,
    )
```

```python
import jax
import jax.numpy as jnp
from jax import lax
from jax.experimental import pallas as pl
from jax.experimental.pallas import tpu as pltpu
from jax.experimental.layout import Layout, with_layout_constraint
from jax.sharding import PartitionSpec as P

HEADS = 16
HEAD = 72
SLOTS = 4
STEP = 10


BETA_ONE = 0.9
BETA_TWO = 0.95
ADAM_EPS = 1e-08
RATE = 0.08
DECAY = 0.01
CLIP_NORM = 1.0
NORM_EPS = 1e-06
MASKED = -1e30
HIGH = lax.Precision.HIGHEST


def layer_norm(value):
    centered = value - jnp.mean(value, axis=-1, keepdims=True)
    spread = jnp.mean(centered * centered, axis=-1, keepdims=True)
    return centered * lax.rsqrt(spread + NORM_EPS)


def modulate(value, shift, scale):
    return layer_norm(value) * (1.0 + scale) + shift


def geometry(height, width, count):
    lengths = height * width
    ends = jnp.cumsum(lengths)
    starts = ends - lengths
    places = jnp.arange(count, dtype=jnp.int32)
    segment = jnp.sum((places[:, None] >= ends[None, :]).astype(jnp.int32), axis=1)
    member = segment[:, None] == jnp.arange(height.shape[0], dtype=jnp.int32)[None, :]
    start_tok = jnp.sum(jnp.where(member, starts[None, :], 0), axis=1)
    width_tok = jnp.maximum(jnp.sum(jnp.where(member, width[None, :], 0), axis=1), 1)
    offset = places - start_tok
    return (segment, member.astype(jnp.float32), offset // width_tok, offset % width_tok)


def across(left, right, precision=None):
    return lax.dot_general(
        left,
        right,
        (((0,), (0,)), ((), ())),
        preferred_element_type=jnp.float32,
        precision=precision,
    )


def against(left, right):
    return lax.dot_general(
        left, right, (((1,), (1,)), ((), ())), preferred_element_type=jnp.float32
    )


def adam(weight, mean, square, grad):
    mean_new = BETA_ONE * mean + (1.0 - BETA_ONE) * grad
    square_new = BETA_TWO * square + (1.0 - BETA_TWO) * grad * grad
    fixed_mean = mean_new / (1.0 - BETA_ONE**STEP)
    fixed_square = square_new / (1.0 - BETA_TWO**STEP)
    weight_new = weight - RATE * (fixed_mean / (jnp.sqrt(fixed_square) + ADAM_EPS) + DECAY * weight)
    return (mean_new, square_new, weight_new)


BITS = {16: ((3, 2), ((0,), (1,))), 128: ((2, 1, 0), ((3, 4), (5, 6)))}


def orders(count):
    first, (one, two) = BITS[count]
    return first, one + two, two + one


def bit_of(bit):
    return (lax.axis_index("tok") >> bit) & 1


def trade(value, bit, count):
    return lax.ppermute(value, "tok", [(place, place ^ (1 << bit)) for place in range(count)])


def axis_of(bit, count):
    return count.bit_length() - 2 - bit


def swap(value):
    return lax.ppermute(value, "mlp", [(0, 1), (1, 0)])


def swap_rows(value, count):
    blocks = value.reshape((2,) * (count.bit_length() - 1) + (-1, value.shape[-1]))
    return swap(blocks).reshape(value.shape)


def split_rows(value, count):
    axes = (2,) * (count.bit_length() - 1)
    return value.reshape(*axes, value.shape[0] // count, value.shape[1])


def put(out, value, places, count):
    start = [0] * out.ndim
    for axis, place in places.items():
        start[axis] = place
    return lax.dynamic_update_slice(out, value, tuple(start))


def doubled(value, bit, count):
    axis = axis_of(bit, count)
    out = jnp.concatenate([value, value], axis=axis)
    return put(out, trade(value, bit, count), {axis: 1 - bit_of(bit)}, count)


SCORE_SCALE = HEAD ** (-0.5)
PAIR = 2
FEED_BLOCK = 512
FEED_ROWS = 512
TURN_BLOCK = 768
TURN_CHUNKS = 1
NEAR_CHUNKS = 2


def cost(micros):
    return pl.CostEstimate(flops=int(micros * 0.460e9), bytes_accessed=1000, transcendentals=0)


def turn(value, cosine, up, down):
    quarter = HEAD // 4
    above = pltpu.roll(value, HEAD - quarter, 0)
    below = pltpu.roll(value, quarter, 0)
    return value * cosine + above * up + below * down


def dots(left, right, left_axis, right_axis):
    return lax.dot_general(
        left,
        right,
        (((left_axis,), (right_axis,)), ((), ())),
        preferred_element_type=jnp.float32,
    )


def attend_kernel(
    q_ref, k_ref, v_ref, cos_ref, up_ref, down_ref, row_ref, col_ref,
    out_ref, log_ref, q_out, k_out, v_out,
):
    cosine, up, down = cos_ref[...], up_ref[...], down_ref[...]
    for head in range(PAIR):
        query = turn(q_ref[0, head], cosine, up, down).astype(jnp.bfloat16)
        key = turn(k_ref[0, head], cosine, up, down).astype(jnp.bfloat16)
        value = v_ref[0, head].astype(jnp.bfloat16)
        q_out[head], k_out[head], v_out[head] = query, key, value
        scores = dots(key, query, 0, 0) * SCORE_SCALE
        scores = jnp.where(col_ref[...] == row_ref[...], scores, MASKED)
        top = jnp.max(scores, axis=0, keepdims=True)
        weights = jnp.exp(scores - top)
        total = jnp.sum(weights, axis=0, keepdims=True)
        mixed = dots(value, weights.astype(jnp.bfloat16), 1, 0)
        out_ref[head] = (mixed * (1.0 / total)).astype(jnp.bfloat16)
        log_ref[head] = top + jnp.log(total)


def whole(value):
    return pl.BlockSpec(value.shape, lambda i: (0,) * value.ndim)


def attend(mixed, tables):
    _, heads, _, tokens = mixed.shape

    def part(place):
        return pl.BlockSpec((1, PAIR, HEAD, tokens), lambda i: (place, i, 0, 0))

    block = pl.BlockSpec((PAIR, HEAD, tokens), lambda i: (i, 0, 0))
    line = pl.BlockSpec((PAIR, 1, tokens), lambda i: (i, 0, 0))
    shape = jax.ShapeDtypeStruct((heads, HEAD, tokens), jnp.bfloat16)
    return pl.pallas_call(
        attend_kernel,
        grid=(heads // PAIR,),
        in_specs=[part(0), part(1), part(2)] + [whole(value) for value in tables],
        out_specs=[block, line, block, block, block],
        out_shape=[
            shape,
            jax.ShapeDtypeStruct((heads, 1, tokens), jnp.float32),
            shape,
            shape,
            shape,
        ],
        compiler_params=pltpu.CompilerParams(vmem_limit_bytes=32 << 20),
        cost_estimate=cost(6),
        name="attend",
    )(mixed, mixed, mixed, *tables)


def attend_back_kernel(
    q_ref, k_ref, v_ref, g_ref, log_ref, cos_ref, up_ref, down_ref, row_ref, col_ref, out_ref
):
    for head in range(PAIR):
        query, key, value, grad = q_ref[head], k_ref[head], v_ref[head], g_ref[head]
        scores = dots(key, query, 0, 0) * SCORE_SCALE
        scores = jnp.where(col_ref[...] == row_ref[...], scores, MASKED)
        probs = jnp.exp(scores - log_ref[head])
        d_probs = dots(value, grad, 0, 0)
        inner = jnp.sum(probs * d_probs, axis=0, keepdims=True)
        d_scores = (probs * (d_probs - inner) * SCORE_SCALE).astype(jnp.bfloat16)
        d_value = dots(grad, probs.astype(jnp.bfloat16), 1, 1)
        d_key = dots(query, d_scores, 1, 1)
        d_query = dots(key, d_scores, 1, 0)
        cosine, up, down = cos_ref[...], -up_ref[...], -down_ref[...]
        out_ref[0, head] = turn(d_query, cosine, up, down).astype(jnp.bfloat16)
        out_ref[1, head] = turn(d_key, cosine, up, down).astype(jnp.bfloat16)
        out_ref[2, head] = d_value.astype(jnp.bfloat16)


def attend_back(query, key, value, grad, logs, tables):
    heads, _, tokens = query.shape
    block = pl.BlockSpec((PAIR, HEAD, tokens), lambda i: (i, 0, 0))
    line = pl.BlockSpec((PAIR, 1, tokens), lambda i: (i, 0, 0))
    return pl.pallas_call(
        attend_back_kernel,
        grid=(heads // PAIR,),
        in_specs=[block] * 4 + [line] + [whole(item) for item in tables],
        out_specs=pl.BlockSpec((3, PAIR, HEAD, tokens), lambda i: (0, i, 0, 0)),
        out_shape=jax.ShapeDtypeStruct((3, heads, HEAD, tokens), jnp.bfloat16),
        compiler_params=pltpu.CompilerParams(vmem_limit_bytes=32 << 20),
        cost_estimate=cost(10),
        name="attend_back",
    )(query, key, value, grad, logs, *tables)


def turn_tables(rows, cols):
    quarter = HEAD // 4
    freq = 10000.0 ** (-jnp.arange(quarter, dtype=jnp.float32) / quarter)
    row_angle = freq[:, None] * rows.astype(jnp.float32)[None, :]
    col_angle = freq[:, None] * cols.astype(jnp.float32)[None, :]
    zero = jnp.zeros_like(row_angle)
    cosine = jnp.concatenate([jnp.cos(row_angle)] * 2 + [jnp.cos(col_angle)] * 2, axis=0)
    up = jnp.concatenate([-jnp.sin(row_angle), zero, -jnp.sin(col_angle), zero], axis=0)
    down = jnp.concatenate([zero, jnp.sin(row_angle), zero, jnp.sin(col_angle)], axis=0)
    return cosine, up, down


def heads_kernel(x_ref, w_ref, *refs):
    out_ref, turned_ref = refs[-2:]
    step = min(256, x_ref.shape[0])
    for start in range(0, x_ref.shape[0], step):
        rows = slice(start, start + step)
        product = dots(x_ref[rows, :], w_ref[:, : out_ref.shape[0]], 1, 0)
        out_ref[:, rows] = product.T
        turned_ref[:, rows] = x_ref[rows, :].T


def heads_of(value, weight, columns, *others):
    shape = (columns, value.shape[0])
    return pl.pallas_call(
        heads_kernel,
        in_specs=[pl.BlockSpec(memory_space=pltpu.VMEM)] * 2
        + [pl.BlockSpec(memory_space=pl.ANY)] * len(others),
        out_shape=[
            jax.ShapeDtypeStruct(shape, jnp.float32),
            jax.ShapeDtypeStruct(value.shape[::-1], value.dtype),
        ],
        compiler_params=pltpu.CompilerParams(vmem_limit_bytes=48 << 20),
        cost_estimate=cost(5),
        name="heads_of",
    )(value, weight, *others)


def back_kernel(one_ref, two_ref, w_one_ref, w_two_ref, out_ref, one_turn, two_turn):
    @pl.when(pl.program_id(0) == 0)
    def _():
        for ref, turn_ref in ((one_ref, one_turn), (two_ref, two_turn)):
            for start in range(0, ref.shape[1], 128):
                turn_ref[start : start + 128, :] = ref[:, start : start + 128].T

    size = one_turn.shape[1]
    out_ref[...] = dots(one_turn[...], w_one_ref[:, :size], 1, 1) + dots(
        two_turn[...], w_two_ref[:, :size], 1, 1
    )


def back_through(one, two, weight_one, weight_two):
    columns, tokens = one.shape
    rows = weight_one.shape[0]
    block = 384
    fixed = pl.BlockSpec((columns, tokens), lambda i: (0, 0))
    moving = pl.BlockSpec((block, weight_one.shape[1]), lambda i: (i, 0))
    return pl.pallas_call(
        back_kernel,
        grid=(rows // block,),
        in_specs=[fixed, fixed, moving, moving],
        out_specs=pl.BlockSpec((tokens, block), lambda i: (0, i)),
        out_shape=jax.ShapeDtypeStruct((tokens, rows), jnp.float32),
        scratch_shapes=[pltpu.VMEM((tokens, columns), jnp.bfloat16)] * 2,
        compiler_params=pltpu.CompilerParams(vmem_limit_bytes=48 << 20),
        cost_estimate=cost(9),
        name="back_through",
    )(one, two, weight_one, weight_two)


def feed_kernel(
    x_one, x_two, r_one, r_two, gate_ref, up_ref, down_ref,
    hidden_ref, gate_out, up_out, own_ref, sent_ref, total_ref,
):
    step = pl.program_id(0)
    count = x_one.shape[0]
    rows = min(FEED_ROWS, count)
    low = jnp.bfloat16

    @pl.when(step == 0)
    def _():
        total_ref[...] = jnp.zeros_like(total_ref)

    for half, (x_ref, r_ref) in enumerate(((x_one, r_one), (x_two, r_two))):
        for start in range(0, count, rows):
            here = slice(start, start + rows)
            place = slice(half * count + start, half * count + start + rows)
            gate = dots(x_ref[here, :], gate_ref[...], 1, 0)
            up = dots(x_ref[here, :], up_ref[...], 1, 0)
            d_hidden = dots(r_ref[here, :], down_ref[...], 1, 0)
            sig = 1.0 / (1.0 + jnp.exp(-gate))
            active = gate * sig
            hidden_ref[place, :] = (active * up).astype(low)
            d_gate = (d_hidden * up * sig * (1.0 + gate * (1.0 - sig))).astype(low)
            d_up = (d_hidden * active).astype(low)
            gate_out[place, :] = d_gate
            up_out[place, :] = d_up
            total_ref[place, :] += dots(d_gate, gate_ref[...], 1, 1) + dots(
                d_up, up_ref[...], 1, 1
            )

    @pl.when(step == pl.num_programs(0) - 1)
    def _():
        own_ref[...] = total_ref[:count, :]
        sent_ref[...] = total_ref[count:, :].astype(low)


def feed_both_ways(x_one, x_two, r_one, r_two, far):
    count, width = x_one.shape
    size = far.shape[1] // 3
    block = FEED_BLOCK
    steps = size // block
    fixed = pl.BlockSpec((count, width), lambda i: (0, 0))

    def weight(place):
        return pl.BlockSpec((width, block), lambda i: (0, place * steps + i))

    moving = pl.BlockSpec((2 * count, block), lambda i: (0, i))
    wide = jax.ShapeDtypeStruct((2 * count, size), jnp.bfloat16)
    return pl.pallas_call(
        feed_kernel,
        grid=(steps,),
        in_specs=[fixed] * 4 + [weight(place) for place in range(3)],
        out_specs=[moving] * 3 + [fixed] * 2,
        out_shape=[wide] * 3
        + [
            jax.ShapeDtypeStruct((count, width), jnp.float32),
            jax.ShapeDtypeStruct((count, width), jnp.bfloat16),
        ],
        scratch_shapes=[pltpu.VMEM((2 * count, width), jnp.float32)],
        compiler_params=pltpu.CompilerParams(vmem_limit_bytes=56 << 20),
        cost_estimate=cost(22),
        name="feed_both_ways",
    )(x_one, x_two, r_one, r_two, far, far, far)


def hand_out(block_ref, outs, parts, count):
    for out, fixed_bits in zip(outs, parts):
        rest = other_bits(fixed_bits, count)
        for chip in range(count):
            if all((chip >> bit) & 1 == wanted for bit, wanted in fixed_bits.items()):
                out[block_index(chip, rest)] = block_ref[chip]


def turned_parts(lefts, rights, parts, count, *others):
    tokens, rows = lefts[0].shape
    columns = rights[0].shape[1]
    size = rows // count
    chunk = rows // TURN_CHUNKS
    block = TURN_BLOCK
    steps = columns // block

    def kernel(tok_ref, one_ref, two_ref, *refs):
        right_refs = refs[: len(rights)]
        outs = refs[len(rights) + len(others) :]
        outs, (turn_ref, block_ref) = outs[: len(parts)], outs[len(parts) :]
        step = pl.program_id(0)
        tok = tok_ref[0]

        @pl.when(step == 0)
        def _():
            for half, ref in enumerate((one_ref, two_ref)):
                for start in range(0, rows, 128):
                    turn_ref[start : start + 128, half * tokens : (half + 1) * tokens] = ref[
                        :, start : start + 128
                    ].T

        for place, right_ref in enumerate(right_refs):

            @pl.when(step // steps == place)
            def _():
                for piece in range(rows // chunk):
                    total = dots(turn_ref[piece * chunk : (piece + 1) * chunk, :], right_ref[...], 1, 0)
                    for inner in range(chunk // size):
                        value = total[inner * size : (inner + 1) * size, :].astype(jnp.bfloat16)
                        block_ref[(piece * (chunk // size) + inner) ^ tok] = value
                hand_out(block_ref, outs, parts, count)

    fixed = pl.BlockSpec((tokens, rows), lambda i: (0, 0))

    def moving(place):
        return pl.BlockSpec(
            (2 * tokens, block), lambda i: (0, jnp.clip(i - place * steps, 0, steps - 1))
        )

    shapes = [(count >> len(part), size) for part in parts]
    return pl.pallas_call(
        kernel,
        grid=(steps * len(rights),),
        in_specs=[pl.BlockSpec(memory_space=pltpu.SMEM), fixed, fixed]
        + [moving(place) for place in range(len(rights))]
        + [pl.BlockSpec(memory_space=pl.ANY)] * len(others),
        out_specs=[pl.BlockSpec(shape + (block,), lambda i: (0, 0, i)) for shape in shapes],
        out_shape=[
            jax.ShapeDtypeStruct(shape + (columns * len(rights),), jnp.bfloat16) for shape in shapes
        ],
        scratch_shapes=[
            pltpu.VMEM((rows, 2 * tokens), jnp.bfloat16),
            pltpu.VMEM((count, size, block), jnp.bfloat16),
        ],
        compiler_params=pltpu.CompilerParams(vmem_limit_bytes=48 << 20),
        cost_estimate=cost(6 * len(rights)),
        name="turned_parts",
    )(lax.axis_index("tok").reshape(1), *lefts, *rights, *others)


def block_index(chip, bits):
    place = 0
    for bit in bits:
        place = place * 2 + ((chip >> bit) & 1)
    return place


def other_bits(bits, count):
    return [bit for bit in range(count.bit_length() - 2, -1, -1) if bit not in bits]


def grad_parts(terms, columns, parts, count):
    left = terms[0][0][0][0]
    rows = left.shape[0]
    size = rows // count
    chunk = rows // NEAR_CHUNKS
    flat = [pair for term, _ in terms for pair in term]
    lefts = []
    for pair in flat:
        if not any(pair[0] is other for other in lefts):
            lefts.append(pair[0])

    def kernel(tok_ref, *refs):
        left_refs = refs[: len(lefts)]
        right_refs = refs[len(lefts) : len(lefts) + len(flat)]
        outs = refs[len(lefts) + len(flat) :]
        step = pl.program_id(0)
        tok = tok_ref[0]
        place = 0
        for term, start in terms:
            total = None
            for left, right, axis in term:
                which = [left is other for other in lefts].index(True)
                product = dots(left_refs[which][...], right_refs[place][...], 1, axis)
                total = product if total is None else total + product
                place += 1
            width = total.shape[1]
            for block in range(chunk // size):
                value = total[block * size : (block + 1) * size, :].astype(jnp.bfloat16)
                mine = (step * (chunk // size) + block) ^ tok
                for out, fixed_bits in zip(outs, parts):
                    index = block_index(mine, other_bits(fixed_bits, count))
                    here = jnp.bool_(True)
                    for bit, wanted in fixed_bits.items():
                        here &= ((mine >> bit) & 1) == wanted

                    @pl.when(here)
                    def _():
                        out[index, :, start : start + width] = value

    def fixed(value):
        return pl.BlockSpec(value.shape, lambda i: (0,) * value.ndim)

    left_specs = [pl.BlockSpec((chunk, value.shape[1]), lambda i: (i, 0)) for value in lefts]
    shapes = [(count >> len(part), size, columns) for part in parts]
    return pl.pallas_call(
        kernel,
        grid=(rows // chunk,),
        in_specs=[pl.BlockSpec(memory_space=pltpu.SMEM)]
        + left_specs
        + [fixed(pair[1]) for pair in flat],
        out_specs=[pl.BlockSpec(shape, lambda i: (0, 0, 0)) for shape in shapes],
        out_shape=[jax.ShapeDtypeStruct(shape, jnp.bfloat16) for shape in shapes],
        compiler_params=pltpu.CompilerParams(vmem_limit_bytes=56 << 20),
        cost_estimate=cost(6 * columns // 1024),
        name="grad_parts",
    )(lax.axis_index("tok").reshape(1), *lefts, *[pair[1] for pair in flat])


def scatter_on(value, left_bits, order, count, last=jnp.bfloat16, hold=()):
    left_bits = list(left_bits)
    sent = []
    for bit in order:
        value = value.reshape((2,) * len(left_bits) + value.shape[-2:])
        axis = left_bits.index(bit)
        away = lax.index_in_dim(value, 1, axis, keepdims=False)
        sent.append(away)
        kept = last if bit == order[-1] else jnp.bfloat16
        stay = lax.index_in_dim(value, 0, axis, keepdims=False)
        if hold and bit == order[-1]:
            stay = after(stay, *hold)
        value = add(stay, trade(away, bit, count), kept)
        left_bits.remove(bit)
    return value, sent


def plain_products(terms, columns):
    pieces = []
    for place, (term, start) in enumerate(terms):
        total = sum(dots(one, two, 1, axis) for one, two, axis in term)
        end = terms[place + 1][1] if place + 1 < len(terms) else columns
        total = jnp.pad(total, ((0, 0), (0, end - start - total.shape[1])))
        pieces.append(total.astype(jnp.bfloat16))
    return pieces


def near_scatter(terms, columns, count, hold=()):
    return across_scatter(
        lambda parts: grad_parts(terms, columns, parts, count),
        lambda: plain_products(terms, columns),
        terms[0][0][0][0].shape[0],
        count,
        hold,
    )


def turned_products(lefts, rights):
    left = jnp.concatenate(lefts, axis=0)
    return [across(left, right).astype(jnp.bfloat16) for right in rights]


def feed_scatter(lefts, rights, count, hold=()):
    return across_scatter(
        lambda parts: turned_parts(lefts, rights, parts, count),
        lambda: turned_products(lefts, rights),
        lefts[0].shape[1],
        count,
        hold,
    )


def chain_scatter(lefts, rights, count, *others):
    first, order, _ = orders(count)
    bits = first[::-1] + order
    if (lefts[0].shape[1] // count) % 8:
        half, sent = half_scatter(turned_products(lefts, rights), count)
        return sent[:1], [half], lambda value, *_: last_scatter(value[0], count)
    away, kept = turned_parts(lefts, rights, [{bits[0]: 1}, {bits[0]: 0}], count, *others)
    left_bits = other_bits(bits[:1], count)
    value = add(kept, trade(away, bits[0], count))
    value = value.reshape((2,) * len(left_bits) + value.shape[-2:])
    axis = left_bits.index(bits[1])
    away = lax.index_in_dim(value, 1, axis, keepdims=False)
    stay = lax.index_in_dim(value, 0, axis, keepdims=False)
    moved = trade(away, bits[1], count)
    left_bits.remove(bits[1])

    def finish(_, before, hold):
        value = add(after(stay, *before), moved)
        return scatter_on(value, left_bits, bits[2:], count, jnp.float32, hold)[0]

    return [away], [], finish


def across_scatter(make_parts, make_plain, rows, count, hold=()):
    first, order_a, order_b = orders(count)
    if (rows // count) % 8:
        half, sent = half_scatter(make_plain(), count)
        return [half], sent, [], lambda value, *_: value, lambda value, *_: last_scatter(value[0], count)
    half_bit = first[-1]
    parts = [
        {half_bit: half, order[-1]: away}
        for half, order in enumerate((order_a, order_b))
        for away in (1, 0)
    ]
    blocks = make_parts(parts)
    halves, mids = [], []
    for place, order in enumerate((order_a, order_b)):
        away, kept = blocks[2 * place : 2 * place + 2]
        left_bits = other_bits((order[-1], half_bit), count)
        moved = trade(away, order[-1], count)
        value = add(after(kept, *hold) if hold else kept, moved)
        halves.append((value, left_bits, order[-2::-1]))
        mids += scatter_on(value, left_bits, order[-2::-1], count)[1][:1]

    def begin(halves, before=()):
        return [scatter_on(*half, count, hold=before)[0] for half in halves]

    def finish(halves, between=()):
        kept, away = halves
        kept = after(kept, *between[:2]) if between else kept
        value = add(kept, trade(away, half_bit, count))
        left_bits = [bit for bit in other_bits((), count) if bit in first[:-1]]
        return scatter_on(value, left_bits, first[-2::-1], count, jnp.float32, between[2:])[0]

    return halves, [blocks[0], blocks[2]], mids, begin, finish


def row_major(value):
    return with_layout_constraint(value, Layout(tuple(range(value.ndim))))


def add(one, two, kept=jnp.bfloat16):
    return (one.astype(jnp.float32) + two.astype(jnp.float32)).astype(kept)


def after(value, *others, micros=1):
    def keep(*refs):
        pass

    anywhere = pl.BlockSpec(memory_space=pl.ANY)
    return pl.pallas_call(
        keep,
        in_specs=[anywhere] * (1 + len(others)),
        out_specs=anywhere,
        out_shape=jax.ShapeDtypeStruct(value.shape, value.dtype),
        input_output_aliases={0: 0},
        cost_estimate=cost(micros),
        name="after",
    )(value, *others)


def first_gather(shard, count):
    first, _, _ = orders(count)
    value = shard.reshape((1,) * (count.bit_length() - 1) + shard.shape)
    for bit in first:
        value = doubled(value, bit, count)
    return value


def next_gather(value, count):
    first, order_a, order_b = orders(count)
    axis = axis_of(first[-1], count)
    halves = [
        lax.slice_in_dim(value, 0, 1, axis=axis),
        lax.slice_in_dim(value, 1, 2, axis=axis),
    ]
    for one, two in zip(order_a[:-1], order_b[:-1]):
        halves = [doubled(half, bit, count) for half, bit in zip(halves, (one, two))]
    return halves


def last_gather(halves, count, *others):
    first, order_a, order_b = orders(count)
    axis = axis_of(first[-1], count)
    lasts = (order_a[-1], order_b[-1])
    moved = [trade(half, bit, count) for half, bit in zip(halves, lasts)]
    out = jnp.concatenate(
        [
            jnp.concatenate([half, half], axis=axis_of(bit, count))
            for half, bit in zip(halves, lasts)
        ],
        axis=axis,
    )
    out = after(out, *others) if others else out
    for place, (bit, value) in enumerate(zip(lasts, moved)):
        out = put(out, value, {axis: place, axis_of(bit, count): 1 - bit_of(bit)}, count)
    return out.reshape(-1, out.shape[-1])


def halved(pieces, bit, count, kept):
    axis = axis_of(bit, count)
    digit = bit_of(bit)

    def part(place):
        parts = [lax.dynamic_slice_in_dim(piece, place, 1, axis) for piece in pieces]
        return parts[0] if len(parts) == 1 else jnp.concatenate(parts, axis=-1)

    sent = part(1 - digit).astype(jnp.bfloat16)
    total = part(digit).astype(jnp.float32) + trade(sent, bit, count).astype(jnp.float32)
    return total.astype(kept), sent


def half_scatter(values, count):
    first, order_a, order_b = orders(count)
    values = [split_rows(value, count) for value in values]
    axis = axis_of(first[-1], count)
    first_sent, out = [], []
    for place, order in enumerate((order_a[::-1], order_b[::-1])):
        pieces = [lax.slice_in_dim(value, place, place + 1, axis=axis) for value in values]
        for step, bit in enumerate(order):
            total, sent = halved(pieces, bit, count, jnp.bfloat16)
            if step == 0:
                first_sent.append(sent)
            pieces = [total]
        out.append(pieces[0])
    return jnp.concatenate(out, axis=axis), first_sent


def last_scatter(value, count):
    first, _, _ = orders(count)
    for bit in first[::-1]:
        value, _ = halved([value], bit, count, jnp.bfloat16 if bit != first[0] else jnp.float32)
    return value.reshape(value.shape[-2:])


def gather_small(value, count, bits):
    for bit in bits:
        value = jnp.concatenate([value, trade(value, bit, count)], axis=axis_of(bit, count))
    return value


def spread(value, count):
    return value.reshape((1,) * (count.bit_length() - 1) + value.shape)


def stacked(value, count):
    return value.reshape((-1,) + value.shape[count.bit_length() :])


def scatter_small(value, count, bits):
    for bit in bits:
        axis = axis_of(bit, count)
        sent = lax.slice_in_dim(value, 1, 2, axis=axis).astype(jnp.bfloat16)
        moved = trade(sent, bit, count).astype(jnp.float32)
        value = lax.slice_in_dim(value, 0, 1, axis=axis) + moved
    return value


def sum_all(value, count):
    value = value + swap(value)
    for bit in range(count.bit_length() - 1):
        value = value + trade(value, bit, count)
    return value


def pick(segment, table):
    out = jnp.zeros((segment.shape[0], table.shape[1]), jnp.float32)
    for slot in range(SLOTS):
        out = jnp.where(segment[:, None] == slot, table[slot][None, :], out)
    return out


def body(
    block_input,
    out_grad,
    class_table,
    time_table,
    class_label,
    time_index,
    grid_height,
    grid_width,
    mix_weight,
    proj_weight,
    cond_weight,
    cond_bias,
    feed_weight,
    down_weight,
    mix_mean,
    proj_mean,
    cond_mean,
    bias_mean,
    feed_mean,
    down_mean,
    mix_square,
    proj_square,
    cond_square,
    bias_square,
    feed_square,
    down_square,
):
    half = jnp.bfloat16
    count = block_input.shape[0]
    width = block_input.shape[1]
    chips = lax.axis_size("tok")
    tok = lax.axis_index("tok")
    side = lax.axis_index("mlp")
    first_side = side == 0
    rows_own = mix_weight.shape[0]
    mix_cols = mix_weight.shape[1]
    proj_cols = proj_weight.shape[1]
    hidden_cols = feed_weight.shape[2]
    cond_cols = cond_weight.shape[1]
    group = mix_cols // 3
    heads = HEADS // 2

    def joined(own, other, axis=1):
        low = jnp.where(first_side, own, other)
        high = jnp.where(first_side, other, own)
        return jnp.concatenate([low, high], axis=axis)

    def parted(value):
        size = value.shape[1] // 2
        low, high = value[:, :size], value[:, size:]
        return jnp.where(first_side, low, high), jnp.where(first_side, high, low)

    codes = jnp.stack([class_label, time_index], axis=1)
    first, order, _ = orders(chips)
    codes = spread(jnp.concatenate([codes, swap(codes)], axis=0), chips)
    codes = gather_small(codes, chips, order)

    mix_low = mix_weight.astype(half)
    mix_parts = [mix_low[:, :group], mix_low[:, group : 2 * group], mix_low[:, 2 * group :]]
    mix_moved = swap(mix_parts[1])
    mix_shard = jnp.where(
        first_side,
        jnp.concatenate([mix_parts[0], mix_parts[2], mix_moved], axis=1),
        jnp.concatenate([mix_moved, mix_parts[0], mix_parts[2]], axis=1),
    )
    mix_shard = jnp.concatenate([mix_shard, proj_weight.astype(half)], axis=1)
    codes = gather_small(after(codes, mix_shard), chips, first)
    mix_first = after(spread(mix_shard, chips), codes)
    mix_first = doubled(mix_first, first[0], chips)
    nothing = jnp.minimum(jnp.abs(mix_first.reshape(-1)[0].astype(jnp.float32)), 0.0)
    codes = stacked(codes, chips)
    labels, times = codes[:, 0], codes[:, 1]
    for bit in first[1:]:
        mix_first = doubled(mix_first, bit, chips)

    start = tok * rows_own
    class_part = lax.dynamic_slice_in_dim(class_table, start, rows_own, 1)
    time_part = lax.dynamic_slice_in_dim(time_table, start, rows_own, 1)
    class_hot = (labels[:, None] == jnp.arange(class_table.shape[0])[None, :]).astype(half)
    time_hot = (times[:, None] == jnp.arange(time_table.shape[0])[None, :]).astype(half)
    embed = jnp.dot(class_hot, class_part, preferred_element_type=jnp.float32) + jnp.dot(
        time_hot, time_part, preferred_element_type=jnp.float32
    )
    cond_low = jax.nn.silu(embed).astype(half)
    partial_mod = jnp.dot(cond_low, cond_weight.astype(half), preferred_element_type=jnp.float32)
    bias_low = cond_bias.astype(half).astype(jnp.float32)
    bias_pair = joined(bias_low[None, :], swap(bias_low)[None, :])[0]
    bias_start = tok * bias_pair.shape[0]
    bias_side = bias_start // cond_cols
    bias_pair = jnp.where(bias_side == side, bias_pair, 0.0)
    bias_row = lax.dynamic_update_slice(
        jnp.zeros((cond_cols,), jnp.float32), bias_pair, (bias_start - bias_side * cond_cols,)
    )
    mod_half = split_rows(partial_mod + bias_row[None, :], chips)
    mod_half = scatter_small(mod_half, chips, order[:1])
    mod_half = scatter_small(mod_half, chips, order[1:])
    mix_halves = next_gather(mix_first, chips)
    mod_half = scatter_small(after(mod_half, *mix_halves), chips, first[::-1])
    mod_half = mod_half.reshape(-1, cond_cols)
    slots = class_label.shape[0]
    modulation = joined(mod_half[:slots], swap(mod_half[slots:]))

    later = nothing.astype(jnp.int32)
    segment, member, rows, cols = geometry(grid_height + later, grid_width + later, count)
    tables = turn_tables(rows, cols) + (segment[None, :], segment[:, None])
    valid = (segment < SLOTS).astype(jnp.float32)[:, None]
    shift_a, scale_a, gate_a, shift_b, scale_b, gate_b = (
        pick(segment, table) for table in jnp.split(modulation, 6, axis=1)
    )
    inputs = block_input.astype(jnp.float32) + nothing
    first_in = modulate(inputs, shift_a, scale_a).astype(half)

    mix_own = last_gather(mix_halves, chips, first_in)
    far = jnp.concatenate(
        [(value + nothing).astype(half) for value in (feed_weight[0], feed_weight[1], down_weight.T)],
        axis=1,
    )
    far = doubled(spread(after(far, mix_first), chips), first[0], chips)
    far = after(far, mod_half)
    for bit in first[1:]:
        far = doubled(far, bit, chips)
    far = last_gather(next_gather(after(far, first_in), chips), chips)
    mix_other = swap_rows(mix_own, chips)
    proj_full = joined(mix_own[:, mix_cols:], mix_other[:, mix_cols:])

    shape = (3, heads, HEAD, count)
    raw_own, first_turned = heads_of(first_in, mix_own, mix_cols)
    first_moved = swap(first_turned)
    att_own, log_own, *qkv_own = attend(raw_own.reshape(shape), tables)
    att_other, log_other, *qkv_other = attend(
        heads_of(first_in, mix_other, mix_cols, first_moved)[0].reshape(shape), tables
    )
    attended = joined(att_own, att_other, 0).reshape(width, count)
    attended_moved = swap(attended)
    branch = dots(attended, proj_full, 0, 0)
    middle = inputs + gate_a * branch
    second_in = modulate(middle, shift_b, scale_b).astype(half)
    grad_out = valid * out_grad.astype(jnp.float32)
    result_grad = (gate_b * grad_out).astype(half)
    second_other, result_other = swap(second_in), swap(result_grad)
    hidden, gate_grad, up_grad, second_own, second_sent = feed_both_ways(
        second_in, second_other, result_grad, result_other, far
    )
    down_sent, down_half, down_finish = chain_scatter(
        (result_grad, result_other), [hidden], chips, attended_moved
    )
    second_grad = second_own + swap(second_sent).astype(jnp.float32)
    pull_second = jax.vjp(modulate, middle, shift_b, scale_b)[1]
    d_middle, d_shift_b, d_scale_b = pull_second(second_grad)
    d_middle = d_middle + grad_out
    d_gate_a = d_middle * branch
    branch_grad = (gate_a * d_middle).astype(half)
    attended_grad = dots(proj_full, branch_grad, 1, 1).astype(half).reshape(HEADS, HEAD, count)
    grad_own = lax.dynamic_slice_in_dim(attended_grad, side * heads, heads, 0)
    grad_other = lax.dynamic_slice_in_dim(attended_grad, (1 - side) * heads, heads, 0)
    mg_other = attend_back(*qkv_other, grad_other, log_other, tables).reshape(mix_cols, count)
    mg_moved = swap(mg_other)
    grad_own = after(grad_own, mg_other, *down_sent)
    mg_own = attend_back(*qkv_own, grad_own, log_own, tables).reshape(mix_cols, count)
    feed_half, _, feed_mids, feed_begin, feed_finish = feed_scatter(
        (second_in, second_other), [gate_grad, up_grad], chips, (mg_own,)
    )
    mg_moved = after(mg_moved, *feed_mids) if feed_mids else mg_moved
    branch_grad_own, branch_grad_other = parted(branch_grad)
    proj_start = -(-mix_cols // 128) * 128
    near_half, near_sent, near_mids, near_begin, near_finish = near_scatter(
        [
            ([(first_turned, mg_own, 1), (first_moved, mg_moved, 1)], 0),
            ([(attended, branch_grad_own, 0), (attended_moved, swap_rows(branch_grad_other, chips), 0)], proj_start),
        ],
        proj_start + proj_cols,
        chips,
    )
    feed_half = feed_begin(feed_half, near_sent)
    near_half = near_begin(near_half)
    down_grad = down_finish(down_half, near_half[-1:], near_half[-1:]).T
    feed_grad = feed_finish(feed_half, [*near_mids, near_half[-1]])
    feed_grad = jnp.stack([feed_grad[:, :hidden_cols], feed_grad[:, hidden_cols:]])
    near_grad = near_finish(near_half)
    proj_grad = near_grad[:, proj_start:]
    mix_parts = [near_grad[:, place * group : (place + 1) * group] for place in range(3)]
    mix_moved = swap(jnp.where(first_side, mix_parts[2], mix_parts[0]))
    mix_grad = jnp.where(
        first_side,
        jnp.concatenate([mix_parts[0], mix_moved, mix_parts[1]], axis=1),
        jnp.concatenate([mix_parts[1], mix_moved, mix_parts[2]], axis=1),
    )

    partial_value = against(after(hidden, *near_sent), far[:, 2 * hidden_cols :])
    result = partial_value[:count] + swap(partial_value[count:].astype(half)).astype(jnp.float32)
    block_output = (valid * (middle + gate_b * result)).astype(half)
    d_gate_b = grad_out * result
    held = [*near_sent, feed_half[-1]]
    mg_own, mg_other = after(mg_own, *held), after(mg_other, *held)
    first_grad = back_through(mg_own, mg_other, mix_own, mix_other)
    pull_first = jax.vjp(modulate, inputs, shift_a, scale_a)[1]
    d_inputs, d_shift_a, d_scale_a = pull_first(first_grad)
    input_grad = d_inputs + d_middle
    member_low = after(member.astype(half), *near_sent, *near_mids, near_half[-1])
    d_modulation = jnp.concatenate(
        [
            across(member_low, piece.astype(half))
            for piece in (d_shift_a, d_scale_a, d_gate_a, d_shift_b, d_scale_b, d_gate_b)
        ],
        axis=1,
    ).astype(half)
    mod_own, mod_other = parted(d_modulation)
    mod_all = spread(jnp.concatenate([mod_own, swap(mod_other)], axis=0), chips)
    mod_all = gather_small(after(mod_all, *near_mids), chips, first + order)
    mod_all = stacked(mod_all, chips)
    cond_grad = across(cond_low, mod_all)
    bias_half = jnp.sum(mod_all.astype(jnp.float32), axis=0)[None, :]
    bias_full = joined(bias_half, swap(bias_half))[0]
    bias_size = cond_bias.shape[0]
    bias_grad = lax.dynamic_slice_in_dim(bias_full, (2 * tok + side) * bias_size, bias_size, 0)

    grads = (mix_grad, proj_grad, cond_grad, bias_grad, feed_grad, down_grad)
    local_squares = jnp.float32(0.0)
    for grad in (near_grad[:, :mix_cols], *grads[1:]):
        local_squares = local_squares + jnp.sum(grad * grad)
    grad_norm = jnp.sqrt(sum_all(local_squares, chips))
    factor = CLIP_NORM / jnp.maximum(grad_norm, CLIP_NORM)
    params = (mix_weight, proj_weight, cond_weight, cond_bias, feed_weight, down_weight)
    means = (mix_mean, proj_mean, cond_mean, bias_mean, feed_mean, down_mean)
    squares_old = (mix_square, proj_square, cond_square, bias_square, feed_square, down_square)
    updates = [adam(w, m, v, g * factor) for w, m, v, g in zip(params, means, squares_old, grads)]
    return (
        block_output,
        input_grad,
        grad_norm,
        updates[0][0],
        updates[1][0],
        updates[2][0],
        updates[3][0],
        updates[4][0],
        updates[5][0],
        updates[0][1],
        updates[1][1],
        updates[2][1],
        updates[3][1],
        updates[4][1],
        updates[5][1],
        updates[0][2],
        updates[1][2],
        updates[2][2],
        updates[3][2],
        updates[4][2],
        updates[5][2],
    )


def solution(mesh):
    placed = (
        P(("tok", "mlp"), None),
        P(("tok", "mlp"), None),
        P(),
        P(),
        P(("tok", "mlp")),
        P(("tok", "mlp")),
        P(("tok", "mlp")),
        P(("tok", "mlp")),
        P("tok", "mlp"),
        P("tok", "mlp"),
        P("tok", "mlp"),
        P(("tok", "mlp")),
        P(None, "tok", "mlp"),
        P("mlp", "tok"),
        P("tok", "mlp"),
        P("tok", "mlp"),
        P("tok", "mlp"),
        P(("tok", "mlp")),
        P(None, "tok", "mlp"),
        P("mlp", "tok"),
        P("tok", "mlp"),
        P("tok", "mlp"),
        P("tok", "mlp"),
        P(("tok", "mlp")),
        P(None, "tok", "mlp"),
        P("mlp", "tok"),
    )
    return jax.shard_map(
        body,
        mesh=mesh,
        in_specs=placed,
        out_specs=(
            P(("tok", "mlp"), None),
            P(("tok", "mlp"), None),
            P(),
            P("tok", "mlp"),
            P("tok", "mlp"),
            P("tok", "mlp"),
            P(("tok", "mlp")),
            P(None, "tok", "mlp"),
            P("mlp", "tok"),
            P("tok", "mlp"),
            P("tok", "mlp"),
            P("tok", "mlp"),
            P(("tok", "mlp")),
            P(None, "tok", "mlp"),
            P("mlp", "tok"),
            P("tok", "mlp"),
            P("tok", "mlp"),
            P("tok", "mlp"),
            P(("tok", "mlp")),
            P(None, "tok", "mlp"),
            P("mlp", "tok"),
        ),
        check_vma=False,
    )
```
